32 devices in a mesh: dp: 8 (over z, x), seq: 4 (over y, core).
Axes of the slice: x: 2, y: 2, z: 4, core: 2. Of those that a mesh axis runs over, the one named last changes fastest.
Arguments:
- inputs: bfloat16 [1024, 24, 512], P('seq', 'dp'), may hold values from -6 to 6
- cotangent: bfloat16 [1024, 24, 512], P('seq', 'dp'), may hold values from -6 to 6
- w_qkv: bfloat16 [2, 512, 1536], P(None, ('dp', 'seq')), may hold values from -0.25 to 0.25
- w_out: bfloat16 [2, 512, 512], P(None, ('dp', 'seq')), may hold values from -0.25 to 0.25
- w_up: bfloat16 [2, 512, 2048], P(None, ('dp', 'seq')), may hold values from -0.25 to 0.25
- w_down: bfloat16 [2, 2048, 512], P(None, ('dp', 'seq')), may hold values from -0.25 to 0.25
- norm_gains: bfloat16 [2, 1024], P(None, ('dp', 'seq')), may hold values from 0.5 to 1.5
- biases: bfloat16 [2, 5120], P(None, ('dp', 'seq')), may hold values from -1.75 to 1.75
- time_table: bfloat16 [2, 1000, 512], P(None, None, ('dp', 'seq')), may hold values from -6 to 6
- timesteps: int32 [24], P('dp'), may hold values from 0 to 999
- importance: float32 [1000], replicated, may hold values from 0.25 to 4
Outputs:
- activations: float32 [1024, 24, 512], P('seq', 'dp')
- input_grad: float32 [1024, 24, 512], P('seq', 'dp')
- grad_qkv: float32 [2, 512, 1536], P(None, ('dp', 'seq'))
- grad_out: float32 [2, 512, 512], P(None, ('dp', 'seq'))
- up_weight_gradient: float32 [2, 512, 2048], P(None, ('dp', 'seq'))
- down_weight_gradient: float32 [2, 2048, 512], P(None, ('dp', 'seq'))
- grad_gains: float32 [2, 1024], P(None, ('dp', 'seq'))
- grad_biases: float32 [2, 5120], P(None, ('dp', 'seq'))
- grad_table: float32 [2, 1000, 512], P(None, None, ('dp', 'seq'))
The draws below stay inside these ranges and needn't reach their ends.
All inputs are finite; a program needn't handle non-finite values.
Results may differ from the reference program's by a relative error of at most 0.01.
Values may be sent and summed in bfloat16 or wider, within the bound.
A program may use at most 192 MiB of HBM per device.

```python
import math
import jax
import jax.numpy as jnp
from jax import lax

D = 512
HEADS = 8
HEAD_DIM = 64
FF = 2048
STEPS = 1000
LAYERS = 2
LEN = 1024
SEQ_DEV = 3
SEQS = 24


def with_ends(entries, key, smallest, high):
    dims = entries.shape
    place = [jax.random.randint(jax.random.fold_in(key, axis), (), 0, dims[axis]) for axis in range(len(dims))]
    entries = entries.at[tuple(place)].set(smallest)
    longest = dims.index(max(dims))
    place[longest] = (place[longest] + 1) % dims[longest]
    return entries.at[tuple(place)].set(high)


def levels(key, extent, shards, least, top_value):
    level = 1.0
    for dim, shards_of in shards:
        steps = jax.random.uniform(jax.random.fold_in(jax.random.fold_in(key, 6), dim), (shards_of,), jnp.float32, least / len(shards), top_value / len(shards))
        level = level * jnp.repeat(jnp.exp(steps), extent[dim] // shards_of).reshape((-1,) + (1,) * (len(extent) - 1 - dim))
    return level


def noise(own_key, dims, width, reach, pieces=(), dtype=jnp.bfloat16):
    entries = jax.random.normal(own_key, dims, jnp.float32) * width
    if len(pieces) > 0:
        entries = levels(own_key, dims, pieces, -0.22, 0.18) * entries
    return jnp.clip(entries, min=-reach, max=reach).astype(dtype)


def setup_inputs(seed: int = 0) -> dict:
    key_list = jax.random.split(jax.random.key(seed), 12)
    return {
        "inputs": noise(key_list[0], (LEN, SEQS, D), 1.0, 6.0, ((0, 4), (1, 8))),
        "cotangent": noise(key_list[1], (LEN, SEQS, D), 1.0, 6.0, ((0, 4), (1, 8))),
        "w_qkv": noise(key_list[2], (LAYERS, D, 3 * D), D ** -0.5, 0.25, ((1, 32),)),
        "w_out": noise(key_list[3], (LAYERS, D, D), D ** -0.5, 0.25, ((1, 32),)),
        "w_up": noise(key_list[4], (LAYERS, D, FF), D ** -0.5, 0.25, ((1, 32),)),
        "w_down": noise(key_list[5], (LAYERS, FF, D), D ** -0.5, 0.25, ((1, 32),)),
        "norm_gains": jnp.clip(1.0 + 0.1 * jax.random.normal(key_list[6], (LAYERS, 2 * D), jnp.float32), 0.5, 1.5).astype(jnp.bfloat16),
        "biases": noise(key_list[7], (LAYERS, 6 * D + FF), 0.3, 1.75, ((1, 32),)),
        "time_table": noise(key_list[8], (LAYERS, STEPS, D), 1.0, 6.0, ((2, 32),)),
        "timesteps": with_ends(jax.random.randint(key_list[9], (SEQS,), 0, STEPS), jax.random.fold_in(key_list[9], 1), 0, STEPS - 1).astype(jnp.int32),
        "importance": jnp.clip(jnp.exp(jax.random.uniform(key_list[10], (STEPS,), jnp.float32, math.log(0.25), math.log(4.0))), 0.25, 4.0),
    }


EPS = 1e-05
HIGH = lax.Precision.HIGHEST

@jax.custom_vjp
def low(v):
    return lax.optimization_barrier(v.astype(jnp.bfloat16)).astype(jnp.float32)

@jax.custom_vjp
def low_back(v):
    return v

def low_keep(v):
    return (low(v), None)

def low_pass(kept, grad):
    return (grad,)

def back_keep(v):
    return (v, None)

def back_low(kept, grad):
    return (low(grad),)
low.defvjp(low_keep, low_pass)
low_back.defvjp(back_keep, back_low)

def product(left, right):
    return jnp.matmul(left, right, precision=HIGH)

def layer_norm(values, gain_vec, bias_vec):
    centered = values - lax.optimization_barrier(jnp.mean(values, axis=-1, keepdims=True))
    spread = lax.optimization_barrier(jnp.mean(centered * centered, axis=-1, keepdims=True))
    return centered * lax.rsqrt(spread + EPS) * gain_vec + bias_vec

def one_layer(hidden, seq_embed, mat_qkv, mat_out, up_matrix, down_matrix, gain_vec, bias_vec):
    score_scale = 1.0 / math.sqrt(HEAD_DIM)
    summed_in = hidden + seq_embed[None]
    normed_one = low(layer_norm(summed_in, gain_vec[:D], bias_vec[4 * D + FF:5 * D + FF]))
    linear = low_back(product(normed_one, mat_qkv))
    queries = low(linear[..., :D] + bias_vec[:D])
    keys_all = low(linear[..., D:2 * D])
    values_all = low(linear[..., 2 * D:] + bias_vec[D:2 * D])
    split_shape = queries.shape[:2] + (HEADS, HEAD_DIM)
    scores = low_back(jnp.einsum('lghd,mghd->ghlm', queries.reshape(split_shape), keys_all.reshape(split_shape), precision=HIGH) * score_scale)
    attention_probability = low(jax.nn.softmax(scores, axis=-1))
    attn_out = low(low_back(jnp.einsum('ghlm,mghd->lghd', attention_probability, values_all.reshape(split_shape), precision=HIGH))).reshape(queries.shape)
    after_attn = summed_in + low_back(product(attn_out, mat_out)) + bias_vec[2 * D:3 * D]
    second_normalized = low(layer_norm(after_attn, gain_vec[D:], bias_vec[5 * D + FF:]))
    upward = low_back(product(second_normalized, up_matrix)) + bias_vec[3 * D:3 * D + FF]
    gelu_output = low(jax.nn.gelu(upward))
    return after_attn + low_back(product(gelu_output, down_matrix)) + bias_vec[3 * D + FF:4 * D + FF]

def stack_forward(params, hidden, step_ids):
    for layer_id in range(LAYERS):
        seq_embed = params[6][layer_id][step_ids]
        hidden = one_layer(hidden, seq_embed, params[0][layer_id], params[1][layer_id], params[2][layer_id], params[3][layer_id], params[4][layer_id], params[5][layer_id])
    return hidden

def reference(inputs, cotangent, w_qkv, w_out, w_up, w_down, norm_gains, biases, time_table, timesteps, importance):
    params = tuple((member.astype(jnp.float32) for member in (w_qkv, w_out, w_up, w_down, norm_gains, biases, time_table)))
    group_size = min(SEQ_DEV, 4)
    groups = SEQS // group_size

    def split_groups(array):
        return jnp.swapaxes(array.astype(jnp.float32).reshape(LEN, groups, group_size, D), 0, 1)

    def join_groups(array):
        return jnp.swapaxes(array, 0, 1).reshape(LEN, SEQS, D)

    def per_group(totals, item):
        hidden, cot_part, step_ids = item
        result, back_fn = jax.vjp(lambda prm, hid: stack_forward(prm, hid, step_ids), params, hidden)
        weights_seq = importance[step_ids]
        grad_params, grad_hidden = back_fn(cot_part * weights_seq[None, :, None])
        return (tuple((left + right for left, right in zip(totals, grad_params))), (result, grad_hidden))
    zeros = tuple((jnp.zeros_like(member) for member in params))
    items = (split_groups(inputs), split_groups(cotangent), timesteps.reshape(groups, group_size))
    totals, (results, grads_in) = lax.scan(per_group, zeros, items)
    return (join_groups(results), join_groups(grads_in), totals[0], totals[1], totals[2], totals[3], totals[4], totals[5], totals[6])
```

```python
import math

import jax
import jax.numpy as jnp
from jax import lax
from jax.experimental import pallas as pl
from jax.experimental.pallas import tpu as pltpu
from jax.sharding import PartitionSpec as P

D = 512
HEADS = 8
HEAD_DIM = 64
FF = 2048
STEPS = 1000
LAYERS = 2


EPS = 1e-05
HIGH = lax.Precision.HIGHEST


def layer_norm(values, gain_vec, bias_vec):
    centered = values - jnp.mean(values, axis=-1, keepdims=True)
    spread = jnp.mean(centered * centered, axis=-1, keepdims=True)
    return centered * lax.rsqrt(spread + EPS) * gain_vec + bias_vec


def attend(queries, keys_all, values_all):
    row_count, seq_count, model_width = queries.shape
    score_scale = 1.0 / math.sqrt(HEAD_DIM)

    def per_seq(seq_index, loop_state):
        outputs, log_tot = loop_state
        query_per_head = lax.dynamic_index_in_dim(queries, seq_index, 1, keepdims=False).reshape(
            row_count, HEADS, HEAD_DIM
        )
        key_per_head = lax.dynamic_index_in_dim(keys_all, seq_index, 1, keepdims=False).reshape(
            -1, HEADS, HEAD_DIM
        )
        value_per_head = lax.dynamic_index_in_dim(values_all, seq_index, 1, keepdims=False).reshape(
            -1, HEADS, HEAD_DIM
        )
        scores = (
            jnp.einsum(
                "xsv,usv->sxu", query_per_head, key_per_head, preferred_element_type=jnp.float32
            )
            * score_scale
        )
        row_max = jnp.max(scores, axis=-1, keepdims=True)
        expon = jnp.exp(scores - row_max)
        summed = jnp.sum(expon, axis=-1, keepdims=True)
        attention_probability = (expon / summed).astype(jnp.bfloat16)
        attn_out = jnp.einsum(
            "gir,rgo->igo",
            attention_probability,
            value_per_head,
            preferred_element_type=jnp.float32,
        )
        attn_out = attn_out.astype(jnp.bfloat16).reshape(row_count, 1, model_width)
        outputs = lax.dynamic_update_slice_in_dim(outputs, attn_out, seq_index, 1)
        log_tot = lax.dynamic_update_slice_in_dim(
            log_tot, (row_max + jnp.log(summed))[None, :, :, 0], seq_index, 0
        )
        return (outputs, log_tot)

    start_state = (
        jnp.zeros(queries.shape, jnp.bfloat16),
        jnp.zeros((seq_count, HEADS, row_count), jnp.float32),
    )
    return lax.fori_loop(0, seq_count, per_seq, start_state)


def attend_back(queries, keys_all, values_all, log_tot, grad_attn):
    row_count, seq_count, model_width = queries.shape
    key_count = keys_all.shape[0]
    score_scale = 1.0 / math.sqrt(HEAD_DIM)

    def per_seq(seq_index, loop_state):
        grad_query, part_key, part_value = loop_state
        query_per_head = lax.dynamic_index_in_dim(queries, seq_index, 1, keepdims=False).reshape(
            row_count, HEADS, HEAD_DIM
        )
        key_per_head = lax.dynamic_index_in_dim(keys_all, seq_index, 1, keepdims=False).reshape(
            key_count, HEADS, HEAD_DIM
        )
        value_per_head = lax.dynamic_index_in_dim(values_all, seq_index, 1, keepdims=False).reshape(
            key_count, HEADS, HEAD_DIM
        )
        hidden_state_gradient = lax.dynamic_index_in_dim(
            grad_attn, seq_index, 1, keepdims=False
        ).reshape(row_count, HEADS, HEAD_DIM)
        log_seq = lax.dynamic_index_in_dim(log_tot, seq_index, 0, keepdims=False)
        scores = (
            jnp.einsum(
                "xsv,usv->sxu", query_per_head, key_per_head, preferred_element_type=jnp.float32
            )
            * score_scale
        )
        attn_f = jnp.exp(scores - log_seq[:, :, None])
        attention_probability = attn_f.astype(jnp.bfloat16)
        value_part = jnp.einsum(
            "uxo,xuc->ouc",
            attention_probability,
            hidden_state_gradient,
            preferred_element_type=jnp.float32,
        )
        probability_gradient = jnp.einsum(
            "xsv,usv->sxu",
            hidden_state_gradient,
            value_per_head,
            preferred_element_type=jnp.float32,
        )
        row_delta = jnp.sum(probability_gradient * attn_f, axis=-1, keepdims=True)
        score_gradient = (attn_f * (probability_gradient - row_delta)).astype(jnp.bfloat16)
        query_part = (
            jnp.einsum(
                "gir,rgo->igo", score_gradient, key_per_head, preferred_element_type=jnp.float32
            )
            * score_scale
        )
        key_part = (
            jnp.einsum(
                "uxo,xuc->ouc", score_gradient, query_per_head, preferred_element_type=jnp.float32
            )
            * score_scale
        )
        grad_query = lax.dynamic_update_slice_in_dim(
            grad_query, query_part.reshape(row_count, 1, model_width), seq_index, 1
        )
        part_key = lax.dynamic_update_slice_in_dim(
            part_key, key_part.reshape(key_count, 1, model_width), seq_index, 1
        )
        part_value = lax.dynamic_update_slice_in_dim(
            part_value, value_part.reshape(key_count, 1, model_width), seq_index, 1
        )
        return (grad_query, part_key, part_value)

    start_state = (
        jnp.zeros(queries.shape, jnp.float32),
        jnp.zeros(keys_all.shape, jnp.float32),
        jnp.zeros(keys_all.shape, jnp.float32),
    )
    return lax.fori_loop(0, seq_count, per_seq, start_state)


def forward_layer(hidden, fetched, onehot):
    mat_qkv, mat_out, up_matrix, down_matrix, gain_row, bias_row, time_rows = fetched
    gain_f = gain_row.astype(jnp.float32)
    bias_f = bias_row.astype(jnp.float32)
    seq_embed = jnp.dot(onehot.astype(jnp.bfloat16), time_rows, preferred_element_type=jnp.float32)
    summed_in = hidden + seq_embed[None]
    normed_one = layer_norm(summed_in, gain_f[:D], bias_f[4 * D + FF : 5 * D + FF]).astype(
        jnp.bfloat16
    )
    linear = jnp.dot(normed_one, mat_qkv, preferred_element_type=jnp.float32)
    queries = (linear[..., :D] + bias_f[:D]).astype(jnp.bfloat16)
    keys_loc = linear[..., D : 2 * D].astype(jnp.bfloat16)
    values_loc = (linear[..., 2 * D :] + bias_f[D : 2 * D]).astype(jnp.bfloat16)
    keys_all, values_all = (
        lax.all_gather(keys_loc, "seq", axis=0, tiled=True),
        lax.all_gather(values_loc, "seq", axis=0, tiled=True),
    )
    attn_out, log_tot = attend(queries, keys_all, values_all)
    after_attn = (
        summed_in
        + jnp.dot(attn_out, mat_out, preferred_element_type=jnp.float32)
        + bias_f[2 * D : 3 * D]
    )
    second_normalized = layer_norm(after_attn, gain_f[D:], bias_f[5 * D + FF :]).astype(
        jnp.bfloat16
    )
    upward = (
        jnp.dot(second_normalized, up_matrix, preferred_element_type=jnp.float32)
        + bias_f[3 * D : 3 * D + FF]
    )
    gelu_output = jax.nn.gelu(upward).astype(jnp.bfloat16)
    result = (
        after_attn
        + jnp.dot(gelu_output, down_matrix, preferred_element_type=jnp.float32)
        + bias_f[3 * D + FF : 4 * D + FF]
    )
    record = (
        summed_in,
        normed_one,
        queries,
        keys_loc,
        values_loc,
        attn_out,
        log_tot,
        after_attn,
        second_normalized,
        upward,
        gelu_output,
        keys_all,
        values_all,
    )
    return (result, record)


def backward_layer(hidden_state_gradient, fetched, record, onehot, kv_pair):
    mat_qkv = fetched[0]
    mat_out = fetched[1]
    up_matrix = fetched[2]
    down_matrix = fetched[3]
    gain_f = fetched[4].astype(jnp.float32)
    bias_f = fetched[5].astype(jnp.float32)
    summed_in, normed_one, queries = (record[0], record[1], record[2])
    attn_out, log_tot, after_attn = (record[5], record[6], record[7])
    second_normalized, upward, gelu_output = (record[8], record[9], record[10])
    keys_all, values_all = kv_pair
    gradient_bfloat = hidden_state_gradient.astype(jnp.bfloat16)
    down_weight_gradient = jnp.einsum(
        "awt,awg->tg", gelu_output, gradient_bfloat, preferred_element_type=jnp.float32
    )
    bias_down = jnp.sum(hidden_state_gradient, axis=(0, 1))
    activation_gradient = jnp.einsum(
        "ngb,rb->ngr", gradient_bfloat, down_matrix, preferred_element_type=jnp.float32
    )
    _, gelu_back = jax.vjp(jax.nn.gelu, upward)
    grad_upward = gelu_back(activation_gradient)[0]
    bias_up = jnp.sum(grad_upward, axis=(0, 1))
    upward_bfloat = grad_upward.astype(jnp.bfloat16)
    up_weight_gradient = jnp.einsum(
        "xew,xem->wm", second_normalized, upward_bfloat, preferred_element_type=jnp.float32
    )
    second_norm_gradient = jnp.einsum(
        "iyv,tv->iyt", upward_bfloat, up_matrix, preferred_element_type=jnp.float32
    )
    _, second_back = jax.vjp(layer_norm, after_attn, gain_f[D:], bias_f[5 * D + FF :])
    from_second, gain_two, shift_two = second_back(second_norm_gradient)
    grad_mid = hidden_state_gradient + from_second
    mid_bf = grad_mid.astype(jnp.bfloat16)
    grad_out = jnp.einsum("lsc,lsd->cd", attn_out, mid_bf, preferred_element_type=jnp.float32)
    bias_out = jnp.sum(grad_mid, axis=(0, 1))
    grad_attn = jnp.einsum(
        "lsd,cd->lsc", mid_bf, mat_out, preferred_element_type=jnp.float32
    ).astype(jnp.bfloat16)
    grad_query, part_key, part_value = attend_back(
        queries, keys_all, values_all, log_tot, grad_attn
    )
    grad_key, grad_value = (
        lax.psum_scatter(
            part_key.astype(jnp.bfloat16), "seq", scatter_dimension=0, tiled=True
        ).astype(jnp.float32),
        lax.psum_scatter(
            part_value.astype(jnp.bfloat16), "seq", scatter_dimension=0, tiled=True
        ).astype(jnp.float32),
    )
    bias_query = jnp.sum(grad_query, axis=(0, 1))
    bias_value = jnp.sum(grad_value, axis=(0, 1))
    grad_linear = jnp.concatenate([grad_query, grad_key, grad_value], axis=-1).astype(jnp.bfloat16)
    grad_qkv = jnp.einsum(
        "lsc,lse->ce", normed_one, grad_linear, preferred_element_type=jnp.float32
    )
    grad_norm_one = jnp.einsum(
        "lse,ce->lsc", grad_linear, mat_qkv, preferred_element_type=jnp.float32
    )
    _, first_back = jax.vjp(layer_norm, summed_in, gain_f[:D], bias_f[4 * D + FF : 5 * D + FF])
    from_first, gain_one, shift_one = first_back(grad_norm_one)
    grad_in = grad_mid + from_first
    grad_table = jnp.dot(onehot.T, jnp.sum(grad_in, axis=0), precision=HIGH)
    grad_gain = jnp.concatenate([gain_one, gain_two])
    grad_bias = jnp.concatenate(
        [bias_query, bias_value, bias_out, bias_up, bias_down, shift_one, shift_two]
    )
    return (
        grad_in,
        (
            grad_qkv,
            grad_out,
            up_weight_gradient,
            down_weight_gradient,
            grad_gain,
            grad_bias,
            grad_table,
        ),
    )


def body(
    inputs,
    cotangent,
    w_qkv,
    w_out,
    w_up,
    w_down,
    norm_gains,
    biases,
    time_table,
    timesteps,
    importance,
):
    onehot = (timesteps[:, None] == jnp.arange(STEPS, dtype=jnp.int32)[None, :]).astype(jnp.float32)
    seq_weight = jnp.dot(onehot, importance, precision=HIGH)
    hidden = inputs.astype(jnp.float32)
    records = []
    fetched_all = []
    for layer_id in range(LAYERS):
        fetched = (
            lax.all_gather(w_qkv[layer_id], ("dp", "seq"), axis=0, tiled=True),
            lax.all_gather(w_out[layer_id], ("dp", "seq"), axis=0, tiled=True),
            lax.all_gather(w_up[layer_id], ("dp", "seq"), axis=0, tiled=True),
            lax.all_gather(w_down[layer_id], ("dp", "seq"), axis=0, tiled=True),
            lax.all_gather(norm_gains[layer_id], ("dp", "seq"), axis=0, tiled=True),
            lax.all_gather(biases[layer_id], ("dp", "seq"), axis=0, tiled=True),
            lax.all_gather(time_table[layer_id], ("dp", "seq"), axis=1, tiled=True),
        )
        hidden, record = forward_layer(hidden, fetched, onehot)
        records.append(record)
        fetched_all.append(fetched)
    hidden_state_gradient = cotangent.astype(jnp.float32) * seq_weight[None, :, None]
    shards = [None] * LAYERS
    for layer_id in reversed(range(LAYERS)):
        record = records[layer_id]
        fetched = (
            lax.all_gather(w_qkv[layer_id], ("dp", "seq"), axis=0, tiled=True),
            lax.all_gather(w_out[layer_id], ("dp", "seq"), axis=0, tiled=True),
            lax.all_gather(w_up[layer_id], ("dp", "seq"), axis=0, tiled=True),
            lax.all_gather(w_down[layer_id], ("dp", "seq"), axis=0, tiled=True),
            lax.all_gather(norm_gains[layer_id], ("dp", "seq"), axis=0, tiled=True),
            lax.all_gather(biases[layer_id], ("dp", "seq"), axis=0, tiled=True),
            lax.all_gather(time_table[layer_id], ("dp", "seq"), axis=1, tiled=True),
        )
        kv_pair = (
            lax.all_gather(record[3], "seq", axis=0, tiled=True),
            lax.all_gather(record[4], "seq", axis=0, tiled=True),
        )
        hidden_state_gradient, grads = backward_layer(
            hidden_state_gradient, fetched, record, onehot, kv_pair
        )
        shards[layer_id] = (
            lax.psum_scatter(grads[0], ("dp", "seq"), scatter_dimension=0, tiled=True),
            lax.psum_scatter(grads[1], ("dp", "seq"), scatter_dimension=0, tiled=True),
            lax.psum_scatter(grads[2], ("dp", "seq"), scatter_dimension=0, tiled=True),
            lax.psum_scatter(grads[3], ("dp", "seq"), scatter_dimension=0, tiled=True),
            lax.psum_scatter(grads[4], ("dp", "seq"), scatter_dimension=0, tiled=True),
            lax.psum_scatter(grads[5], ("dp", "seq"), scatter_dimension=0, tiled=True),
            lax.psum_scatter(grads[6], ("dp", "seq"), scatter_dimension=1, tiled=True),
        )
    stacked = [
        jnp.stack([shards[layer_id][member] for layer_id in range(LAYERS)]) for member in range(7)
    ]
    return (
        hidden,
        hidden_state_gradient,
        stacked[0],
        stacked[1],
        stacked[2],
        stacked[3],
        stacked[4],
        stacked[5],
        stacked[6],
    )


MESH_ID = pl.DeviceIdType.MESH
LOG2E = 1.4426950408889634
F32 = jnp.float32
BF = jnp.bfloat16
TILE = 256
PAIRS = HEADS // 2
N_SEMS = 256
GELU_A = math.sqrt(2.0 / math.pi)
GELU_B = 0.044715

B_Q, B_V, B_O, B_U, B_D, B_S1, B_S2 = 0, D, 2 * D, 3 * D, 3 * D + FF, 4 * D + FF, 5 * D + FF


def nn(left, right):
    return jnp.dot(left, right, preferred_element_type=F32)


def nt(left, right, precision=None):
    return lax.dot_general(left, right, (((1,), (1,)), ((), ())), preferred_element_type=F32, precision=precision)


def tn(left, right):
    return lax.dot_general(left, right, (((0,), (0,)), ((), ())), preferred_element_type=F32)


def rows_sum(value):
    return jnp.sum(value, axis=0, keepdims=True)


def ln_parts(value):
    centered = value - jnp.mean(value, axis=-1, keepdims=True)
    scale = lax.rsqrt(jnp.mean(centered * centered, axis=-1, keepdims=True) + EPS)
    return centered * scale, scale


def gelu_parts(up):
    square = up * up
    tanh = jnp.tanh(GELU_A * up * (1.0 + GELU_B * square))
    return square, tanh


class Fused:
    def __init__(self, n_z, refs):
        (self.ts, self.imp, self.xin, self.cot, self.wq_i, self.wo_i, self.wu_i, self.wd_i, self.sm_i, self.tab,
         self.act_o, self.gin_o, self.gq_o, self.go_o, self.gu_o, self.gd_o, self.small_o, self.t24_o,
         self.Wq, self.Wo, self.Wu, self.Wd, self.SM, self.TS, self.TT, self.TR, self.BV, self.GV, self.BG, self.GG,
         self.TG, self.X, self.N, self.NT, self.Q, self.KV, self.AO, self.LSE, self.DL, self.Y, self.GB, self.DO, self.G,
         self.GN, self.GL, self.ACC, self.PB, self.PC, self.RB1, self.RB2, self.RB3, self.A1, self.A2,
         self.R1, self.R2, self.R3, self.R4, self.SR, self.SX, self.SZ, self.SY,
         self.ssem, self.rsem, self.lsem, self.credit) = refs
        dp, seq = lax.axis_index("dp"), lax.axis_index("seq")
        self.n_z = n_z
        self.dp, self.seq = dp, seq
        self.z, self.x, self.y, self.c = dp // 2, dp % 2, seq // 2, seq % 2
        self.next_sem = 0
        self.next_local = 0
        self.mine = {"z": self.z, "x": self.x, "y": self.y, "c": self.c}
        self.other = {"x": 1 - self.x, "y": 1 - self.y, "c": 1 - self.c}
        self.around = [(self.z + hop) % n_z for hop in range(n_z)]
        self.device = {("z", hop): {"dp": self.around[hop] * 2 + self.x, "seq": seq} for hop in range(1, n_z)}
        self.device["x", 1] = {"dp": self.z * 2 + self.other["x"], "seq": seq}
        self.device["y", 1] = {"dp": dp, "seq": self.other["y"] * 2 + self.c}
        self.device["c", 1] = {"dp": dp, "seq": self.y * 2 + self.other["c"]}

    def hops(self, dim):
        return range(1, self.n_z) if dim == "z" else range(1, 2)

    def enter(self):
        barrier = pltpu.get_barrier_semaphore()
        who = [(dim, hop) for dim in "zxyc" for hop in self.hops(dim)]
        for dim, hop in who:
            pl.semaphore_signal(barrier, inc=1, device_id=self.device[dim, hop], device_id_type=MESH_ID)
        pl.semaphore_wait(barrier, len(who))

    def remote(self, src, dst, dim, hop=1):
        number = self.next_sem
        self.next_sem += 1
        return pltpu.make_async_remote_copy(
            src, dst, self.ssem.at[number], self.rsem.at[number], device_id=self.device[dim, hop], device_id_type=MESH_ID
        )

    def local(self, src, dst):
        number = self.next_local
        self.next_local += 1
        return pltpu.make_async_copy(src, dst, self.lsem.at[number])


class Gather:
    def __init__(self, me, view, order):
        self.copies = []
        for stage, dim in enumerate(order):
            block = view(*[slice(None) if other in order[:stage] else me.mine[other] for other in "zxyc"])
            self.copies.append([me.remote(block, block, dim, hop) for hop in me.hops(dim)])

    def start(self, stage):
        if stage:
            self.arrive(stage - 1)
        for copy in self.copies[stage]:
            copy.start()

    def arrive(self, stage=-1):
        for copy in self.copies[stage]:
            copy.wait_recv()

    def drain(self):
        for copies in self.copies:
            for copy in copies:
                copy.wait_send()


class Reduce:
    def __init__(self, me, layer, grad, recv, out, cols, order):
        self.me, self.layer, self.grad, self.recv, self.out, self.cols, self.order = me, layer, grad, recv, out, cols, order
        self.copies = [self.build(stage) for stage in range(4)]

    def block(self, fixed):
        return tuple(fixed.get(dim, slice(None)) for dim in "zxyc")

    def kept(self, stage):
        return {dim: self.me.mine[dim] for dim in self.order[:stage]}

    def build(self, stage):
        me, dim = self.me, self.order[stage]
        fixed = self.kept(stage)
        copies = []
        for hop in me.hops(dim):
            if dim == "z":
                fixed["z"] = me.around[hop]
                dst = self.recv[3].at[hop - 1, :, self.cols]
            else:
                fixed[dim] = me.other[dim]
                dst = self.recv[stage].at[(slice(None),) * (3 - stage) + (slice(None), self.cols)]
            src = self.grad.at[(self.layer, *self.block(fixed), slice(None), self.cols)]
            copies.append(me.remote(src, dst, dim, hop))
        return copies

    def start(self, stage):
        for copy in self.copies[stage]:
            copy.start()

    def add(self, stage):
        me = self.me
        for copy in self.copies[stage]:
            copy.wait_recv()
        fixed = self.kept(stage + 1)
        if self.order[stage] == "z":
            where = (self.layer, *self.block(fixed), slice(None), self.cols)
            total = self.grad[where].astype(F32)
            for hop in me.hops("z"):
                total = total + self.recv[3][hop - 1, :, self.cols].astype(F32)
            self.out[self.layer, :, self.cols] = total
            return

        def one(z, carry):
            where = (self.layer, *self.block({**fixed, "z": z}), slice(None), self.cols)
            came = (z,) + (slice(None),) * (2 - stage) + (slice(None), self.cols)
            self.grad[where] = self.grad[where] + self.recv[stage][came]
            return carry

        lax.fori_loop(0, me.n_z, one, 0)

    def drain(self):
        for copies in self.copies:
            for copy in copies:
                copy.wait_send()


class Bundle:
    def __init__(self, me, number, parts, gives, takes):
        self.me, self.number, self.parts, self.gives, self.takes = me, number, parts, gives, takes

    def step(self, stage):
        me = self.me
        if stage:
            for part in self.parts:
                part.add(stage - 1)
            if self.gives:
                for half in range(2):
                    dim = self.parts[half].order[stage - 1]
                    for hop in me.hops(dim):
                        pl.semaphore_signal(
                            me.credit.at[self.number, stage - 1, half], inc=1, device_id=me.device[dim, hop], device_id_type=MESH_ID
                        )
        if stage < 4:
            if self.takes:
                for half in range(2):
                    count = len(me.hops(self.parts[half].order[stage]))
                    pl.semaphore_wait(me.credit.at[self.number, stage, half], count)
            for part in self.parts:
                part.start(stage)

    def drain(self):
        for part in self.parts:
            part.drain()


def at_step(index, hooks):
    for when, action in hooks:
        pl.when(index == when)(action)


def fused_kernel(n_z, *refs):
    me = Fused(n_z, refs)
    x, y, z, c = me.x, me.y, me.z, me.c
    n_dp = 2 * n_z
    spare = slice(None)

    mats = ((me.wq_i, me.Wq), (me.wo_i, me.Wo), (me.wu_i, me.Wu), (me.wd_i, me.Wd))
    loads = [me.local(src.at[layer], dst.at[layer, z, x, y, c]) for layer in range(LAYERS) for src, dst in mats]
    loads.append(me.local(me.sm_i, me.SM.at[z, x, y, c]))
    for load in loads:
        load.start()
    own_tokens = [
        me.local(src.at[seq], dst.at[tile]) for src, dst in ((me.xin, me.DO), (me.cot, me.GB)) for seq, tile in ((y, 0), (2, 2))
    ]
    for load in own_tokens:
        load.start()

    row = lax.broadcasted_iota(jnp.int32, (32, 128), 0)
    steps = jnp.zeros((32, 128), jnp.int32)
    for j in range(3):
        steps = jnp.where(row == 3 * me.dp + j, me.ts[j], steps)
    me.TT[z, x] = steps
    me.BG[...] = jnp.zeros_like(me.BG)
    me.GG[...] = jnp.zeros_like(me.GG)

    me.enter()
    for load in loads:
        load.wait()

    def weight(layer, ref, order, cols):
        return Gather(me, lambda *where: ref.at[(layer, *where, spare, cols)], order)

    def halves(layer, ref):
        width = ref.shape[-1]
        return [weight(layer, ref, "zxyc", slice(0, width // 2)), weight(layer, ref, "zyxc", slice(width // 2, width))]

    steps_all = Gather(me, lambda gz, gx, gy, gc: me.TT.at[gz, gx], "zx")
    small = Gather(me, lambda *where: me.SM.at[where], "zxyc")
    times = Gather(me, lambda *where: me.TS.at[where], "zyxc")
    first = halves(0, me.Wq)
    second = [part for ref in (me.Wo, me.Wu, me.Wd) for part in halves(0, ref)]
    third = [part for ref in (me.Wq, me.Wo, me.Wu, me.Wd) for part in halves(1, ref)]

    def go(parts, stage):
        def run():
            for part in parts:
                part.start(stage)

        return run

    token_in = me.remote(me.xin.at[me.other["y"]], me.DO.at[1], "y")
    cot_in = me.remote(me.cot.at[me.other["y"]], me.GB.at[1], "y")
    steps_all.start(0)
    go(first + [small], 0)()
    token_in.start()
    steps_all.start(1)
    go(first + [small], 1)()
    steps_all.arrive()
    t24 = jnp.sum(me.TT[...].reshape(n_dp, 32, 128), axis=0)
    me.t24_o[...] = t24
    hot = (t24[:, 0:1] == lax.broadcasted_iota(jnp.int32, (32, STEPS), 1)).astype(F32).astype(BF)
    picked = jnp.concatenate([nn(hot, me.tab[layer])[:24] for layer in range(LAYERS)], axis=0).astype(BF)
    lane = lax.broadcasted_iota(jnp.int32, (16, 128), 1)
    spread = (lane == 16 * (4 * x + me.seq) + lax.broadcasted_iota(jnp.int32, (16, 128), 0)).astype(F32).astype(BF)
    me.TS[z, x, y, c] = nn(picked, spread).astype(BF)
    times.start(0)
    go(first + [small], 2)()
    times.start(1)
    go(first + [small], 3)()
    times.start(2)
    times.start(3)
    cot_in.start()
    go(second, 0)()

    small.arrive()
    for gz in range(n_z):
        for gx in range(2):
            block = jnp.sum(me.SM[gz, gx].reshape(4, 16, 128).astype(F32), axis=0)
            dp = 2 * gz + gx
            for layer in range(LAYERS):
                for r in range(5):
                    at = (5 * dp + r) * 128
                    me.BV[layer, :, at : at + 128] = block[6 * layer + r : 6 * layer + r + 1]
                me.GV[layer, :, 128 * dp : 128 * dp + 128] = block[6 * layer + 5 : 6 * layer + 6]
    times.arrive()
    slabs = jnp.concatenate(
        [jnp.sum(me.TS[gz].reshape(8, 48, 128).astype(F32), axis=0) for gz in range(n_z)], axis=1
    ).astype(BF)
    r8 = lax.broadcasted_iota(jnp.int32, (16, 48), 0)
    c48 = lax.broadcasted_iota(jnp.int32, (16, 48), 1)
    for layer in range(LAYERS):
        base = 24 * layer + 3 * me.dp
        pick = ((r8 == 0) & (c48 == base + y)) | ((r8 == 1) & (c48 == base + 2))
        me.TR[layer] = nn(pick.astype(F32).astype(BF), slabs)[:8]

    def time_row(layer, tile):
        return me.TR[layer, 1:2, :] if tile == 2 else me.TR[layer, 0:1, :]

    def bias(layer, at, width=D):
        return me.BV[layer, :, at : at + width]

    for load in own_tokens:
        load.wait()
    token_in.wait_recv()
    for tile in range(3):
        me.X[0, tile] = me.DO[tile].astype(F32) + time_row(0, tile)

    for part in first:
        part.arrive()

    sends = [token_in, cot_in]

    def send(src, dst, dim):
        copy = me.remote(src, dst, dim)
        sends.append(copy)
        return copy

    def qkv(layer, tile):
        hat, _ = ln_parts(me.X[layer, tile])
        normed = (hat * me.GV[layer, :, :D] + bias(layer, B_S1)).astype(BF)
        slot = 4 if tile == 2 else tile
        lin = [nn(normed, me.Wq[layer, :, :, :, :, :, D * j : D * j + D].reshape(D, D)) for j in range(3)]
        me.Q[layer, tile] = (lin[0] + bias(layer, B_Q)).astype(BF) * jnp.asarray(1.0 / math.sqrt(HEAD_DIM), BF)
        me.KV[layer, 0, slot] = lin[1].astype(BF)
        me.KV[layer, 1, slot] = (lin[2] + bias(layer, B_V)).astype(BF)

    low_lanes = lax.broadcasted_iota(jnp.int32, (TILE, 128), 1) < HEAD_DIM

    def two_heads(pair):
        zero = jnp.zeros_like(pair)
        return jnp.concatenate([jnp.where(low_lanes, pair, zero), jnp.where(low_lanes, zero, pair)], axis=0)

    def place(step, order):
        turn, pair = step // PAIRS, step % PAIRS
        if order == "012":
            tile = turn
        else:
            tile = (turn + 2) % 3
        base = (tile // 2) * 4
        return tile, base, pair, pl.ds(pl.multiple_of(pair * 128, 128), 128)

    def keys_of(layer, which, base, cols):
        return me.KV[layer, which, pl.ds(base, 4), :, cols].reshape(4 * TILE, 128)

    def attend_step(layer, step):
        tile, base, pair, cols = place(step, "012")
        keys, values = keys_of(layer, 0, base, cols), keys_of(layer, 1, base, cols)
        scores = nt(keys, two_heads(me.Q[layer, tile, :, cols]))
        top = jnp.max(scores, axis=0, keepdims=True) * LOG2E
        prob = jnp.exp2(scores * LOG2E - top).astype(BF)
        mixed = nn(jnp.concatenate([values.T, jnp.ones((16, 4 * TILE), BF)], axis=0), prob)
        total = mixed[128:129]
        mixed = mixed[:128] * (1.0 / total)
        me.LSE[layer, tile, pair] = top + jnp.log2(total)
        out = jnp.concatenate([mixed[:HEAD_DIM, :TILE], mixed[HEAD_DIM:, TILE:]], axis=0)
        me.AO[layer, tile, :, cols] = out.T.astype(BF)

    def forward(layer, hooks, ffn_hooks, wait_weights):
        kv = me.KV
        to_y = send(kv.at[layer, :, 4], kv.at[layer, :, 5], "y")
        to_c = [send(kv.at[layer, :, a], kv.at[layer, :, b], "c") for a, b in ((4, 6), (0, 2), (1, 3), (5, 7))]
        qkv(layer, 2)
        to_y.start()
        to_c[0].start()
        qkv(layer, 0)
        to_c[1].start()
        qkv(layer, 1)
        to_c[2].start()
        to_c[1].wait_recv()
        to_c[2].wait_recv()

        def pass_on():
            to_y.wait_recv()
            to_c[3].start()

        def have_all():
            to_c[0].wait_recv()
            to_c[3].wait_recv()

        def step(index, carry):
            at_step(index, hooks + [(7, pass_on), (8, have_all)])
            attend_step(layer, index)
            return carry

        lax.fori_loop(0, 3 * PAIRS, step, 0)
        wait_weights()
        w_out = me.Wo[layer].reshape(D, D)
        for tile in range(3):
            after = me.X[layer, tile] + nn(me.AO[layer, tile], w_out) + bias(layer, B_O)
            me.Y[layer, tile] = after
            hat, _ = ln_parts(after)
            me.N[tile] = (hat * me.GV[layer, :, D:] + bias(layer, B_S2)).astype(BF)
            me.GN[tile] = after + bias(layer, B_D)

        def ffn(slab, carry):
            at_step(slab, ffn_hooks)
            cols = pl.ds(pl.multiple_of(slab * D, D), D)
            w_up = me.Wu[layer, :, :, :, :, :, cols].reshape(D, D)
            w_down = me.Wd[layer, slab].reshape(D, D)
            b_up = me.BV[layer, :, pl.ds(pl.multiple_of(B_U + slab * D, D), D)]
            for tile in range(3):
                up = nn(me.N[tile], w_up) + b_up
                _, tanh = gelu_parts(up)
                me.GN[tile] += nn((0.5 * up * (1.0 + tanh)).astype(BF), w_down)
            return carry

        lax.fori_loop(0, FF // D, ffn, 0)

    def arrive(parts):
        def run():
            for part in parts:
                part.arrive()
        return run

    forward(0, [(0, go(second, 1)), (3, go(second, 2)), (6, go(second, 3)), (9, go(third, 0))], [(2, go(third, 1))], arrive(second))
    for tile in range(3):
        me.X[1, tile] = me.GN[tile] + time_row(1, tile)
    go(third, 2)()
    go(third, 3)()
    arrive(third)()
    forward(1, [], [], lambda: None)
    for tile in range(3):
        me.ACC[0, pl.ds(TILE * tile, TILE)] = me.GN[tile]
    act = [me.ACC.at[0, pl.ds(TILE * tile, TILE)] for tile in range(3)]
    act_out = me.remote(act[1], me.act_o.at[y], "y")
    act_out.start()
    act_own = [me.local(act[0], me.act_o.at[y]), me.local(act[2], me.act_o.at[2])]
    for copy in act_own:
        copy.start()

    cot_in.wait_recv()
    weight_y, weight_2 = me.imp[me.ts[y]], me.imp[me.ts[2]]
    for tile in range(3):
        grad = me.GB[tile].astype(F32) * (weight_2 if tile == 2 else weight_y)
        me.G[tile] = grad
    for part in [steps_all, small, times] + first + second + third:
        part.drain()
    for copy in sends:
        copy.wait_send()
    sends.clear()

    outs = {"q": me.gq_o, "o": me.go_o, "u": me.gu_o, "d": me.gd_o}
    grads = {"q": me.Wq, "o": me.Wo, "u": me.Wu, "d": me.Wd}
    recvs = {
        name: [me.R1[i], me.R2[i], me.R3[i], me.R4[i]] for i, name in enumerate("qoud")
    }

    def bundle(layer, number, names):
        parts = []
        for name in names:
            width = grads[name].shape[-1]
            for half, order in enumerate(("cyxz", "cxyz")):
                cols = slice(half * (width // 2), (half + 1) * (width // 2))
                parts.append(Reduce(me, layer, grads[name], recvs[name], outs[name], cols, order))
        return Bundle(me, number, parts, gives=layer == LAYERS - 1, takes=layer < LAYERS - 1)

    def add_bias(layer, at, value):
        me.BG[layer, :, at : at + value.shape[-1]] += value

    def ln_back(layer, gain_at, shift_at, source, grad):
        hat, scale = ln_parts(source)
        me.GG[layer, :, gain_at : gain_at + D] += rows_sum(grad * hat)
        add_bias(layer, shift_at, rows_sum(grad))
        inner = grad * me.GV[layer, :, gain_at : gain_at + D]
        return scale * (inner - jnp.mean(inner, axis=-1, keepdims=True) - hat * jnp.mean(inner * hat, axis=-1, keepdims=True))

    def normed_t(layer, source, gain_at, shift_at):
        for tile in range(3):
            hat, _ = ln_parts(source[layer, tile])
            normed = (hat * me.GV[layer, :, gain_at : gain_at + D] + bias(layer, shift_at)).astype(BF)
            me.N[tile] = normed
            me.NT[:, TILE * tile : TILE * tile + TILE] = normed.T

    head_of = lax.broadcasted_iota(jnp.int32, (HEADS, D), 1) // HEAD_DIM
    selector = (head_of == lax.broadcasted_iota(jnp.int32, (HEADS, D), 0)).astype(F32)

    def backward(layer, ffn_hooks, up_bundle, before_attn, attn_hooks, qkv_bundle, tail):
        normed_t(layer, me.Y, D, B_S2)
        for tile in range(3):
            me.GB[tile] = me.G[tile].astype(BF)
            add_bias(layer, B_D, rows_sum(me.G[tile]))
            me.GN[tile] = jnp.zeros((TILE, D), F32)

        def ffn(chunk, carry):
            at_step(chunk, ffn_hooks)
            cols = pl.ds(pl.multiple_of(chunk * TILE, TILE), TILE)
            b_cols = pl.ds(pl.multiple_of(B_U + chunk * TILE, TILE), TILE)
            w_up = me.Wu[layer, :, :, :, :, :, cols].reshape(D, TILE)
            w_down = me.Wd[layer, chunk // 2, chunk % 2].reshape(TILE, D)
            total = jnp.zeros((1, TILE), F32)
            for tile in range(3):
                up = nn(me.N[tile], w_up) + me.BV[layer, :, b_cols]
                square, tanh = gelu_parts(up)
                me.A1[pl.ds(TILE * tile, TILE)] = (0.5 * up * (1.0 + tanh)).astype(BF)
                slope = 0.5 * (1.0 + tanh) + (0.5 * GELU_A) * up * (1.0 - tanh * tanh) * (1.0 + 3.0 * GELU_B * square)
                grad_up = nt(me.GB[tile], w_down) * slope
                total = total + rows_sum(grad_up)
                grad_up = grad_up.astype(BF)
                me.A2[pl.ds(TILE * tile, TILE)] = grad_up
                me.GN[tile] += nt(grad_up, w_up)
            me.BG[layer, :, b_cols] += total
            d_down = tn(me.A1[...], me.GB[...].reshape(3 * TILE, D))
            me.Wd[layer, chunk // 2, chunk % 2] = d_down.astype(BF).reshape(2, 2, 64, D)
            d_up = nn(me.NT[...], me.A2[...])
            me.Wu[layer, :, :, :, :, :, cols] = d_up.astype(BF).reshape(n_z, 2, 2, 2, 16, TILE)
            return carry

        lax.fori_loop(0, FF // TILE, ffn, 0)
        for tile in range(3):
            mid = me.G[tile] + ln_back(layer, D, B_S2, me.Y[layer, tile], me.GN[tile])
            me.G[tile] = mid
            add_bias(layer, B_O, rows_sum(mid))
            me.GB[tile] = mid.astype(BF)
        w_out = me.Wo[layer].reshape(D, D)
        for tile in range(3):
            grad_attn = nt(me.GB[tile], w_out).astype(BF)
            me.DO[tile] = grad_attn
            delta = nt(selector, grad_attn.astype(F32) * me.AO[layer, tile].astype(F32), lax.Precision.HIGHEST)
            for pair in range(PAIRS):
                both = jnp.concatenate([delta[2 * pair : 2 * pair + 1], delta[2 * pair + 1 : 2 * pair + 2]], axis=1)
                me.DL[tile, pair] = both
        d_out = tn(me.AO[layer].reshape(3 * TILE, D), me.GB[...].reshape(3 * TILE, D))
        me.Wo[layer] = d_out.astype(BF).reshape(n_z, 2, 2, 2, 16, D)
        up_bundle.step(0)

        before_attn()
        me.ACC[...] = jnp.zeros_like(me.ACC)
        third_c = send(me.PB.at[:, 1:3], me.RB1, "c")
        third_y = send(me.PB.at[:, 0], me.RB2, "y")
        from_c = send(me.PC, me.RB3, "c")

        def third_done():
            me.GN[0:2] = me.ACC[:, 0:TILE]
            me.PB[...] = me.ACC[:, TILE : 4 * TILE].reshape(2, 3, TILE, D).astype(BF)
            me.ACC[...] = jnp.zeros_like(me.ACC)
            third_c.start()

        def third_on():
            third_c.wait_recv()
            me.GN[0:2] += me.RB1[:, 0].astype(F32)
            me.PB[:, 0] = me.PB[:, 0] + me.RB1[:, 1]
            third_y.start()

        def attend_back(step, carry):
            at_step(step, attn_hooks + [(PAIRS, third_done), (PAIRS + 2, third_on)])
            tile, base, pair, cols = place(step, "201")
            keys, values = keys_of(layer, 0, base, cols), keys_of(layer, 1, base, cols)
            queries, grads_o = two_heads(me.Q[layer, tile, :, cols]), two_heads(me.DO[tile, :, cols])
            prob = jnp.exp2(nt(keys, queries) * LOG2E - me.LSE[layer, tile, pair])
            grad_s = (prob * (nt(values, grads_o) - me.DL[tile, pair])).astype(BF)
            me.ACC[1, :, cols] += nn(prob.astype(BF), grads_o)
            me.ACC[0, :, cols] += nn(grad_s, queries)
            d_query = nn(keys.T, grad_s)
            d_query = jnp.concatenate([d_query[:HEAD_DIM, :TILE], d_query[HEAD_DIM:, TILE:]], axis=0).T
            d_query = d_query * (1.0 / math.sqrt(HEAD_DIM))
            me.BG[layer, :, cols] += rows_sum(d_query)
            me.GL[tile, :, cols] = d_query.astype(BF)
            return carry

        lax.fori_loop(0, 3 * PAIRS, attend_back, 0)
        me.PC[...] = me.ACC[:, 2 * TILE :].astype(BF)
        from_c.start()
        normed_t(layer, me.X, 0, B_S1)
        third_y.wait_recv()
        third = me.GN[0:2] + me.RB2[...].astype(F32)
        me.GL[2, :, D : 2 * D] = third[0].astype(BF)
        me.GL[2, :, 2 * D :] = third[1].astype(BF)
        add_bias(layer, B_V, rows_sum(third[1]))
        from_c.wait_recv()
        for tile in range(2):
            rows = slice(TILE * tile, TILE * tile + TILE)
            key = me.ACC[0, rows] + me.RB3[0, rows].astype(F32)
            value = me.ACC[1, rows] + me.RB3[1, rows].astype(F32)
            add_bias(layer, B_V, rows_sum(value))
            me.GL[tile, :, D : 2 * D] = key.astype(BF)
            me.GL[tile, :, 2 * D :] = value.astype(BF)
        w_qkv = me.Wq[layer].reshape(D, 3 * D)
        for tile in range(3):
            me.GN[tile] = nt(me.GL[tile], w_qkv)
        for j in range(3):
            d_qkv = nn(me.NT[...], me.GL[:, :, D * j : D * j + D].reshape(3 * TILE, D))
            me.Wq[layer, :, :, :, :, :, D * j : D * j + D] = d_qkv.astype(BF).reshape(n_z, 2, 2, 2, 16, D)
        qkv_bundle.step(0)
        sums = []
        for tile in (1, 0, 2):
            grad = me.G[tile] + ln_back(layer, 0, B_S1, me.X[layer, tile], me.GN[tile])
            me.G[tile] = grad
            sums.append(rows_sum(grad))
            tail(tile, grad)
        me.TG[layer, 0:1] = sums[0] + sums[1]
        me.TG[layer, 1:2] = sums[2]
        for copy in sends:
            copy.wait_send()
        sends.clear()

    up_1, qkv_1 = bundle(1, 0, "uod"), bundle(1, 1, "q")
    up_0, qkv_0 = bundle(0, 0, "uod"), bundle(0, 1, "q")

    def at(part, stage):
        return lambda: part.step(stage)

    def act_done():
        for copy in act_own + [act_out]:
            copy.wait()

    backward(
        1, [], up_1, act_done, [(1, at(up_1, 1)), (5, at(up_1, 2)), (9, at(up_1, 3))], qkv_1, lambda tile, grad: None
    )
    finals = []

    def out_tile(tile, grad):
        if tile == 1:
            me.GB[1] = grad.astype(BF)
            finals.append(me.remote(me.GB.at[1], me.RB1.at[0, 0], "y"))
        else:
            finals.append(me.local(me.G.at[tile], me.gin_o.at[y if tile == 0 else 2]))
        finals[-1].start()

    backward(
        0,
        [(0, at(up_1, 4)), (1, at(qkv_1, 1)), (3, at(qkv_1, 2)), (5, at(qkv_1, 3)), (7, at(qkv_1, 4))],
        up_0,
        lambda: None,
        [(1, at(up_0, 1)), (5, at(up_0, 2)), (9, at(up_0, 3))],
        qkv_0,
        out_tile,
    )

    seq_row = lax.broadcasted_iota(jnp.int32, (24, 128), 0)
    for gz in range(n_z):
        tables = []
        for layer in range(LAYERS):
            lanes = slice(128 * gz, 128 * gz + 128)
            first_seq = jnp.where(seq_row == 3 * me.dp + y, me.TG[layer, 0:1, lanes], 0.0)
            tables.append(jnp.where(seq_row == 3 * me.dp + 2, me.TG[layer, 1:2, lanes], first_seq))
        for gx in range(2):
            dp = 2 * gz + gx
            for layer in range(LAYERS):
                for r in range(5):
                    at_lane = (5 * dp + r) * 128
                    me.SR[gz, gx, 6 * layer + r : 6 * layer + r + 1] = me.BG[layer, :, at_lane : at_lane + 128]
                me.SR[gz, gx, 6 * layer + 5 : 6 * layer + 6] = me.GG[layer, :, 128 * dp : 128 * dp + 128]
                me.SR[gz, gx, 16 + 24 * layer : 40 + 24 * layer] = tables[layer]
            me.SR[gz, gx, 12:16] = jnp.zeros((4, 128), F32)
    small_x = me.remote(me.SR.at[:, me.other["x"]], me.SX, "x")
    small_x.start()
    qkv_0.step(1)
    small_x.wait_recv()
    for gz in range(n_z):
        me.SR[gz, x] = me.SR[gz, x] + me.SX[gz]
    small_z = [me.remote(me.SR.at[me.around[hop], x], me.SZ.at[hop - 1], "z", hop) for hop in me.hops("z")]
    for copy in small_z:
        copy.start()
    qkv_0.step(2)
    up_0.step(4)
    finals[0].wait()
    me.GN[0] = me.RB1[0, 0].astype(F32)
    last = me.local(me.GN.at[0], me.gin_o.at[me.other["y"]])
    last.start()
    for copy in small_z:
        copy.wait_recv()
    total = me.SR[z, x]
    for hop in me.hops("z"):
        total = total + me.SZ[hop - 1]
    me.SY[0] = total
    small_y = me.remote(me.SY.at[0], me.SY.at[1], "y")
    small_y.start()
    qkv_0.step(3)
    small_y.wait_recv()
    me.SY[2] = me.SY[0] + me.SY[1]
    small_c = me.remote(me.SY.at[2], me.SY.at[3], "c")
    small_c.start()
    small_c.wait_recv()
    me.small_o[...] = me.SY[2] + me.SY[3]
    qkv_0.step(4)

    for copy in [small_x, small_y, small_c] + small_z:
        copy.wait_send()
    for copy in finals[1:]:
        copy.wait()
    last.wait()
    for part in (up_1, qkv_1, up_0, qkv_0):
        part.drain()


def fused_call(n_z, *operands):
    any_space, vmem, smem = (pl.BlockSpec(memory_space=space) for space in (pl.ANY, pltpu.VMEM, pltpu.SMEM))
    cube = (n_z, 2, 2, 2)
    tokens = (3, TILE, D)
    sizes = ((16, 3 * D), (16, D), (16, FF), (64, D))

    def many(lead):
        return [tuple(pltpu.VMEM((*lead, *size), BF) for size in sizes)]

    flat, tree = jax.tree.flatten(
        [pltpu.VMEM((LAYERS, *cube, *size), BF) for size in sizes]
        + [
            pltpu.VMEM((*cube, 16, 128), BF),
            pltpu.VMEM((*cube, 48, 128), BF),
            pltpu.VMEM((n_z, 2, 32, 128), jnp.int32),
            pltpu.VMEM((LAYERS, 8, D), F32),
            pltpu.VMEM((LAYERS, 1, 6 * D + FF), F32),
            pltpu.VMEM((LAYERS, 1, 2 * D), F32),
            pltpu.VMEM((LAYERS, 1, 6 * D + FF), F32),
            pltpu.VMEM((LAYERS, 1, 2 * D), F32),
            pltpu.VMEM((LAYERS, 8, D), F32),
            pltpu.VMEM((LAYERS, *tokens), F32),
            pltpu.VMEM(tokens, BF),
            pltpu.VMEM((D, 3 * TILE), BF),
            pltpu.VMEM((LAYERS, *tokens), BF),
            pltpu.VMEM((LAYERS, 2, 8, TILE, D), BF),
            pltpu.VMEM((LAYERS, *tokens), BF),
            pltpu.VMEM((LAYERS, 3, PAIRS, 1, 2 * TILE), F32),
            pltpu.VMEM((3, PAIRS, 1, 2 * TILE), F32),
            pltpu.VMEM((LAYERS, *tokens), F32),
            pltpu.VMEM(tokens, BF),
            pltpu.VMEM(tokens, BF),
            pltpu.VMEM(tokens, F32),
            pltpu.VMEM(tokens, F32),
            pltpu.VMEM((3, TILE, 3 * D), BF),
            pltpu.VMEM((2, 4 * TILE, D), F32),
            pltpu.VMEM((2, 3, TILE, D), BF),
            pltpu.VMEM((2, 2 * TILE, D), BF),
            pltpu.VMEM((2, 2, TILE, D), BF),
            pltpu.VMEM((2, TILE, D), BF),
            pltpu.VMEM((2, 2 * TILE, D), BF),
            pltpu.VMEM((3 * TILE, TILE), BF),
            pltpu.VMEM((3 * TILE, TILE), BF),
        ]
        + many((n_z, 2, 2))
        + many((n_z, 2))
        + many((n_z,))
        + many((n_z - 1,))
        + [
            pltpu.VMEM((n_z, 2, 64, 128), F32),
            pltpu.VMEM((n_z, 64, 128), F32),
            pltpu.VMEM((n_z - 1, 64, 128), F32),
            pltpu.VMEM((4, 64, 128), F32),
            pltpu.SemaphoreType.DMA((N_SEMS,)),
            pltpu.SemaphoreType.DMA((N_SEMS,)),
            pltpu.SemaphoreType.DMA((32,)),
            pltpu.SemaphoreType.REGULAR((2, 4, 2)),
        ]
    )
    outs = [
        jax.ShapeDtypeStruct(tokens, F32),
        jax.ShapeDtypeStruct(tokens, F32),
        *[jax.ShapeDtypeStruct((LAYERS, *size), F32) for size in sizes],
        jax.ShapeDtypeStruct((64, 128), F32),
        jax.ShapeDtypeStruct((32, 128), jnp.int32),
    ]

    def run(*refs):
        head = len(operands) + len(outs)
        fused_kernel(n_z, *refs[:head], *jax.tree.unflatten(tree, refs[head:]))

    return pl.pallas_call(
        run,
        out_shape=outs,
        in_specs=[smem, smem] + [any_space] * 6 + [vmem] * 2,
        out_specs=[any_space] * 2 + [vmem] * 6,
        scratch_shapes=flat,
        compiler_params=pltpu.CompilerParams(collective_id=0, has_side_effects=True, vmem_limit_bytes=VMEM_BYTES),
    )(*operands)


VMEM_BYTES = 63 * 1024 * 1024


def fused_body(
    inputs, cotangent, w_qkv, w_out, w_up, w_down, norm_gains, biases, time_table, timesteps, importance
):
    n_z = lax.axis_size("dp") // 2
    seq = lax.axis_index("seq")
    mine = (jnp.arange(4) == seq)[None, :, None]
    bias_rows = jnp.where(mine, biases[:, None, :], 0).reshape(LAYERS, 5, 128)
    gain_rows = jnp.where(mine, norm_gains[:, None, :], 0).reshape(LAYERS, 1, 128)
    small = jnp.concatenate([bias_rows, gain_rows], axis=1).reshape(6 * LAYERS, 128)
    small = jnp.pad(small, ((0, 16 - 6 * LAYERS), (0, 0))).astype(BF)
    act, grad_in, g_qkv, g_out, g_up, g_down, sums, steps = fused_call(
        n_z, timesteps, importance, jnp.swapaxes(inputs, 0, 1), jnp.swapaxes(cotangent, 0, 1),
        w_qkv, w_out, w_up, w_down, small, time_table,
    )
    rows = sums[: 6 * LAYERS].reshape(LAYERS, 6, 128)
    grad_biases = lax.dynamic_slice_in_dim(rows[:, :5].reshape(LAYERS, 640), 160 * seq, 160, 1)
    grad_gains = lax.dynamic_slice_in_dim(rows[:, 5], 32 * seq, 32, 1)
    place = (lax.axis_index("dp") % 2) * 4 + seq
    table_rows = lax.dynamic_slice_in_dim(sums[16:].reshape(LAYERS, 24, 128), 16 * place, 16, 2)
    onehot = (jnp.arange(STEPS, dtype=jnp.int32)[:, None] == steps[:24, 0][None, :]).astype(F32)
    grad_table = jnp.einsum("tj,ljf->ltf", onehot, table_rows, precision=HIGH)
    return (
        jnp.swapaxes(act, 0, 1), jnp.swapaxes(grad_in, 0, 1), g_qkv, g_out, g_up, g_down, grad_gains, grad_biases, grad_table,
    )


def solution(mesh):
    devices = mesh.shape["dp"] * mesh.shape["seq"]
    whole_tiles = mesh.shape["seq"] == 4 and mesh.shape["dp"] % 2 == 0 and D // devices == 16
    in_specs = (
        P("seq", "dp", None),
        P("seq", "dp", None),
        P(None, ("dp", "seq"), None),
        P(None, ("dp", "seq"), None),
        P(None, ("dp", "seq"), None),
        P(None, ("dp", "seq"), None),
        P(None, ("dp", "seq")),
        P(None, ("dp", "seq")),
        P(None, None, ("dp", "seq")),
        P("dp"),
        P(),
    )
    out_specs = (
        P("seq", "dp", None),
        P("seq", "dp", None),
        P(None, ("dp", "seq"), None),
        P(None, ("dp", "seq"), None),
        P(None, ("dp", "seq"), None),
        P(None, ("dp", "seq"), None),
        P(None, ("dp", "seq")),
        P(None, ("dp", "seq")),
        P(None, None, ("dp", "seq")),
    )
    return jax.shard_map(
        fused_body if whole_tiles else body, mesh=mesh, in_specs=in_specs, out_specs=out_specs, check_vma=False)
```

```python
import functools
import math

import jax
import jax.numpy as jnp
from jax import lax
from jax.experimental import pallas as pl
from jax.experimental.pallas import tpu as pltpu
from jax.sharding import PartitionSpec as P

D = 512
HEADS = 8
HEAD_DIM = 64
FF = 2048
STEPS = 1000
LAYERS = 2


EPS = 1e-05
HIGH = lax.Precision.HIGHEST


def layer_norm(values, gain_vec, bias_vec):
    centered = values - jnp.mean(values, axis=-1, keepdims=True)
    spread = jnp.mean(centered * centered, axis=-1, keepdims=True)
    return centered * lax.rsqrt(spread + EPS) * gain_vec + bias_vec


def attend(queries, keys_all, values_all):
    row_count, seq_count, model_width = queries.shape
    score_scale = 1.0 / math.sqrt(HEAD_DIM)

    def per_seq(seq_index, loop_state):
        outputs, log_tot = loop_state
        query_per_head = lax.dynamic_index_in_dim(queries, seq_index, 1, keepdims=False).reshape(
            row_count, HEADS, HEAD_DIM
        )
        key_per_head = lax.dynamic_index_in_dim(keys_all, seq_index, 1, keepdims=False).reshape(
            -1, HEADS, HEAD_DIM
        )
        value_per_head = lax.dynamic_index_in_dim(values_all, seq_index, 1, keepdims=False).reshape(
            -1, HEADS, HEAD_DIM
        )
        scores = (
            jnp.einsum(
                "xsv,usv->sxu", query_per_head, key_per_head, preferred_element_type=jnp.float32
            )
            * score_scale
        )
        row_max = jnp.max(scores, axis=-1, keepdims=True)
        expon = jnp.exp(scores - row_max)
        summed = jnp.sum(expon, axis=-1, keepdims=True)
        attention_probability = (expon / summed).astype(jnp.bfloat16)
        attn_out = jnp.einsum(
            "gir,rgo->igo",
            attention_probability,
            value_per_head,
            preferred_element_type=jnp.float32,
        )
        attn_out = attn_out.astype(jnp.bfloat16).reshape(row_count, 1, model_width)
        outputs = lax.dynamic_update_slice_in_dim(outputs, attn_out, seq_index, 1)
        log_tot = lax.dynamic_update_slice_in_dim(
            log_tot, (row_max + jnp.log(summed))[None, :, :, 0], seq_index, 0
        )
        return (outputs, log_tot)

    start_state = (
        jnp.zeros(queries.shape, jnp.bfloat16),
        jnp.zeros((seq_count, HEADS, row_count), jnp.float32),
    )
    return lax.fori_loop(0, seq_count, per_seq, start_state)


def attend_back(queries, keys_all, values_all, log_tot, grad_attn):
    row_count, seq_count, model_width = queries.shape
    key_count = keys_all.shape[0]
    score_scale = 1.0 / math.sqrt(HEAD_DIM)

    def per_seq(seq_index, loop_state):
        grad_query, part_key, part_value = loop_state
        query_per_head = lax.dynamic_index_in_dim(queries, seq_index, 1, keepdims=False).reshape(
            row_count, HEADS, HEAD_DIM
        )
        key_per_head = lax.dynamic_index_in_dim(keys_all, seq_index, 1, keepdims=False).reshape(
            key_count, HEADS, HEAD_DIM
        )
        value_per_head = lax.dynamic_index_in_dim(values_all, seq_index, 1, keepdims=False).reshape(
            key_count, HEADS, HEAD_DIM
        )
        hidden_state_gradient = lax.dynamic_index_in_dim(
            grad_attn, seq_index, 1, keepdims=False
        ).reshape(row_count, HEADS, HEAD_DIM)
        log_seq = lax.dynamic_index_in_dim(log_tot, seq_index, 0, keepdims=False)
        scores = (
            jnp.einsum(
                "xsv,usv->sxu", query_per_head, key_per_head, preferred_element_type=jnp.float32
            )
            * score_scale
        )
        attn_f = jnp.exp(scores - log_seq[:, :, None])
        attention_probability = attn_f.astype(jnp.bfloat16)
        value_part = jnp.einsum(
            "uxo,xuc->ouc",
            attention_probability,
            hidden_state_gradient,
            preferred_element_type=jnp.float32,
        )
        probability_gradient = jnp.einsum(
            "xsv,usv->sxu",
            hidden_state_gradient,
            value_per_head,
            preferred_element_type=jnp.float32,
        )
        row_delta = jnp.sum(probability_gradient * attn_f, axis=-1, keepdims=True)
        score_gradient = (attn_f * (probability_gradient - row_delta)).astype(jnp.bfloat16)
        query_part = (
            jnp.einsum(
                "gir,rgo->igo", score_gradient, key_per_head, preferred_element_type=jnp.float32
            )
            * score_scale
        )
        key_part = (
            jnp.einsum(
                "uxo,xuc->ouc", score_gradient, query_per_head, preferred_element_type=jnp.float32
            )
            * score_scale
        )
        grad_query = lax.dynamic_update_slice_in_dim(
            grad_query, query_part.reshape(row_count, 1, model_width), seq_index, 1
        )
        part_key = lax.dynamic_update_slice_in_dim(
            part_key, key_part.reshape(key_count, 1, model_width), seq_index, 1
        )
        part_value = lax.dynamic_update_slice_in_dim(
            part_value, value_part.reshape(key_count, 1, model_width), seq_index, 1
        )
        return (grad_query, part_key, part_value)

    start_state = (
        jnp.zeros(queries.shape, jnp.float32),
        jnp.zeros(keys_all.shape, jnp.float32),
        jnp.zeros(keys_all.shape, jnp.float32),
    )
    return lax.fori_loop(0, seq_count, per_seq, start_state)


def forward_layer(hidden, fetched, onehot):
    mat_qkv, mat_out, up_matrix, down_matrix, gain_row, bias_row, time_rows = fetched
    gain_f = gain_row.astype(jnp.float32)
    bias_f = bias_row.astype(jnp.float32)
    seq_embed = jnp.dot(onehot.astype(jnp.bfloat16), time_rows, preferred_element_type=jnp.float32)
    summed_in = hidden + seq_embed[None]
    normed_one = layer_norm(summed_in, gain_f[:D], bias_f[4 * D + FF : 5 * D + FF]).astype(
        jnp.bfloat16
    )
    linear = jnp.dot(normed_one, mat_qkv, preferred_element_type=jnp.float32)
    queries = (linear[..., :D] + bias_f[:D]).astype(jnp.bfloat16)
    keys_loc = linear[..., D : 2 * D].astype(jnp.bfloat16)
    values_loc = (linear[..., 2 * D :] + bias_f[D : 2 * D]).astype(jnp.bfloat16)
    keys_all, values_all = (
        lax.all_gather(keys_loc, "seq", axis=0, tiled=True),
        lax.all_gather(values_loc, "seq", axis=0, tiled=True),
    )
    attn_out, log_tot = attend(queries, keys_all, values_all)
    after_attn = (
        summed_in
        + jnp.dot(attn_out, mat_out, preferred_element_type=jnp.float32)
        + bias_f[2 * D : 3 * D]
    )
    second_normalized = layer_norm(after_attn, gain_f[D:], bias_f[5 * D + FF :]).astype(
        jnp.bfloat16
    )
    upward = (
        jnp.dot(second_normalized, up_matrix, preferred_element_type=jnp.float32)
        + bias_f[3 * D : 3 * D + FF]
    )
    gelu_output = jax.nn.gelu(upward).astype(jnp.bfloat16)
    result = (
        after_attn
        + jnp.dot(gelu_output, down_matrix, preferred_element_type=jnp.float32)
        + bias_f[3 * D + FF : 4 * D + FF]
    )
    record = (
        summed_in,
        normed_one,
        queries,
        keys_loc,
        values_loc,
        attn_out,
        log_tot,
        after_attn,
        second_normalized,
        upward,
        gelu_output,
        keys_all,
        values_all,
    )
    return (result, record)


def backward_layer(hidden_state_gradient, fetched, record, onehot, kv_pair):
    mat_qkv = fetched[0]
    mat_out = fetched[1]
    up_matrix = fetched[2]
    down_matrix = fetched[3]
    gain_f = fetched[4].astype(jnp.float32)
    bias_f = fetched[5].astype(jnp.float32)
    summed_in, normed_one, queries = (record[0], record[1], record[2])
    attn_out, log_tot, after_attn = (record[5], record[6], record[7])
    second_normalized, upward, gelu_output = (record[8], record[9], record[10])
    keys_all, values_all = kv_pair
    gradient_bfloat = hidden_state_gradient.astype(jnp.bfloat16)
    down_weight_gradient = jnp.einsum(
        "awt,awg->tg", gelu_output, gradient_bfloat, preferred_element_type=jnp.float32
    )
    bias_down = jnp.sum(hidden_state_gradient, axis=(0, 1))
    activation_gradient = jnp.einsum(
        "ngb,rb->ngr", gradient_bfloat, down_matrix, preferred_element_type=jnp.float32
    )
    _, gelu_back = jax.vjp(jax.nn.gelu, upward)
    grad_upward = gelu_back(activation_gradient)[0]
    bias_up = jnp.sum(grad_upward, axis=(0, 1))
    upward_bfloat = grad_upward.astype(jnp.bfloat16)
    up_weight_gradient = jnp.einsum(
        "xew,xem->wm", second_normalized, upward_bfloat, preferred_element_type=jnp.float32
    )
    second_norm_gradient = jnp.einsum(
        "iyv,tv->iyt", upward_bfloat, up_matrix, preferred_element_type=jnp.float32
    )
    _, second_back = jax.vjp(layer_norm, after_attn, gain_f[D:], bias_f[5 * D + FF :])
    from_second, gain_two, shift_two = second_back(second_norm_gradient)
    grad_mid = hidden_state_gradient + from_second
    mid_bf = grad_mid.astype(jnp.bfloat16)
    grad_out = jnp.einsum("lsc,lsd->cd", attn_out, mid_bf, preferred_element_type=jnp.float32)
    bias_out = jnp.sum(grad_mid, axis=(0, 1))
    grad_attn = jnp.einsum(
        "lsd,cd->lsc", mid_bf, mat_out, preferred_element_type=jnp.float32
    ).astype(jnp.bfloat16)
    grad_query, part_key, part_value = attend_back(
        queries, keys_all, values_all, log_tot, grad_attn
    )
    grad_key, grad_value = (
        lax.psum_scatter(
            part_key.astype(jnp.bfloat16), "seq", scatter_dimension=0, tiled=True
        ).astype(jnp.float32),
        lax.psum_scatter(
            part_value.astype(jnp.bfloat16), "seq", scatter_dimension=0, tiled=True
        ).astype(jnp.float32),
    )
    bias_query = jnp.sum(grad_query, axis=(0, 1))
    bias_value = jnp.sum(grad_value, axis=(0, 1))
    grad_linear = jnp.concatenate([grad_query, grad_key, grad_value], axis=-1).astype(jnp.bfloat16)
    grad_qkv = jnp.einsum(
        "lsc,lse->ce", normed_one, grad_linear, preferred_element_type=jnp.float32
    )
    grad_norm_one = jnp.einsum(
        "lse,ce->lsc", grad_linear, mat_qkv, preferred_element_type=jnp.float32
    )
    _, first_back = jax.vjp(layer_norm, summed_in, gain_f[:D], bias_f[4 * D + FF : 5 * D + FF])
    from_first, gain_one, shift_one = first_back(grad_norm_one)
    grad_in = grad_mid + from_first
    grad_table = jnp.dot(onehot.T, jnp.sum(grad_in, axis=0), precision=HIGH)
    grad_gain = jnp.concatenate([gain_one, gain_two])
    grad_bias = jnp.concatenate(
        [bias_query, bias_value, bias_out, bias_up, bias_down, shift_one, shift_two]
    )
    return (
        grad_in,
        (
            grad_qkv,
            grad_out,
            up_weight_gradient,
            down_weight_gradient,
            grad_gain,
            grad_bias,
            grad_table,
        ),
    )


def body(
    inputs,
    cotangent,
    w_qkv,
    w_out,
    w_up,
    w_down,
    norm_gains,
    biases,
    time_table,
    timesteps,
    importance,
):
    onehot = (timesteps[:, None] == jnp.arange(STEPS, dtype=jnp.int32)[None, :]).astype(jnp.float32)
    seq_weight = jnp.dot(onehot, importance, precision=HIGH)
    hidden = inputs.astype(jnp.float32)
    records = []
    fetched_all = []
    for layer_id in range(LAYERS):
        fetched = (
            lax.all_gather(w_qkv[layer_id], ("dp", "seq"), axis=0, tiled=True),
            lax.all_gather(w_out[layer_id], ("dp", "seq"), axis=0, tiled=True),
            lax.all_gather(w_up[layer_id], ("dp", "seq"), axis=0, tiled=True),
            lax.all_gather(w_down[layer_id], ("dp", "seq"), axis=0, tiled=True),
            lax.all_gather(norm_gains[layer_id], ("dp", "seq"), axis=0, tiled=True),
            lax.all_gather(biases[layer_id], ("dp", "seq"), axis=0, tiled=True),
            lax.all_gather(time_table[layer_id], ("dp", "seq"), axis=1, tiled=True),
        )
        hidden, record = forward_layer(hidden, fetched, onehot)
        records.append(record)
        fetched_all.append(fetched)
    hidden_state_gradient = cotangent.astype(jnp.float32) * seq_weight[None, :, None]
    shards = [None] * LAYERS
    for layer_id in reversed(range(LAYERS)):
        record = records[layer_id]
        fetched = (
            lax.all_gather(w_qkv[layer_id], ("dp", "seq"), axis=0, tiled=True),
            lax.all_gather(w_out[layer_id], ("dp", "seq"), axis=0, tiled=True),
            lax.all_gather(w_up[layer_id], ("dp", "seq"), axis=0, tiled=True),
            lax.all_gather(w_down[layer_id], ("dp", "seq"), axis=0, tiled=True),
            lax.all_gather(norm_gains[layer_id], ("dp", "seq"), axis=0, tiled=True),
            lax.all_gather(biases[layer_id], ("dp", "seq"), axis=0, tiled=True),
            lax.all_gather(time_table[layer_id], ("dp", "seq"), axis=1, tiled=True),
        )
        kv_pair = (
            lax.all_gather(record[3], "seq", axis=0, tiled=True),
            lax.all_gather(record[4], "seq", axis=0, tiled=True),
        )
        hidden_state_gradient, grads = backward_layer(
            hidden_state_gradient, fetched, record, onehot, kv_pair
        )
        shards[layer_id] = (
            lax.psum_scatter(grads[0], ("dp", "seq"), scatter_dimension=0, tiled=True),
            lax.psum_scatter(grads[1], ("dp", "seq"), scatter_dimension=0, tiled=True),
            lax.psum_scatter(grads[2], ("dp", "seq"), scatter_dimension=0, tiled=True),
            lax.psum_scatter(grads[3], ("dp", "seq"), scatter_dimension=0, tiled=True),
            lax.psum_scatter(grads[4], ("dp", "seq"), scatter_dimension=0, tiled=True),
            lax.psum_scatter(grads[5], ("dp", "seq"), scatter_dimension=0, tiled=True),
            lax.psum_scatter(grads[6], ("dp", "seq"), scatter_dimension=1, tiled=True),
        )
    stacked = [
        jnp.stack([shards[layer_id][member] for layer_id in range(LAYERS)]) for member in range(7)
    ]
    return (
        hidden,
        hidden_state_gradient,
        stacked[0],
        stacked[1],
        stacked[2],
        stacked[3],
        stacked[4],
        stacked[5],
        stacked[6],
    )


MESH_ID = pl.DeviceIdType.MESH
LOG2E = 1.4426950408889634
F32 = jnp.float32
BF = jnp.bfloat16
TILE = 256
PAIRS = HEADS // 2
N_SEMS = 272
GELU_A = math.sqrt(2.0 / math.pi)
GELU_B = 0.044715

B_Q, B_V, B_O, B_U, B_D, B_S1, B_S2 = 0, D, 2 * D, 3 * D, 3 * D + FF, 4 * D + FF, 5 * D + FF


def nn(left, right):
    return jnp.dot(left, right, preferred_element_type=F32)


def nt(left, right, precision=None):
    return lax.dot_general(left, right, (((1,), (1,)), ((), ())), preferred_element_type=F32, precision=precision)


def tn(left, right):
    return lax.dot_general(left, right, (((0,), (0,)), ((), ())), preferred_element_type=F32)


def rows_sum(value):
    return jnp.sum(value, axis=0, keepdims=True)


def ln_parts(value):
    centered = value - jnp.mean(value, axis=-1, keepdims=True)
    scale = lax.rsqrt(jnp.mean(centered * centered, axis=-1, keepdims=True) + EPS)
    return centered * scale, scale


def gelu_parts(up):
    square = up * up
    tanh = jnp.tanh(GELU_A * up * (1.0 + GELU_B * square))
    return square, tanh


class Fused:
    def __init__(self, n_z, refs):
        (self.ts, self.imp, self.xin, self.cot, self.wq_i, self.wo_i, self.wu_i, self.wd_i, self.sm_i, self.tab,
         self.act_o, self.gin_o, self.gq_o, self.go_o, self.gu_o, self.gd_o, self.small_o, self.t24_o,
         self.Wq, self.Wo, self.Wu, self.Wd, self.SM, self.TS, self.TT, self.TR, self.BV, self.GV, self.BG, self.GG,
         self.TG, self.X, self.N, self.NT, self.Q, self.KV, self.AO, self.LSE, self.DL, self.Y, self.GB, self.DO, self.G,
         self.GN, self.GL, self.ACC, self.OWN, self.PB, self.PC, self.RB1, self.RB2, self.RB3, self.A1, self.A2,
         self.R1, self.R2, self.R3, self.R4, self.SR, self.SX, self.SZ, self.SY,
         self.ssem, self.rsem, self.lsem, self.credit) = refs
        dp, seq = lax.axis_index("dp"), lax.axis_index("seq")
        self.n_z = n_z
        self.dp, self.seq = dp, seq
        self.z, self.x, self.y, self.c = dp // 2, dp % 2, seq // 2, seq % 2
        self.next_sem = 0
        self.next_local = 0
        self.mine = {"z": self.z, "x": self.x, "y": self.y, "c": self.c}
        self.other = {"x": 1 - self.x, "y": 1 - self.y, "c": 1 - self.c}
        self.around = [(self.z + hop) % n_z for hop in range(n_z)]
        self.device = {("z", hop): {"dp": self.around[hop] * 2 + self.x, "seq": seq} for hop in range(1, n_z)}
        self.device["x", 1] = {"dp": self.z * 2 + self.other["x"], "seq": seq}
        self.device["y", 1] = {"dp": dp, "seq": self.other["y"] * 2 + self.c}
        self.device["c", 1] = {"dp": dp, "seq": self.y * 2 + self.other["c"]}

    def hops(self, dim):
        return range(1, self.n_z) if dim == "z" else range(1, 2)

    def enter(self):
        barrier = pltpu.get_barrier_semaphore()
        who = [(dim, hop) for dim in "zxyc" for hop in self.hops(dim)]
        for dim, hop in who:
            pl.semaphore_signal(barrier, inc=1, device_id=self.device[dim, hop], device_id_type=MESH_ID)
        pl.semaphore_wait(barrier, len(who))

    def remote(self, src, dst, dim, hop=1):
        number = self.next_sem
        self.next_sem += 1
        return pltpu.make_async_remote_copy(
            src, dst, self.ssem.at[number], self.rsem.at[number], device_id=self.device[dim, hop], device_id_type=MESH_ID
        )

    def local(self, src, dst):
        number = self.next_local
        self.next_local += 1
        return pltpu.make_async_copy(src, dst, self.lsem.at[number])


class Gather:
    def __init__(self, me, view, order):
        self.copies = []
        for stage, dim in enumerate(order):
            block = view(*[slice(None) if other in order[:stage] else me.mine[other] for other in "zxyc"])
            self.copies.append([me.remote(block, block, dim, hop) for hop in me.hops(dim)])

    def start(self, stage):
        if stage:
            self.arrive(stage - 1)
        for copy in self.copies[stage]:
            copy.start()

    def arrive(self, stage=-1):
        for copy in self.copies[stage]:
            copy.wait_recv()

    def drain(self):
        for copies in self.copies:
            for copy in copies:
                copy.wait_send()


class Reduce:
    def __init__(self, me, layer, grad, recv, out, cols, order, number):
        self.me, self.layer, self.grad, self.recv, self.out, self.cols, self.order = me, layer, grad, recv, out, cols, order
        self.number = number
        self.copies = [self.build(stage) for stage in range(4)]

    def block(self, fixed):
        return tuple(fixed.get(dim, slice(None)) for dim in "zxyc")

    def kept(self, stage):
        return {dim: self.me.mine[dim] for dim in self.order[:stage]}

    def build(self, stage):
        me, dim = self.me, self.order[stage]
        fixed = self.kept(stage)
        copies = []
        for hop in me.hops(dim):
            fixed[dim] = me.around[hop] if dim == "z" else me.other[dim]
            src = self.grad.at[(self.layer, *self.block(fixed), slice(None), self.cols)]
            dst = self.recv[stage].at[(*self.landing(stage, hop), slice(None), self.cols)]
            copies.append(me.remote(src, dst, dim, hop))
        return copies

    def landing(self, stage, hop):
        if stage == 3:
            return (hop - 1,)
        if self.order[stage] == "z":
            return (slice(2 * hop - 2, 2 * hop),)
        return (slice(0, self.me.n_z),) + (slice(None),) * (2 - stage)

    def start(self, stage):
        me = self.me
        if stage:
            self.add(stage - 1)
            dim = self.order[stage - 1]
            if self.layer == LAYERS - 1:
                for hop in me.hops(dim):
                    pl.semaphore_signal(
                        me.credit.at[self.number, stage - 1], inc=1, device_id=me.device[dim, hop], device_id_type=MESH_ID
                    )
        if stage < 4:
            if self.layer < LAYERS - 1:
                pl.semaphore_wait(me.credit.at[self.number, stage], len(me.hops(self.order[stage])))
            for copy in self.copies[stage]:
                copy.start()

    def add(self, stage):
        me, dim = self.me, self.order[stage]
        for copy in self.copies[stage]:
            copy.wait_recv()
        fixed = self.kept(stage + 1)
        if stage == 3 or dim == "z":
            where = (self.layer, *self.block(fixed), slice(None), self.cols)
            total = self.grad[where].astype(F32)
            for hop in me.hops(dim):
                total = total + self.recv[stage][(*self.landing(stage, hop), slice(None), self.cols)].astype(F32)
            if stage == 3:
                self.out[self.layer, :, self.cols] = total
            else:
                self.grad[where] = total.astype(BF)
            return

        def one(z, carry):
            where = (self.layer, *self.block({**fixed, "z": z}), slice(None), self.cols)
            came = (z,) + (slice(None),) * (2 - stage) + (slice(None), self.cols)
            self.grad[where] = self.grad[where] + self.recv[stage][came]
            return carry

        lax.fori_loop(0, me.n_z, one, 0)

    def drain(self):
        for copies in self.copies:
            for copy in copies:
                copy.wait_send()


def at_step(index, hooks):
    for when, action in hooks:
        pl.when(index == when)(action)


FORWARD_AT = (7, 30)
BACKWARD_AT = (31, 0)
END_AT = 62
GATHER_AT = (
    (0, 1, 3, 4),
    (0, 2, 3, 5),
    (1, 13, 17, 20),
    (13, 15, 19, 21),
    (4, 7, 17, 22),
    (2, 3, 7, 14),
    (2, 4, 6, 19),
    (2, 4, 8, 20),
    (9, 15, 20, 29),
    (9, 11, 20, 25),
    (8, 14, 20, 32),
    (2, 5, 24, 34),
    (5, 26, 39, 47),
    (16, 22, 31, 40),
    (28, 35, 42, 47),
    (4, 20, 29, 32),
    (2, 3, 3, 4),
)
REDUCE_AT = (
    (8, 10, 16, 24, 42),
    (12, 17, 24, 31, 44),
    (16, 25, 35, 43, 48),
    (15, 17, 24, 29, 43),
    (12, 16, 24, 48, 55),
    (16, 33, 45, 55, 57),
    (25, 33, 48, 52, 57),
    (25, 31, 35, 40, 55),
    (34, 39, 52, 57, 60),
    (37, 42, 47, 55, 61),
    (39, 41, 48, 55, 65),
    (39, 50, 55, 62, 64),
    (36, 47, 52, 56, 65),
    (44, 46, 51, 59, 62),
    (43, 46, 57, 62, 63),
    (47, 54, 56, 60, 62),
    (56, 57, 62, 63, 66),
    (62, 62, 63, 64, 66),
    (59, 60, 63, 64, 66),
    (58, 59, 62, 63, 64),
)

ORDERS = ("zxyc", "zyxc")
SMALL = "small"


def by_place(moves, places):
    timeline = {}
    for move, stages in zip(moves, places, strict=True):
        for stage, place in enumerate(stages):
            timeline.setdefault(place, []).append((move, stage))
    return timeline


def fused_kernel(n_z, *refs):
    me = Fused(n_z, refs)
    x, y, z, c = me.x, me.y, me.z, me.c
    n_dp = 2 * n_z
    spare = slice(None)

    mats = ((me.wq_i, me.Wq), (me.wo_i, me.Wo), (me.wu_i, me.Wu), (me.wd_i, me.Wd))
    loads = [me.local(src.at[layer], dst.at[layer, z, x, y, c]) for layer in range(LAYERS) for src, dst in mats]
    loads.append(me.local(me.sm_i, me.SM.at[z, x, y, c]))
    for load in loads:
        load.start()
    own_tokens = [
        me.local(src.at[seq], dst.at[tile]) for src, dst in ((me.xin, me.DO), (me.cot, me.GB)) for seq, tile in ((y, 0), (2, 2))
    ]
    for load in own_tokens:
        load.start()

    row = lax.broadcasted_iota(jnp.int32, (32, 128), 0)
    steps = jnp.zeros((32, 128), jnp.int32)
    for j in range(3):
        steps = jnp.where(row == 3 * me.dp + j, me.ts[j], steps)
    me.TT[z, x] = steps
    me.BG[...] = jnp.zeros_like(me.BG)
    me.GG[...] = jnp.zeros_like(me.GG)

    me.enter()
    for load in loads:
        load.wait()

    def weight(layer, ref, order, cols):
        return Gather(me, lambda *where: ref.at[(layer, *where, spare, cols)], order)

    grads = {"q": me.Wq, "o": me.Wo, "u": me.Wu, "d": me.Wd}

    steps_all = Gather(me, lambda gz, gx, gy, gc: me.TT.at[gz, gx], "zx")
    small = Gather(me, lambda *where: me.SM.at[where], "zxyc")
    times = Gather(me, lambda *where: me.TS.at[where], "zyxc")
    moves = {}
    for layer in range(LAYERS):
        for name, ref in grads.items():
            width = ref.shape[-1] // 2
            for half, order in enumerate(ORDERS):
                moves[name, half, layer] = weight(layer, ref, order, slice(width * half, width * (half + 1)))
    moves[SMALL] = small
    timeline = by_place(moves.values(), GATHER_AT)

    def have(names, layer):
        for name in names:
            for half in range(2):
                moves[name, half, layer].arrive()

    def fire(place):
        for move, stage in timeline.get(place, ()):
            move.start(stage)

    def fires(first, count):
        return [(i, functools.partial(fire, first + i)) for i in range(count) if first + i in timeline]

    token_in = me.remote(me.xin.at[me.other["y"]], me.DO.at[1], "y")
    cot_in = me.remote(me.cot.at[me.other["y"]], me.GB.at[1], "y")
    steps_all.start(0)
    fire(0)
    token_in.start()
    steps_all.start(1)
    fire(1)
    steps_all.arrive()
    t24 = jnp.sum(me.TT[...].reshape(n_dp, 32, 128), axis=0)
    me.t24_o[...] = t24
    hot = (t24[:, 0:1] == lax.broadcasted_iota(jnp.int32, (32, STEPS), 1)).astype(F32).astype(BF)
    picked = jnp.concatenate([nn(hot, me.tab[layer])[:24] for layer in range(LAYERS)], axis=0).astype(BF)
    lane = lax.broadcasted_iota(jnp.int32, (16, 128), 1)
    spread = (lane == 16 * (4 * x + me.seq) + lax.broadcasted_iota(jnp.int32, (16, 128), 0)).astype(F32).astype(BF)
    me.TS[z, x, y, c] = nn(picked, spread).astype(BF)
    times.start(0)
    fire(2)
    times.start(1)
    fire(3)
    times.start(2)
    fire(4)
    times.start(3)
    fire(5)

    small.arrive()
    for gz in range(n_z):
        for gx in range(2):
            block = jnp.sum(me.SM[gz, gx].reshape(4, 16, 128).astype(F32), axis=0)
            dp = 2 * gz + gx
            for layer in range(LAYERS):
                for r in range(5):
                    at = (5 * dp + r) * 128
                    me.BV[layer, :, at : at + 128] = block[6 * layer + r : 6 * layer + r + 1]
                me.GV[layer, :, 128 * dp : 128 * dp + 128] = block[6 * layer + 5 : 6 * layer + 6]
    times.arrive()
    slabs = jnp.concatenate(
        [jnp.sum(me.TS[gz].reshape(8, 48, 128).astype(F32), axis=0) for gz in range(n_z)], axis=1
    ).astype(BF)
    r8 = lax.broadcasted_iota(jnp.int32, (16, 48), 0)
    c48 = lax.broadcasted_iota(jnp.int32, (16, 48), 1)
    for layer in range(LAYERS):
        base = 24 * layer + 3 * me.dp
        pick = ((r8 == 0) & (c48 == base + y)) | ((r8 == 1) & (c48 == base + 2))
        me.TR[layer] = nn(pick.astype(F32).astype(BF), slabs)[:8]

    def time_row(layer, tile):
        return me.TR[layer, 1:2, :] if tile == 2 else me.TR[layer, 0:1, :]

    def bias(layer, at, width=D):
        return me.BV[layer, :, at : at + width]

    for load in own_tokens:
        load.wait()
    token_in.wait_recv()
    for tile in range(3):
        me.X[0, tile] = me.DO[tile].astype(F32) + time_row(0, tile)

    fire(6)
    have("q", 0)

    sends = [token_in, cot_in]

    def send(src, dst, dim):
        copy = me.remote(src, dst, dim)
        sends.append(copy)
        return copy

    def qkv(layer, tile):
        hat, _ = ln_parts(me.X[layer, tile])
        normed = (hat * me.GV[layer, :, :D] + bias(layer, B_S1)).astype(BF)
        slot = 4 if tile == 2 else tile
        lin = [nn(normed, me.Wq[layer, :, :, :, :, :, D * j : D * j + D].reshape(D, D)) for j in range(3)]
        me.Q[layer, tile] = (lin[0] + bias(layer, B_Q)).astype(BF) * jnp.asarray(1.0 / math.sqrt(HEAD_DIM), BF)
        me.KV[layer, 0, slot] = lin[1].astype(BF)
        me.KV[layer, 1, slot] = (lin[2] + bias(layer, B_V)).astype(BF)

    low_lanes = lax.broadcasted_iota(jnp.int32, (TILE, 128), 1) < HEAD_DIM

    def two_heads(pair):
        zero = jnp.zeros_like(pair)
        return jnp.concatenate([jnp.where(low_lanes, pair, zero), jnp.where(low_lanes, zero, pair)], axis=0)

    def place(step, order):
        turn, pair = step // PAIRS, step % PAIRS
        if order == "012":
            tile = turn
        else:
            tile = (turn + 2) % 3
        base = (tile // 2) * 4
        return tile, base, pair, pl.ds(pl.multiple_of(pair * 128, 128), 128)

    def attend_step(layer, step):
        tile, base, pair, cols = place(step, "012")
        queries = two_heads(me.Q[layer, tile, :, cols])
        scores = [nt(me.KV[layer, 0, base + part, :, cols], queries) for part in range(4)]
        tops = [jnp.max(score, axis=0, keepdims=True) for score in scores]
        top = jnp.maximum(jnp.maximum(tops[0], tops[1]), jnp.maximum(tops[2], tops[3])) * LOG2E
        mixed = jnp.zeros((144, 2 * TILE), F32)
        for part, score in enumerate(scores):
            values = jnp.concatenate([me.KV[layer, 1, base + part, :, cols].T, jnp.ones((16, TILE), BF)], axis=0)
            mixed = mixed + nn(values, jnp.exp2(score * LOG2E - top).astype(BF))
        total = mixed[128:129]
        mixed = mixed[:128] * (1.0 / total)
        me.LSE[layer, tile, pair] = top + jnp.log2(total)
        out = jnp.concatenate([mixed[:HEAD_DIM, :TILE], mixed[HEAD_DIM:, TILE:]], axis=0)
        me.AO[layer, tile, :, cols] = out.T.astype(BF)

    def forward(layer):
        kv, base = me.KV, FORWARD_AT[layer]
        to_y = send(kv.at[layer, :, 4], kv.at[layer, :, 5], "y")
        to_c = [send(kv.at[layer, :, a], kv.at[layer, :, b], "c") for a, b in ((4, 6), (0, 2), (1, 3), (5, 7))]
        qkv(layer, 2)
        to_y.start()
        to_c[0].start()
        fire(base)
        qkv(layer, 0)
        to_c[1].start()
        fire(base + 1)
        qkv(layer, 1)
        to_c[2].start()
        fire(base + 2)
        to_c[1].wait_recv()
        to_c[2].wait_recv()

        def pass_on():
            to_y.wait_recv()
            to_c[3].start()

        def have_all():
            to_c[0].wait_recv()
            to_c[3].wait_recv()

        def step(index, carry):
            at_step(index, [(7, pass_on), (8, have_all)] + fires(base + 3, 3 * PAIRS))
            attend_step(layer, index)
            return carry

        lax.fori_loop(0, 3 * PAIRS, step, 0)
        have("o", layer)
        w_out = me.Wo[layer].reshape(D, D)
        for tile in range(3):
            fire(base + 15 + tile)
            after = me.X[layer, tile] + nn(me.AO[layer, tile], w_out) + bias(layer, B_O)
            me.Y[layer, tile] = after
            hat, _ = ln_parts(after)
            me.N[tile] = (hat * me.GV[layer, :, D:] + bias(layer, B_S2)).astype(BF)
            me.GN[tile] = after + bias(layer, B_D)

        have("ud", layer)

        def ffn(slab, carry):
            at_step(slab, fires(base + 18, 4))
            cols = pl.ds(pl.multiple_of(slab * D, D), D)
            w_up = me.Wu[layer, :, :, :, :, :, cols].reshape(D, D)
            w_down = me.Wd[layer, slab].reshape(D, D)
            b_up = me.BV[layer, :, pl.ds(pl.multiple_of(B_U + slab * D, D), D)]
            for tile in range(3):
                up = nn(me.N[tile], w_up) + b_up
                _, tanh = gelu_parts(up)
                me.GN[tile] += nn((0.5 * up * (1.0 + tanh)).astype(BF), w_down)
            return carry

        lax.fori_loop(0, FF // D, ffn, 0)

    forward(0)
    for tile in range(3):
        me.X[1, tile] = me.GN[tile] + time_row(1, tile)
    fire(FORWARD_AT[1] - 1)
    have("q", 1)
    cot_in.start()
    forward(1)
    for tile in range(3):
        me.ACC[0, pl.ds(TILE * tile, TILE)] = me.GN[tile]
    act = [me.ACC.at[0, pl.ds(TILE * tile, TILE)] for tile in range(3)]
    act_out = me.remote(act[1], me.act_o.at[y], "y")
    act_out.start()
    act_own = [me.local(act[0], me.act_o.at[y]), me.local(act[2], me.act_o.at[2])]
    for copy in act_own:
        copy.start()

    cot_in.wait_recv()
    weight_y, weight_2 = me.imp[me.ts[y]], me.imp[me.ts[2]]
    for tile in range(3):
        grad = me.GB[tile].astype(F32) * (weight_2 if tile == 2 else weight_y)
        me.G[tile] = grad
    for part in [steps_all, times, *moves.values()]:
        part.drain()
    for copy in sends:
        copy.wait_send()
    sends.clear()

    outs = {"q": me.gq_o, "o": me.go_o, "u": me.gu_o, "d": me.gd_o}
    recvs = {
        name: [me.R1[i], me.R2[i], me.R3[i], me.R4[i]] for i, name in enumerate("qoud")
    }

    spans = {
        "d": ("d", 0, D), "u": ("u", 0, FF), "o": ("o", 0, D), "p": ("q", 0, D), "q": ("q", D, 3 * D)
    }

    def piece(layer, number, name, half):
        kind, begin, end = spans[name]
        width = (end - begin) // 2
        start = begin + width * half
        return Reduce(
            me, layer, grads[kind], recvs[kind], outs[kind], slice(start, start + width), ORDERS[half][::-1], number
        )

    def add_bias(layer, at, value):
        me.BG[layer, :, at : at + value.shape[-1]] += value

    def ln_back(layer, gain_at, shift_at, source, grad):
        hat, scale = ln_parts(source)
        me.GG[layer, :, gain_at : gain_at + D] += rows_sum(grad * hat)
        add_bias(layer, shift_at, rows_sum(grad))
        inner = grad * me.GV[layer, :, gain_at : gain_at + D]
        return scale * (inner - jnp.mean(inner, axis=-1, keepdims=True) - hat * jnp.mean(inner * hat, axis=-1, keepdims=True))

    def normed_t(layer, source, gain_at, shift_at):
        for tile in range(3):
            hat, _ = ln_parts(source[layer, tile])
            normed = (hat * me.GV[layer, :, gain_at : gain_at + D] + bias(layer, shift_at)).astype(BF)
            me.N[tile] = normed
            me.NT[:, TILE * tile : TILE * tile + TILE] = normed.T

    head_of = lax.broadcasted_iota(jnp.int32, (HEADS, D), 1) // HEAD_DIM
    selector = (head_of == lax.broadcasted_iota(jnp.int32, (HEADS, D), 0)).astype(F32)

    def backward(layer, before_attn, tail):
        base = BACKWARD_AT[layer]
        normed_t(layer, me.Y, D, B_S2)
        for tile in range(3):
            me.GB[tile] = me.G[tile].astype(BF)
            add_bias(layer, B_D, rows_sum(me.G[tile]))
            me.GN[tile] = jnp.zeros((TILE, D), F32)

        def ffn(chunk, carry):
            at_step(chunk, fires(base, 8))
            cols = pl.ds(pl.multiple_of(chunk * TILE, TILE), TILE)
            b_cols = pl.ds(pl.multiple_of(B_U + chunk * TILE, TILE), TILE)
            w_up = me.Wu[layer, :, :, :, :, :, cols].reshape(D, TILE)
            w_down = me.Wd[layer, chunk // 2, chunk % 2].reshape(TILE, D)
            total = jnp.zeros((1, TILE), F32)
            for tile in range(3):
                up = nn(me.N[tile], w_up) + me.BV[layer, :, b_cols]
                square, tanh = gelu_parts(up)
                me.A1[pl.ds(TILE * tile, TILE)] = (0.5 * up * (1.0 + tanh)).astype(BF)
                slope = 0.5 * (1.0 + tanh) + (0.5 * GELU_A) * up * (1.0 - tanh * tanh) * (1.0 + 3.0 * GELU_B * square)
                grad_up = nt(me.GB[tile], w_down) * slope
                total = total + rows_sum(grad_up)
                grad_up = grad_up.astype(BF)
                me.A2[pl.ds(TILE * tile, TILE)] = grad_up
                me.GN[tile] += nt(grad_up, w_up)
            me.BG[layer, :, b_cols] += total
            d_down = tn(me.A1[...], me.GB[...].reshape(3 * TILE, D))
            me.Wd[layer, chunk // 2, chunk % 2] = d_down.astype(BF).reshape(2, 2, 64, D)
            d_up = nn(me.NT[...], me.A2[...])
            me.Wu[layer, :, :, :, :, :, cols] = d_up.astype(BF).reshape(n_z, 2, 2, 2, 16, TILE)
            return carry

        lax.fori_loop(0, FF // TILE, ffn, 0)
        fire(base + 8)
        for tile in range(3):
            mid = me.G[tile] + ln_back(layer, D, B_S2, me.Y[layer, tile], me.GN[tile])
            me.G[tile] = mid
            add_bias(layer, B_O, rows_sum(mid))
            me.GB[tile] = mid.astype(BF)
        fire(base + 9)
        w_out = me.Wo[layer].reshape(D, D)
        for tile in range(3):
            grad_attn = nt(me.GB[tile], w_out).astype(BF)
            me.DO[tile] = grad_attn
            delta = nt(selector, grad_attn.astype(F32) * me.AO[layer, tile].astype(F32), lax.Precision.HIGHEST)
            for pair in range(PAIRS):
                both = jnp.concatenate([delta[2 * pair : 2 * pair + 1], delta[2 * pair + 1 : 2 * pair + 2]], axis=1)
                me.DL[tile, pair] = both
        d_out = tn(me.AO[layer].reshape(3 * TILE, D), me.GB[...].reshape(3 * TILE, D))
        me.Wo[layer] = d_out.astype(BF).reshape(n_z, 2, 2, 2, 16, D)
        fire(base + 10)

        before_attn()
        me.ACC[...] = jnp.zeros_like(me.ACC)
        third_c = send(me.PB.at[:, 1:3], me.RB1, "c")
        third_y = send(me.PB.at[:, 0], me.RB2, "y")
        from_c = send(me.PC, me.RB3, "c")

        def third_done():
            me.OWN[...] = me.ACC[:, 0:TILE]
            me.PB[...] = me.ACC[:, TILE : 4 * TILE].reshape(2, 3, TILE, D).astype(BF)
            me.ACC[...] = jnp.zeros_like(me.ACC)
            third_c.start()

        def third_on():
            third_c.wait_recv()
            me.OWN[...] += me.RB1[:, 0].astype(F32)
            me.PB[:, 0] = me.PB[:, 0] + me.RB1[:, 1]
            third_y.start()

        def attend_back(step, carry):
            at_step(step, [(PAIRS, third_done), (PAIRS + 2, third_on)] + fires(base + 12, 3 * PAIRS))
            tile, slot, pair, cols = place(step, "201")
            queries, grads_o = two_heads(me.Q[layer, tile, :, cols]), two_heads(me.DO[tile, :, cols])
            log_sum, delta = me.LSE[layer, tile, pair], me.DL[tile, pair]
            d_query = jnp.zeros((128, 2 * TILE), F32)
            for part in range(4):
                keys, values = me.KV[layer, 0, slot + part, :, cols], me.KV[layer, 1, slot + part, :, cols]
                rows = slice(TILE * part, TILE * part + TILE)
                prob = jnp.exp2(nt(keys, queries) * LOG2E - log_sum)
                grad_s = (prob * (nt(values, grads_o) - delta)).astype(BF)
                me.ACC[1, rows, cols] += nn(prob.astype(BF), grads_o)
                me.ACC[0, rows, cols] += nn(grad_s, queries)
                d_query = d_query + nn(keys.T, grad_s)
            d_query = jnp.concatenate([d_query[:HEAD_DIM, :TILE], d_query[HEAD_DIM:, TILE:]], axis=0).T
            d_query = d_query * (1.0 / math.sqrt(HEAD_DIM))
            me.BG[layer, :, cols] += rows_sum(d_query)
            me.GL[tile, :, cols] = d_query.astype(BF)
            return carry

        fire(base + 11)
        lax.fori_loop(0, 3 * PAIRS, attend_back, 0)
        me.PC[...] = me.ACC[:, 2 * TILE :].astype(BF)
        from_c.start()
        normed_t(layer, me.X, 0, B_S1)
        fire(base + 24)

        def qkv_back(first, last):
            w_qkv = me.Wq[layer, :, :, :, :, :, first:last].reshape(D, last - first)
            for tile in range(3):
                part = nt(me.GL[tile, :, first:last], w_qkv)
                me.GN[tile] = part if first == 0 else me.GN[tile] + part
            for j in range(first, last, D):
                d_qkv = nn(me.NT[...], me.GL[:, :, j : j + D].reshape(3 * TILE, D))
                me.Wq[layer, :, :, :, :, :, j : j + D] = d_qkv.astype(BF).reshape(n_z, 2, 2, 2, 16, D)

        qkv_back(0, D)
        fire(base + 25)
        from_c.wait_recv()
        for tile in range(2):
            rows = slice(TILE * tile, TILE * tile + TILE)
            key = me.ACC[0, rows] + me.RB3[0, rows].astype(F32)
            value = me.ACC[1, rows] + me.RB3[1, rows].astype(F32)
            add_bias(layer, B_V, rows_sum(value))
            me.GL[tile, :, D : 2 * D] = key.astype(BF)
            me.GL[tile, :, 2 * D :] = value.astype(BF)
        third_y.wait_recv()
        third = me.OWN[...] + me.RB2[...].astype(F32)
        me.GL[2, :, D : 2 * D] = third[0].astype(BF)
        me.GL[2, :, 2 * D :] = third[1].astype(BF)
        add_bias(layer, B_V, rows_sum(third[1]))
        fire(base + 26)
        qkv_back(D, 3 * D)
        fire(base + 27)
        totals = []
        for tile in (1, 0, 2):
            grad = me.G[tile] + ln_back(layer, 0, B_S1, me.X[layer, tile], me.GN[tile])
            me.G[tile] = grad
            totals.append(rows_sum(grad))
            tail(tile, grad)
            fire(base + 27 + len(totals))
        me.TG[layer, 0:1] = totals[0] + totals[1]
        me.TG[layer, 1:2] = totals[2]
        for copy in sends:
            copy.wait_send()
        sends.clear()

    sums = [
        piece(layer, number, name, half)
        for layer in reversed(range(LAYERS))
        for number, (name, half) in enumerate((name, half) for name in spans for half in range(2))
    ]
    timeline.clear()
    timeline.update(by_place(sums, REDUCE_AT))

    def act_done():
        for copy in act_own + [act_out]:
            copy.wait()

    backward(1, act_done, lambda tile, grad: None)
    finals = []

    def out_tile(tile, grad):
        if tile == 1:
            me.GB[1] = grad.astype(BF)
            finals.append(me.remote(me.GB.at[1], me.RB1.at[0, 0], "y"))
        else:
            finals.append(me.local(me.G.at[tile], me.gin_o.at[y if tile == 0 else 2]))
        finals[-1].start()

    backward(0, lambda: None, out_tile)

    seq_row = lax.broadcasted_iota(jnp.int32, (24, 128), 0)
    for gz in range(n_z):
        tables = []
        for layer in range(LAYERS):
            lanes = slice(128 * gz, 128 * gz + 128)
            first_seq = jnp.where(seq_row == 3 * me.dp + y, me.TG[layer, 0:1, lanes], 0.0)
            tables.append(jnp.where(seq_row == 3 * me.dp + 2, me.TG[layer, 1:2, lanes], first_seq))
        for gx in range(2):
            dp = 2 * gz + gx
            for layer in range(LAYERS):
                for r in range(5):
                    at_lane = (5 * dp + r) * 128
                    me.SR[gz, gx, 6 * layer + r : 6 * layer + r + 1] = me.BG[layer, :, at_lane : at_lane + 128]
                me.SR[gz, gx, 6 * layer + 5 : 6 * layer + 6] = me.GG[layer, :, 128 * dp : 128 * dp + 128]
                me.SR[gz, gx, 16 + 24 * layer : 40 + 24 * layer] = tables[layer]
            me.SR[gz, gx, 12:16] = jnp.zeros((4, 128), F32)
    small_x = me.remote(me.SR.at[:, me.other["x"]], me.SX, "x")
    small_x.start()
    fire(END_AT)
    small_x.wait_recv()
    for gz in range(n_z):
        me.SR[gz, x] = me.SR[gz, x] + me.SX[gz]
    small_z = [me.remote(me.SR.at[me.around[hop], x], me.SZ.at[hop - 1], "z", hop) for hop in me.hops("z")]
    for copy in small_z:
        copy.start()
    fire(END_AT + 1)
    finals[0].wait()
    me.GN[0] = me.RB1[0, 0].astype(F32)
    last = me.local(me.GN.at[0], me.gin_o.at[me.other["y"]])
    last.start()
    for copy in small_z:
        copy.wait_recv()
    total = me.SR[z, x]
    for hop in me.hops("z"):
        total = total + me.SZ[hop - 1]
    me.SY[0] = total
    small_y = me.remote(me.SY.at[0], me.SY.at[1], "y")
    small_y.start()
    fire(END_AT + 2)
    small_y.wait_recv()
    me.SY[2] = me.SY[0] + me.SY[1]
    small_c = me.remote(me.SY.at[2], me.SY.at[3], "c")
    small_c.start()
    fire(END_AT + 3)
    small_c.wait_recv()
    me.small_o[...] = me.SY[2] + me.SY[3]
    fire(END_AT + 4)

    for copy in [small_x, small_y, small_c] + small_z:
        copy.wait_send()
    for copy in finals[1:]:
        copy.wait()
    last.wait()
    for part in sums:
        part.drain()


def fused_call(n_z, *operands):
    any_space, vmem, smem = (pl.BlockSpec(memory_space=space) for space in (pl.ANY, pltpu.VMEM, pltpu.SMEM))
    cube = (n_z, 2, 2, 2)
    tokens = (3, TILE, D)
    sizes = ((16, 3 * D), (16, D), (16, FF), (64, D))

    def many(lead):
        return [tuple(pltpu.VMEM((*lead, *size), BF) for size in sizes)]

    flat, tree = jax.tree.flatten(
        [pltpu.VMEM((LAYERS, *cube, *size), BF) for size in sizes]
        + [
            pltpu.VMEM((*cube, 16, 128), BF),
            pltpu.VMEM((*cube, 48, 128), BF),
            pltpu.VMEM((n_z, 2, 32, 128), jnp.int32),
            pltpu.VMEM((LAYERS, 8, D), F32),
            pltpu.VMEM((LAYERS, 1, 6 * D + FF), F32),
            pltpu.VMEM((LAYERS, 1, 2 * D), F32),
            pltpu.VMEM((LAYERS, 1, 6 * D + FF), F32),
            pltpu.VMEM((LAYERS, 1, 2 * D), F32),
            pltpu.VMEM((LAYERS, 8, D), F32),
            pltpu.VMEM((LAYERS, *tokens), F32),
            pltpu.VMEM(tokens, BF),
            pltpu.VMEM((D, 3 * TILE), BF),
            pltpu.VMEM((LAYERS, *tokens), BF),
            pltpu.VMEM((LAYERS, 2, 8, TILE, D), BF),
            pltpu.VMEM((LAYERS, *tokens), BF),
            pltpu.VMEM((LAYERS, 3, PAIRS, 1, 2 * TILE), F32),
            pltpu.VMEM((3, PAIRS, 1, 2 * TILE), F32),
            pltpu.VMEM((LAYERS, *tokens), F32),
            pltpu.VMEM(tokens, BF),
            pltpu.VMEM(tokens, BF),
            pltpu.VMEM(tokens, F32),
            pltpu.VMEM(tokens, F32),
            pltpu.VMEM((3, TILE, 3 * D), BF),
            pltpu.VMEM((2, 4 * TILE, D), F32),
            pltpu.VMEM((2, TILE, D), F32),
            pltpu.VMEM((2, 3, TILE, D), BF),
            pltpu.VMEM((2, 2 * TILE, D), BF),
            pltpu.VMEM((2, 2, TILE, D), BF),
            pltpu.VMEM((2, TILE, D), BF),
            pltpu.VMEM((2, 2 * TILE, D), BF),
            pltpu.VMEM((3 * TILE, TILE), BF),
            pltpu.VMEM((3 * TILE, TILE), BF),
        ]
        + many((n_z, 2, 2))
        + many((n_z, 2))
        + many((2 * n_z - 2,))
        + many((n_z - 1,))
        + [
            pltpu.VMEM((n_z, 2, 64, 128), F32),
            pltpu.VMEM((n_z, 64, 128), F32),
            pltpu.VMEM((n_z - 1, 64, 128), F32),
            pltpu.VMEM((4, 64, 128), F32),
            pltpu.SemaphoreType.DMA((N_SEMS,)),
            pltpu.SemaphoreType.DMA((N_SEMS,)),
            pltpu.SemaphoreType.DMA((32,)),
            pltpu.SemaphoreType.REGULAR((10, 4)),
        ]
    )
    outs = [
        jax.ShapeDtypeStruct(tokens, F32),
        jax.ShapeDtypeStruct(tokens, F32),
        *[jax.ShapeDtypeStruct((LAYERS, *size), F32) for size in sizes],
        jax.ShapeDtypeStruct((64, 128), F32),
        jax.ShapeDtypeStruct((32, 128), jnp.int32),
    ]

    def run(*refs):
        head = len(operands) + len(outs)
        fused_kernel(n_z, *refs[:head], *jax.tree.unflatten(tree, refs[head:]))

    return pl.pallas_call(
        run,
        out_shape=outs,
        in_specs=[smem, smem] + [any_space] * 6 + [vmem] * 2,
        out_specs=[any_space] * 2 + [vmem] * 6,
        scratch_shapes=flat,
        compiler_params=pltpu.CompilerParams(collective_id=0, has_side_effects=True, vmem_limit_bytes=VMEM_BYTES),
    )(*operands)


VMEM_BYTES = 63 * 1024 * 1024


def fused_body(
    inputs, cotangent, w_qkv, w_out, w_up, w_down, norm_gains, biases, time_table, timesteps, importance
):
    n_z = lax.axis_size("dp") // 2
    seq = lax.axis_index("seq")
    mine = (jnp.arange(4) == seq)[None, :, None]
    bias_rows = jnp.where(mine, biases[:, None, :], 0).reshape(LAYERS, 5, 128)
    gain_rows = jnp.where(mine, norm_gains[:, None, :], 0).reshape(LAYERS, 1, 128)
    small = jnp.concatenate([bias_rows, gain_rows], axis=1).reshape(6 * LAYERS, 128)
    small = jnp.pad(small, ((0, 16 - 6 * LAYERS), (0, 0))).astype(BF)
    act, grad_in, g_qkv, g_out, g_up, g_down, sums, steps = fused_call(
        n_z, timesteps, importance, jnp.swapaxes(inputs, 0, 1), jnp.swapaxes(cotangent, 0, 1),
        w_qkv, w_out, w_up, w_down, small, time_table,
    )
    rows = sums[: 6 * LAYERS].reshape(LAYERS, 6, 128)
    grad_biases = lax.dynamic_slice_in_dim(rows[:, :5].reshape(LAYERS, 640), 160 * seq, 160, 1)
    grad_gains = lax.dynamic_slice_in_dim(rows[:, 5], 32 * seq, 32, 1)
    place = (lax.axis_index("dp") % 2) * 4 + seq
    table_rows = lax.dynamic_slice_in_dim(sums[16:].reshape(LAYERS, 24, 128), 16 * place, 16, 2)
    onehot = (jnp.arange(STEPS, dtype=jnp.int32)[:, None] == steps[:24, 0][None, :]).astype(F32)
    grad_table = jnp.einsum("tj,ljf->ltf", onehot, table_rows, precision=HIGH)
    return (
        jnp.swapaxes(act, 0, 1), jnp.swapaxes(grad_in, 0, 1), g_qkv, g_out, g_up, g_down, grad_gains, grad_biases, grad_table,
    )


def solution(mesh):
    devices = mesh.shape["dp"] * mesh.shape["seq"]
    whole_tiles = mesh.shape["seq"] == 4 and mesh.shape["dp"] % 2 == 0 and D // devices == 16
    in_specs = (
        P("seq", "dp", None),
        P("seq", "dp", None),
        P(None, ("dp", "seq"), None),
        P(None, ("dp", "seq"), None),
        P(None, ("dp", "seq"), None),
        P(None, ("dp", "seq"), None),
        P(None, ("dp", "seq")),
        P(None, ("dp", "seq")),
        P(None, None, ("dp", "seq")),
        P("dp"),
        P(),
    )
    out_specs = (
        P("seq", "dp", None),
        P("seq", "dp", None),
        P(None, ("dp", "seq"), None),
        P(None, ("dp", "seq"), None),
        P(None, ("dp", "seq"), None),
        P(None, ("dp", "seq"), None),
        P(None, ("dp", "seq")),
        P(None, ("dp", "seq")),
        P(None, None, ("dp", "seq")),
    )
    return jax.shard_map(
        fused_body if whole_tiles else body, mesh=mesh, in_specs=in_specs, out_specs=out_specs, check_vma=False)
```

```python
import functools
import math

import jax
import jax.numpy as jnp
from jax import lax
from jax.experimental import pallas as pl
from jax.experimental.pallas import tpu as pltpu
from jax.sharding import PartitionSpec as P

D = 512
HEADS = 8
HEAD_DIM = 64
FF = 2048
STEPS = 1000
LAYERS = 2


EPS = 1e-05
HIGH = lax.Precision.HIGHEST


def layer_norm(values, gain_vec, bias_vec):
    centered = values - jnp.mean(values, axis=-1, keepdims=True)
    spread = jnp.mean(centered * centered, axis=-1, keepdims=True)
    return centered * lax.rsqrt(spread + EPS) * gain_vec + bias_vec


def attend(queries, keys_all, values_all):
    row_count, seq_count, model_width = queries.shape
    score_scale = 1.0 / math.sqrt(HEAD_DIM)

    def per_seq(seq_index, loop_state):
        outputs, log_tot = loop_state
        query_per_head = lax.dynamic_index_in_dim(queries, seq_index, 1, keepdims=False).reshape(
            row_count, HEADS, HEAD_DIM
        )
        key_per_head = lax.dynamic_index_in_dim(keys_all, seq_index, 1, keepdims=False).reshape(
            -1, HEADS, HEAD_DIM
        )
        value_per_head = lax.dynamic_index_in_dim(values_all, seq_index, 1, keepdims=False).reshape(
            -1, HEADS, HEAD_DIM
        )
        scores = (
            jnp.einsum(
                "xsv,usv->sxu", query_per_head, key_per_head, preferred_element_type=jnp.float32
            )
            * score_scale
        )
        row_max = jnp.max(scores, axis=-1, keepdims=True)
        expon = jnp.exp(scores - row_max)
        summed = jnp.sum(expon, axis=-1, keepdims=True)
        attention_probability = (expon / summed).astype(jnp.bfloat16)
        attn_out = jnp.einsum(
            "gir,rgo->igo",
            attention_probability,
            value_per_head,
            preferred_element_type=jnp.float32,
        )
        attn_out = attn_out.astype(jnp.bfloat16).reshape(row_count, 1, model_width)
        outputs = lax.dynamic_update_slice_in_dim(outputs, attn_out, seq_index, 1)
        log_tot = lax.dynamic_update_slice_in_dim(
            log_tot, (row_max + jnp.log(summed))[None, :, :, 0], seq_index, 0
        )
        return (outputs, log_tot)

    start_state = (
        jnp.zeros(queries.shape, jnp.bfloat16),
        jnp.zeros((seq_count, HEADS, row_count), jnp.float32),
    )
    return lax.fori_loop(0, seq_count, per_seq, start_state)


def attend_back(queries, keys_all, values_all, log_tot, grad_attn):
    row_count, seq_count, model_width = queries.shape
    key_count = keys_all.shape[0]
    score_scale = 1.0 / math.sqrt(HEAD_DIM)

    def per_seq(seq_index, loop_state):
        grad_query, part_key, part_value = loop_state
        query_per_head = lax.dynamic_index_in_dim(queries, seq_index, 1, keepdims=False).reshape(
            row_count, HEADS, HEAD_DIM
        )
        key_per_head = lax.dynamic_index_in_dim(keys_all, seq_index, 1, keepdims=False).reshape(
            key_count, HEADS, HEAD_DIM
        )
        value_per_head = lax.dynamic_index_in_dim(values_all, seq_index, 1, keepdims=False).reshape(
            key_count, HEADS, HEAD_DIM
        )
        hidden_state_gradient = lax.dynamic_index_in_dim(
            grad_attn, seq_index, 1, keepdims=False
        ).reshape(row_count, HEADS, HEAD_DIM)
        log_seq = lax.dynamic_index_in_dim(log_tot, seq_index, 0, keepdims=False)
        scores = (
            jnp.einsum(
                "xsv,usv->sxu", query_per_head, key_per_head, preferred_element_type=jnp.float32
            )
            * score_scale
        )
        attn_f = jnp.exp(scores - log_seq[:, :, None])
        attention_probability = attn_f.astype(jnp.bfloat16)
        value_part = jnp.einsum(
            "uxo,xuc->ouc",
            attention_probability,
            hidden_state_gradient,
            preferred_element_type=jnp.float32,
        )
        probability_gradient = jnp.einsum(
            "xsv,usv->sxu",
            hidden_state_gradient,
            value_per_head,
            preferred_element_type=jnp.float32,
        )
        row_delta = jnp.sum(probability_gradient * attn_f, axis=-1, keepdims=True)
        score_gradient = (attn_f * (probability_gradient - row_delta)).astype(jnp.bfloat16)
        query_part = (
            jnp.einsum(
                "gir,rgo->igo", score_gradient, key_per_head, preferred_element_type=jnp.float32
            )
            * score_scale
        )
        key_part = (
            jnp.einsum(
                "uxo,xuc->ouc", score_gradient, query_per_head, preferred_element_type=jnp.float32
            )
            * score_scale
        )
        grad_query = lax.dynamic_update_slice_in_dim(
            grad_query, query_part.reshape(row_count, 1, model_width), seq_index, 1
        )
        part_key = lax.dynamic_update_slice_in_dim(
            part_key, key_part.reshape(key_count, 1, model_width), seq_index, 1
        )
        part_value = lax.dynamic_update_slice_in_dim(
            part_value, value_part.reshape(key_count, 1, model_width), seq_index, 1
        )
        return (grad_query, part_key, part_value)

    start_state = (
        jnp.zeros(queries.shape, jnp.float32),
        jnp.zeros(keys_all.shape, jnp.float32),
        jnp.zeros(keys_all.shape, jnp.float32),
    )
    return lax.fori_loop(0, seq_count, per_seq, start_state)


def forward_layer(hidden, fetched, onehot):
    mat_qkv, mat_out, up_matrix, down_matrix, gain_row, bias_row, time_rows = fetched
    gain_f = gain_row.astype(jnp.float32)
    bias_f = bias_row.astype(jnp.float32)
    seq_embed = jnp.dot(onehot.astype(jnp.bfloat16), time_rows, preferred_element_type=jnp.float32)
    summed_in = hidden + seq_embed[None]
    normed_one = layer_norm(summed_in, gain_f[:D], bias_f[4 * D + FF : 5 * D + FF]).astype(
        jnp.bfloat16
    )
    linear = jnp.dot(normed_one, mat_qkv, preferred_element_type=jnp.float32)
    queries = (linear[..., :D] + bias_f[:D]).astype(jnp.bfloat16)
    keys_loc = linear[..., D : 2 * D].astype(jnp.bfloat16)
    values_loc = (linear[..., 2 * D :] + bias_f[D : 2 * D]).astype(jnp.bfloat16)
    keys_all, values_all = (
        lax.all_gather(keys_loc, "seq", axis=0, tiled=True),
        lax.all_gather(values_loc, "seq", axis=0, tiled=True),
    )
    attn_out, log_tot = attend(queries, keys_all, values_all)
    after_attn = (
        summed_in
        + jnp.dot(attn_out, mat_out, preferred_element_type=jnp.float32)
        + bias_f[2 * D : 3 * D]
    )
    second_normalized = layer_norm(after_attn, gain_f[D:], bias_f[5 * D + FF :]).astype(
        jnp.bfloat16
    )
    upward = (
        jnp.dot(second_normalized, up_matrix, preferred_element_type=jnp.float32)
        + bias_f[3 * D : 3 * D + FF]
    )
    gelu_output = jax.nn.gelu(upward).astype(jnp.bfloat16)
    result = (
        after_attn
        + jnp.dot(gelu_output, down_matrix, preferred_element_type=jnp.float32)
        + bias_f[3 * D + FF : 4 * D + FF]
    )
    record = (
        summed_in,
        normed_one,
        queries,
        keys_loc,
        values_loc,
        attn_out,
        log_tot,
        after_attn,
        second_normalized,
        upward,
        gelu_output,
        keys_all,
        values_all,
    )
    return (result, record)


def backward_layer(hidden_state_gradient, fetched, record, onehot, kv_pair):
    mat_qkv = fetched[0]
    mat_out = fetched[1]
    up_matrix = fetched[2]
    down_matrix = fetched[3]
    gain_f = fetched[4].astype(jnp.float32)
    bias_f = fetched[5].astype(jnp.float32)
    summed_in, normed_one, queries = (record[0], record[1], record[2])
    attn_out, log_tot, after_attn = (record[5], record[6], record[7])
    second_normalized, upward, gelu_output = (record[8], record[9], record[10])
    keys_all, values_all = kv_pair
    gradient_bfloat = hidden_state_gradient.astype(jnp.bfloat16)
    down_weight_gradient = jnp.einsum(
        "awt,awg->tg", gelu_output, gradient_bfloat, preferred_element_type=jnp.float32
    )
    bias_down = jnp.sum(hidden_state_gradient, axis=(0, 1))
    activation_gradient = jnp.einsum(
        "ngb,rb->ngr", gradient_bfloat, down_matrix, preferred_element_type=jnp.float32
    )
    _, gelu_back = jax.vjp(jax.nn.gelu, upward)
    grad_upward = gelu_back(activation_gradient)[0]
    bias_up = jnp.sum(grad_upward, axis=(0, 1))
    upward_bfloat = grad_upward.astype(jnp.bfloat16)
    up_weight_gradient = jnp.einsum(
        "xew,xem->wm", second_normalized, upward_bfloat, preferred_element_type=jnp.float32
    )
    second_norm_gradient = jnp.einsum(
        "iyv,tv->iyt", upward_bfloat, up_matrix, preferred_element_type=jnp.float32
    )
    _, second_back = jax.vjp(layer_norm, after_attn, gain_f[D:], bias_f[5 * D + FF :])
    from_second, gain_two, shift_two = second_back(second_norm_gradient)
    grad_mid = hidden_state_gradient + from_second
    mid_bf = grad_mid.astype(jnp.bfloat16)
    grad_out = jnp.einsum("lsc,lsd->cd", attn_out, mid_bf, preferred_element_type=jnp.float32)
    bias_out = jnp.sum(grad_mid, axis=(0, 1))
    grad_attn = jnp.einsum(
        "lsd,cd->lsc", mid_bf, mat_out, preferred_element_type=jnp.float32
    ).astype(jnp.bfloat16)
    grad_query, part_key, part_value = attend_back(
        queries, keys_all, values_all, log_tot, grad_attn
    )
    grad_key, grad_value = (
        lax.psum_scatter(
            part_key.astype(jnp.bfloat16), "seq", scatter_dimension=0, tiled=True
        ).astype(jnp.float32),
        lax.psum_scatter(
            part_value.astype(jnp.bfloat16), "seq", scatter_dimension=0, tiled=True
        ).astype(jnp.float32),
    )
    bias_query = jnp.sum(grad_query, axis=(0, 1))
    bias_value = jnp.sum(grad_value, axis=(0, 1))
    grad_linear = jnp.concatenate([grad_query, grad_key, grad_value], axis=-1).astype(jnp.bfloat16)
    grad_qkv = jnp.einsum(
        "lsc,lse->ce", normed_one, grad_linear, preferred_element_type=jnp.float32
    )
    grad_norm_one = jnp.einsum(
        "lse,ce->lsc", grad_linear, mat_qkv, preferred_element_type=jnp.float32
    )
    _, first_back = jax.vjp(layer_norm, summed_in, gain_f[:D], bias_f[4 * D + FF : 5 * D + FF])
    from_first, gain_one, shift_one = first_back(grad_norm_one)
    grad_in = grad_mid + from_first
    grad_table = jnp.dot(onehot.T, jnp.sum(grad_in, axis=0), precision=HIGH)
    grad_gain = jnp.concatenate([gain_one, gain_two])
    grad_bias = jnp.concatenate(
        [bias_query, bias_value, bias_out, bias_up, bias_down, shift_one, shift_two]
    )
    return (
        grad_in,
        (
            grad_qkv,
            grad_out,
            up_weight_gradient,
            down_weight_gradient,
            grad_gain,
            grad_bias,
            grad_table,
        ),
    )


def body(
    inputs,
    cotangent,
    w_qkv,
    w_out,
    w_up,
    w_down,
    norm_gains,
    biases,
    time_table,
    timesteps,
    importance,
):
    onehot = (timesteps[:, None] == jnp.arange(STEPS, dtype=jnp.int32)[None, :]).astype(jnp.float32)
    seq_weight = jnp.dot(onehot, importance, precision=HIGH)
    hidden = inputs.astype(jnp.float32)
    records = []
    fetched_all = []
    for layer_id in range(LAYERS):
        fetched = (
            lax.all_gather(w_qkv[layer_id], ("dp", "seq"), axis=0, tiled=True),
            lax.all_gather(w_out[layer_id], ("dp", "seq"), axis=0, tiled=True),
            lax.all_gather(w_up[layer_id], ("dp", "seq"), axis=0, tiled=True),
            lax.all_gather(w_down[layer_id], ("dp", "seq"), axis=0, tiled=True),
            lax.all_gather(norm_gains[layer_id], ("dp", "seq"), axis=0, tiled=True),
            lax.all_gather(biases[layer_id], ("dp", "seq"), axis=0, tiled=True),
            lax.all_gather(time_table[layer_id], ("dp", "seq"), axis=1, tiled=True),
        )
        hidden, record = forward_layer(hidden, fetched, onehot)
        records.append(record)
        fetched_all.append(fetched)
    hidden_state_gradient = cotangent.astype(jnp.float32) * seq_weight[None, :, None]
    shards = [None] * LAYERS
    for layer_id in reversed(range(LAYERS)):
        record = records[layer_id]
        fetched = (
            lax.all_gather(w_qkv[layer_id], ("dp", "seq"), axis=0, tiled=True),
            lax.all_gather(w_out[layer_id], ("dp", "seq"), axis=0, tiled=True),
            lax.all_gather(w_up[layer_id], ("dp", "seq"), axis=0, tiled=True),
            lax.all_gather(w_down[layer_id], ("dp", "seq"), axis=0, tiled=True),
            lax.all_gather(norm_gains[layer_id], ("dp", "seq"), axis=0, tiled=True),
            lax.all_gather(biases[layer_id], ("dp", "seq"), axis=0, tiled=True),
            lax.all_gather(time_table[layer_id], ("dp", "seq"), axis=1, tiled=True),
        )
        kv_pair = (
            lax.all_gather(record[3], "seq", axis=0, tiled=True),
            lax.all_gather(record[4], "seq", axis=0, tiled=True),
        )
        hidden_state_gradient, grads = backward_layer(
            hidden_state_gradient, fetched, record, onehot, kv_pair
        )
        shards[layer_id] = (
            lax.psum_scatter(grads[0], ("dp", "seq"), scatter_dimension=0, tiled=True),
            lax.psum_scatter(grads[1], ("dp", "seq"), scatter_dimension=0, tiled=True),
            lax.psum_scatter(grads[2], ("dp", "seq"), scatter_dimension=0, tiled=True),
            lax.psum_scatter(grads[3], ("dp", "seq"), scatter_dimension=0, tiled=True),
            lax.psum_scatter(grads[4], ("dp", "seq"), scatter_dimension=0, tiled=True),
            lax.psum_scatter(grads[5], ("dp", "seq"), scatter_dimension=0, tiled=True),
            lax.psum_scatter(grads[6], ("dp", "seq"), scatter_dimension=1, tiled=True),
        )
    stacked = [
        jnp.stack([shards[layer_id][member] for layer_id in range(LAYERS)]) for member in range(7)
    ]
    return (
        hidden,
        hidden_state_gradient,
        stacked[0],
        stacked[1],
        stacked[2],
        stacked[3],
        stacked[4],
        stacked[5],
        stacked[6],
    )


MESH_ID = pl.DeviceIdType.MESH
LOG2E = 1.4426950408889634
F32 = jnp.float32
BF = jnp.bfloat16
TILE = 256
PAIRS = HEADS // 2
N_SEMS = 256
GELU_A = math.sqrt(2.0 / math.pi)
GELU_B = 0.044715

B_Q, B_V, B_O, B_U, B_D, B_S1, B_S2 = 0, D, 2 * D, 3 * D, 3 * D + FF, 4 * D + FF, 5 * D + FF


def nn(left, right):
    return jnp.dot(left, right, preferred_element_type=F32)


def nt(left, right, precision=None):
    return lax.dot_general(left, right, (((1,), (1,)), ((), ())), preferred_element_type=F32, precision=precision)


def tn(left, right):
    return lax.dot_general(left, right, (((0,), (0,)), ((), ())), preferred_element_type=F32)


def rows_sum(value):
    return jnp.sum(value, axis=0, keepdims=True)


def ln_parts(value):
    centered = value - jnp.mean(value, axis=-1, keepdims=True)
    scale = lax.rsqrt(jnp.mean(centered * centered, axis=-1, keepdims=True) + EPS)
    return centered * scale, scale


def gelu_parts(up):
    square = up * up
    tanh = jnp.tanh(GELU_A * up * (1.0 + GELU_B * square))
    return square, tanh


class Fused:
    def __init__(self, n_z, refs):
        (self.ts, self.imp, self.xin, self.cot, self.wq_i, self.wo_i, self.wu_i, self.wd_i, self.gains_i, self.biases_i, self.tab,
         self.act_o, self.gin_o, self.gq_o, self.go_o, self.gu_o, self.gd_o, self.gg_o, self.gb_o, self.gt_o,
         self.Wq, self.Wo, self.Wu, self.Wd, self.SM, self.TS, self.TT, self.T24, self.TR, self.BV, self.GV, self.BG, self.GG,
         self.TG, self.X, self.N, self.NT, self.Q, self.KV, self.AO, self.LSE, self.DL, self.Y, self.GB, self.DO, self.G,
         self.GN, self.GL, self.ACC, self.OWN, self.PB, self.RB1, self.RB2, self.RB3,
         self.R1, self.R2, self.R3, self.R4, self.SR, self.SX, self.SY,
         self.ssem, self.rsem, self.lsem, self.credit) = refs
        dp, seq = lax.axis_index("dp"), lax.axis_index("seq")
        self.n_z = n_z
        self.dp, self.seq = dp, seq
        self.z, self.x, self.y, self.c = dp // 2, dp % 2, seq // 2, seq % 2
        self.next_sem = 0
        self.next_local = 0
        self.mine = {"z": self.z, "x": self.x, "y": self.y, "c": self.c}
        self.other = {"x": 1 - self.x, "y": 1 - self.y, "c": 1 - self.c}
        self.around = [(self.z + hop) % n_z for hop in range(n_z)]
        n_dp = 2 * n_z
        self.far_z = {hop: (dp + hop) % n_dp // 2 for hop in range(1, n_dp)}
        self.far_x = {hop: (dp + hop) % n_dp % 2 for hop in range(1, n_dp)}
        other_x, other_y = self.z * 2 + self.other["x"], self.other["y"] * 2 + self.c
        self.device = {
            **{("z", hop): (self.around[hop] * 2 + self.x, seq) for hop in range(1, n_z)},
            ("x", 1): (other_x, seq),
            ("y", 1): (dp, other_y),
            ("c", 1): (dp, self.y * 2 + self.other["c"]),
            ("p", 1): (other_x, seq),
            ("p", 2): (dp, other_y),
            ("p", 3): (other_x, other_y),
            **{("d", hop): ((dp + hop) % n_dp, seq) for hop in range(1, n_dp)},
            **{("s", hop): (dp, (seq + hop) % 4) for hop in range(1, 4)},
        }
        self.device = {key: {"dp": there[0], "seq": there[1]} for key, there in self.device.items()}

    def hops(self, dim):
        return [hop for name, hop in self.device if name == dim]

    def enter(self):
        barrier = pltpu.get_barrier_semaphore()
        who = [key for key in self.device if key[0] in "ds"] + [("p", 3)]
        for key in who:
            pl.semaphore_signal(barrier, inc=1, device_id=self.device[key], device_id_type=MESH_ID)
        pl.semaphore_wait(barrier, len(who))

    def remote(self, src, dst, dim, hop=1, number=None):
        if number is None:
            number = self.next_sem
            self.next_sem += 1
        return pltpu.make_async_remote_copy(
            src, dst, self.ssem.at[number], self.rsem.at[number], device_id=self.device[dim, hop], device_id_type=MESH_ID
        )

    def local(self, src, dst):
        number = self.next_local
        self.next_local += 1
        return pltpu.make_async_copy(src, dst, self.lsem.at[number])


class Gather:
    def __init__(self, me, view, order):
        self.copies = []
        done = ""
        for dim in order:
            block = view(*[slice(None) if other in done else me.mine[other] for other in "zxyc"])
            self.copies.append([me.remote(block, block, dim, hop) for hop in me.hops(dim)])
            done += "xy" if dim == "p" else dim

    def start(self, stage):
        if stage:
            self.arrive(stage - 1)
        for copy in self.copies[stage]:
            copy.start()

    def arrive(self, stage=-1):
        for copy in self.copies[stage]:
            copy.wait_recv()

    def drain(self):
        for copies in self.copies:
            for copy in copies:
                copy.wait_send()


class Single:
    def __init__(self, copy):
        self.copy = copy

    def start(self, stage):
        self.copy.start()


class Reduce:
    def __init__(self, me, layer, grad, recv, out, cols, order, number, before):
        self.me, self.layer, self.grad, self.recv, self.out, self.cols, self.order = me, layer, grad, recv, out, cols, order
        self.number, self.before = number, before
        self.first_sem = before.first_sem if before else me.next_sem
        self.last = len(order) - 1
        self.copies = [self.build(stage) for stage in range(len(order))]

    def block(self, fixed):
        return tuple(fixed.get(dim, slice(None)) for dim in "zxyc")

    def kept(self, stage):
        done = "".join("xy" if dim == "p" else dim for dim in self.order[:stage])
        return {dim: self.me.mine[dim] for dim in done}

    def build(self, stage):
        me, dim = self.me, self.order[stage]
        copies = []
        number = self.first_sem + sum(len(me.hops(before)) for before in self.order[:stage])
        for hop in me.hops(dim):
            fixed = self.kept(stage)
            if dim == "z":
                fixed["z"] = me.around[hop]
            elif dim == "p":
                fixed["x"] = me.mine["x"] if hop == 2 else me.other["x"]
                fixed["y"] = me.mine["y"] if hop == 1 else me.other["y"]
            else:
                fixed[dim] = me.other[dim]
            src = self.grad.at[(self.layer, *self.block(fixed), slice(None), self.cols)]
            dst = self.landed(stage, hop).at[(*self.landing(stage, hop), slice(None), self.cols)]
            copies.append(me.remote(src, dst, dim, hop, number + len(copies) if self.before else None))
        return copies

    def landed(self, stage, hop):
        return self.recv[3] if stage == self.last else self.recv[stage]

    def landing(self, stage, hop):
        dim = self.order[stage]
        if stage == self.last:
            return (hop - 1,)
        if dim == "p":
            return (slice(None), hop - 1)
        if dim == "z":
            return (slice(2 * hop - 2, 2 * hop),)
        return ((slice(0, self.me.n_z), slice(None), slice(None)), (slice(None), slice(0, 2)), (slice(0, self.me.n_z),))[stage]

    def start(self, stage):
        me = self.me
        if stage:
            self.add(stage - 1)
            dim = self.order[stage - 1]
            if self.layer == LAYERS - 1:
                for hop in me.hops(dim):
                    pl.semaphore_signal(
                        me.credit.at[self.number, stage - 1], inc=1, device_id=me.device[dim, hop], device_id_type=MESH_ID
                    )
        if stage <= self.last:
            if self.layer < LAYERS - 1:
                pl.semaphore_wait(me.credit.at[self.number, stage], len(me.hops(self.order[stage])))
                for copy in self.before.copies[stage]:
                    copy.wait_send()
            for copy in self.copies[stage]:
                copy.start()

    def add(self, stage):
        me, dim = self.me, self.order[stage]
        for copy in self.copies[stage]:
            copy.wait_recv()
        fixed = self.kept(stage + 1)
        if stage == self.last or dim in "zp":
            where = (self.layer, *self.block(fixed), slice(None), self.cols)
            total = self.grad[where].astype(F32)
            for hop in me.hops(dim):
                total = total + self.landed(stage, hop)[(*self.landing(stage, hop), slice(None), self.cols)].astype(F32)
            if stage == self.last:
                self.out[self.layer, :, self.cols] = total
            else:
                self.grad[where] = total.astype(BF)
            return

        def one(z, carry):
            where = (self.layer, *self.block({**fixed, "z": z}), slice(None), self.cols)
            came = (z, *self.landing(stage, 1)[1:], slice(None), self.cols)
            self.grad[where] = self.grad[where] + self.recv[stage][came]
            return carry

        lax.fori_loop(0, me.n_z, one, 0)

    def drain(self):
        for copies in self.copies:
            for copy in copies:
                copy.wait_send()


def at_step(index, hooks):
    for when, action in hooks:
        pl.when(index == when)(action)


BACKWARD_AT = (21, 0)
END_AT = 42
GATHER = (
    ("pzc", 0, 2, 6),
    ("yzxc", 0, 2, 5, 6),
    ("zpc", 0, 2, 3),
    ("zpc", 0, 1, 5),
    ("pzc", 0, 3, 13),
    ("pzc", 2, 3, 10),
    ("zpc", 1, 3, 6),
    ("zpc", 0, 2, 13),
    ("pzc", 0, 4, 14),
    ("zyxc", 0, 4, 11, 14),
    ("zpc", 1, 5, 15),
    ("zpc", 2, 5, 12),
    ("zpc", 7, 18, 26),
    ("zpc", 3, 8, 20),
    ("pzc", 2, 18, 29),
    ("zpc", 7, 16, 27),
    ("pzc", 0, 11, 27),
    ("zpc", 10, 18, 27),
    ("pzc", 0, 1, 2),
    ("y", 0),
    ("y", 29),
)
REDUCE = (
    ("cpz", 5, 6, 12, 28),
    ("cxzy", 4, 11, 14, 33, 38),
    ("cpz", 3, 4, 14, 25),
    ("cxzy", 11, 14, 27, 34, 41),
    ("cpz", 10, 15, 22, 32),
    ("cpz", 9, 12, 32, 35),
    ("cpz", 15, 15, 25, 36),
    ("cpz", 15, 15, 28, 39),
    ("cpz", 19, 24, 32, 35),
    ("cpz", 19, 22, 27, 35),
    ("cpz", 26, 27, 33, 37),
    ("cxzy", 25, 29, 34, 44, 46),
    ("cpz", 23, 25, 32, 43),
    ("cxzy", 32, 33, 36, 44, 46),
    ("cpz", 35, 36, 41, 43),
    ("cpz", 32, 35, 40, 44),
    ("cpz", 36, 36, 43, 46),
    ("cpz", 36, 38, 42, 44),
    ("cpz", 38, 38, 42, 44),
    ("cpz", 38, 39, 42, 44),
    ("y", 39),
)

SMALL = "small"


def pieces(name, layer):
    return 4 if name == "q" and layer == 0 else 2


def by_place(moves, plan):
    timeline = {}
    for move, (_, *places) in zip(moves, plan, strict=True):
        for stage, place in enumerate(places):
            timeline.setdefault(place, []).append((move, stage))
    return timeline


def fused_kernel(n_z, *refs):
    me = Fused(n_z, refs)
    x, y, z, c = me.x, me.y, me.z, me.c
    n_dp = 2 * n_z
    spare = slice(None)

    mats = ((me.wq_i, me.Wq), (me.wo_i, me.Wo), (me.wu_i, me.Wu), (me.wd_i, me.Wd))
    loads = [me.local(src.at[layer], dst.at[layer, z, x, y, c]) for layer in range(LAYERS) for src, dst in mats]
    for load in loads:
        load.start()
    own_tokens = [
        me.local(src.at[seq], dst.at[tile]) for src, dst in ((me.xin, me.DO), (me.cot, me.GB)) for seq, tile in ((y, 0), (2, 2))
    ]
    for load in own_tokens:
        load.start()

    row = lax.broadcasted_iota(jnp.int32, (32, 128), 0)
    steps = jnp.zeros((32, 128), jnp.int32)
    for j in range(3):
        steps = jnp.where(row == 3 * me.dp + j, me.ts[j], steps)
    me.TT[z, x] = steps

    def choose(rows, cols, first):
        here = lax.broadcasted_iota(jnp.int32, (rows, cols), 1) == first + lax.broadcasted_iota(jnp.int32, (rows, cols), 0)
        return here.astype(F32)

    own_biases, own_gains = choose(160, 640, 160 * me.seq), choose(32, 128, 32 * me.seq)
    own_lanes = choose(16, 128, 16 * (4 * x + me.seq))
    spread_b = nn(me.biases_i[...].astype(F32), own_biases)
    spread_g = nn(me.gains_i[...].astype(F32), own_gains)
    rows = []
    for layer in range(LAYERS):
        rows += [spread_b[layer : layer + 1, 128 * r : 128 * r + 128] for r in range(5)] + [spread_g[layer : layer + 1]]
    me.SM[z, x, y, c] = jnp.concatenate(rows + [jnp.zeros((16 - 6 * LAYERS, 128), F32)], axis=0).astype(BF)
    me.BG[...] = jnp.zeros_like(me.BG)
    me.GG[...] = jnp.zeros_like(me.GG)

    me.enter()
    for load in loads:
        load.wait()

    def weight(layer, ref, order, cols):
        return Gather(me, lambda *where: ref.at[(layer, *where, spare, cols)], order)

    grads = {"q": me.Wq, "o": me.Wo, "u": me.Wu, "d": me.Wd}

    steps_all = Gather(me, lambda gz, gx, gy, gc: me.TT.at[gz, gx], "d")
    times = Gather(me, lambda *where: me.TS.at[where], "zpc")
    token_in = me.remote(me.xin.at[me.other["y"]], me.DO.at[1], "y")
    cot_in = me.remote(me.cot.at[me.other["y"]], me.GB.at[1], "y")
    moves = {}
    plan = iter(GATHER)
    for layer in range(LAYERS):
        for name, ref in grads.items():
            width = ref.shape[-1] // pieces(name, layer)
            for part in range(pieces(name, layer)):
                moves[name, part, layer] = weight(layer, ref, next(plan)[0], slice(width * part, width * (part + 1)))
    moves[SMALL] = small = Gather(me, lambda *where: me.SM.at[where], next(plan)[0])
    timeline = by_place([*moves.values(), Single(token_in), Single(cot_in)], GATHER)

    def have(names, layer):
        for name in names:
            for part in range(pieces(name, layer)):
                moves[name, part, layer].arrive()

    def fire(place):
        for move, stage in timeline.get(place, ()):
            move.start(stage)

    def fires(first, count):
        return [(i, functools.partial(fire, first + i)) for i in range(count) if first + i in timeline]

    steps_all.start(0)
    fire(0)
    fire(1)
    steps_all.arrive()
    t24 = jnp.sum(me.TT[...].reshape(n_dp, 32, 128), axis=0)
    me.T24[...] = t24
    hot = (t24[:, 0:1] == lax.broadcasted_iota(jnp.int32, (32, STEPS), 1)).astype(F32).astype(BF)
    picked = jnp.concatenate([nt(hot, me.tab[layer])[:24] for layer in range(LAYERS)], axis=0).astype(BF)
    me.TS[z, x, y, c] = nn(picked, own_lanes.astype(BF)).astype(BF)
    times.start(0)
    fire(2)
    times.start(1)
    fire(3)
    times.start(2)
    fire(4)
    fire(5)

    small.arrive()
    for gz in range(n_z):
        for gx in range(2):
            block = jnp.sum(me.SM[gz, gx].reshape(4, 16, 128).astype(F32), axis=0)
            dp = 2 * gz + gx
            for layer in range(LAYERS):
                for r in range(5):
                    at = (5 * dp + r) * 128
                    me.BV[layer, :, at : at + 128] = block[6 * layer + r : 6 * layer + r + 1]
                me.GV[layer, :, 128 * dp : 128 * dp + 128] = block[6 * layer + 5 : 6 * layer + 6]
    times.arrive()
    slabs = jnp.concatenate(
        [jnp.sum(me.TS[gz].reshape(8, 48, 128).astype(F32), axis=0) for gz in range(n_z)], axis=1
    ).astype(BF)
    r8 = lax.broadcasted_iota(jnp.int32, (16, 48), 0)
    c48 = lax.broadcasted_iota(jnp.int32, (16, 48), 1)
    for layer in range(LAYERS):
        base = 24 * layer + 3 * me.dp
        pick = ((r8 == 0) & (c48 == base + y)) | ((r8 == 1) & (c48 == base + 2))
        me.TR[layer] = nn(pick.astype(F32).astype(BF), slabs)[:8]

    def time_row(layer, tile):
        return me.TR[layer, 1:2, :] if tile == 2 else me.TR[layer, 0:1, :]

    def bias(layer, at, width=D):
        return me.BV[layer, :, at : at + width]

    for load in own_tokens:
        load.wait()
    token_in.wait_recv()
    for tile in range(3):
        me.X[0, tile] = me.DO[tile].astype(F32) + time_row(0, tile)

    fire(6)
    have("q", 0)

    sends = [token_in, cot_in]

    def send(src, dst, dim):
        copy = me.remote(src, dst, dim)
        sends.append(copy)
        return copy

    def qkv(layer, tile):
        hat, _ = ln_parts(me.X[layer, tile])
        normed = (hat * me.GV[layer, :, :D] + bias(layer, B_S1)).astype(BF)
        slot = 4 if tile == 2 else tile
        lin = [nn(normed, me.Wq[layer, :, :, :, :, :, D * j : D * j + D].reshape(D, D)) for j in range(3)]
        me.Q[layer, tile] = (lin[0] + bias(layer, B_Q)).astype(BF) * jnp.asarray(1.0 / math.sqrt(HEAD_DIM), BF)
        me.KV[layer, 0, slot] = lin[1].astype(BF)
        me.KV[layer, 1, slot] = (lin[2] + bias(layer, B_V)).astype(BF)

    low_lanes = lax.broadcasted_iota(jnp.int32, (TILE, 128), 1) < HEAD_DIM

    def two_heads(pair):
        zero = jnp.zeros_like(pair)
        return jnp.concatenate([jnp.where(low_lanes, pair, zero), jnp.where(low_lanes, zero, pair)], axis=0)

    def attend_two(layer, step):
        tile, base = step // 2, step // 4 * 4
        first = step % 2 * 2
        cols = [pl.ds(pl.multiple_of((first + i) * 128, 128), 128) for i in range(2)]
        queries = [two_heads(me.Q[layer, tile, :, cols[i]]) for i in range(2)]

        def block(which, part, i):
            return me.KV[layer, which, pl.ds(base + 2 * part, 2), :, cols[i]].reshape(2 * TILE, 128)

        def scores(part, i):
            return nt(block(0, part, i), queries[i])

        def highest(parts):
            tops = [jnp.max(part, axis=0, keepdims=True) for part in parts]
            return jnp.maximum(tops[0], tops[1]) * LOG2E

        def mix(score, top, part, i):
            values = jnp.concatenate([block(1, part, i).T, jnp.ones((16, 2 * TILE), BF)], axis=0)
            return nn(values, jnp.exp2(score * LOG2E - top).astype(BF))

        def finish(mixed, top, i):
            total = mixed[128:129]
            mixed = mixed[:128] * (1.0 / total)
            me.LSE[layer, tile, first + i] = top + jnp.log2(total)
            out = jnp.concatenate([mixed[:HEAD_DIM, :TILE], mixed[HEAD_DIM:, TILE:]], axis=0)
            me.AO[layer, tile, :, cols[i]] = out.T.astype(BF)

        now = [scores(0, 0), scores(1, 0)]
        top = highest(now)
        later, mixed = [], 0.0
        for part in range(2):
            later.append(scores(part, 1))
            mixed = mixed + mix(now[part], top, part, 0)
        finish(mixed, top, 0)
        top = highest(later)
        finish(mix(later[0], top, 0, 1) + mix(later[1], top, 1, 1), top, 1)

    kv = me.KV
    to_y = [[send(kv.at[layer, i, 4], kv.at[layer, i, 5], "y") for i in range(2)] for layer in range(LAYERS)]
    on_c = [[send(kv.at[layer, i, 5], kv.at[layer, i, 7], "c") for i in range(2)] for layer in range(LAYERS)]
    to_c = [
        [send(kv.at[layer, :, a], kv.at[layer, :, b], "c") for a, b in ((0, 2), (1, 3), (4, 6))] for layer in range(LAYERS)
    ]

    def project(layer, tile):
        qkv(layer, tile)
        if tile == 2:
            for copy in to_y[layer]:
                copy.start()
        to_c[layer][tile].start()

    def attention(layer, first, last, place):
        def step(index, carry):
            at_step(index - first, fires(place, last - first))
            attend_two(layer, index)
            return carry

        lax.fori_loop(first, last, step, 0)

    def rest(layer, tiles, place):
        if tiles[0] == 0:
            have("o", layer)
        fire(place)
        w_out = me.Wo[layer].reshape(D, D)
        for tile in tiles:
            after = me.X[layer, tile] + nn(me.AO[layer, tile], w_out) + bias(layer, B_O)
            me.Y[layer, tile] = after
            hat, _ = ln_parts(after)
            me.N[tile] = (hat * me.GV[layer, :, D:] + bias(layer, B_S2)).astype(BF)
            me.GN[tile] = after + bias(layer, B_D)
        if tiles[0] == 0:
            have("ud", layer)

        def ffn(half, carry):
            at_step(half, fires(place + 1, 2))
            cols = pl.ds(pl.multiple_of(half * (FF // 2), FF // 2), FF // 2)
            w_up = me.Wu[layer, :, :, :, :, :, cols].reshape(D, FF // 2)
            w_down = me.Wd[layer, pl.ds(half * (n_z // 2), n_z // 2)].reshape(FF // 2, D)
            b_up = me.BV[layer, :, pl.ds(pl.multiple_of(B_U + half * (FF // 2), D), FF // 2)]
            for tile in tiles:
                up = nn(me.N[tile], w_up) + b_up
                _, tanh = gelu_parts(up)
                me.GN[tile] += nn((0.5 * up * (1.0 + tanh)).astype(BF), w_down)
            return carry

        lax.fori_loop(0, 2, ffn, 0)

    def pass_on(layer, i):
        to_y[layer][i].wait_recv()
        on_c[layer][i].start()

    def third_keys(layer):
        pass_on(layer, 1)
        for copy in [to_c[layer][2], *on_c[layer]]:
            copy.wait_recv()

    project(0, 2)
    fire(7)
    project(0, 0)
    fire(8)
    project(0, 1)
    fire(9)
    to_c[0][0].wait_recv()
    to_c[0][1].wait_recv()
    attention(0, 0, 4, 10)
    rest(0, (0, 1), 14)
    pass_on(0, 0)
    for tile in range(2):
        me.X[1, tile] = me.GN[tile] + time_row(1, tile)
    fire(17)
    have("q", 1)
    project(1, 0)
    project(1, 1)
    fire(18)
    third_keys(0)
    attention(0, 4, 6, 19)
    rest(0, (2,), 21)
    me.X[1, 2] = me.GN[2] + time_row(1, 2)
    project(1, 2)
    fire(24)
    to_c[1][0].wait_recv()
    to_c[1][1].wait_recv()
    attention(1, 0, 4, 25)
    rest(1, (0, 1), 29)
    pass_on(1, 0)
    act_out = [
        me.local(me.DO.at[0], me.act_o.at[y]), me.remote(me.DO.at[1], me.act_o.at[y], "y"), me.local(me.DO.at[2], me.act_o.at[2])
    ]
    for tile in range(2):
        me.DO[tile] = me.GN[tile].astype(BF)
    third_keys(1)
    attention(1, 4, 6, 32)
    rest(1, (2,), 34)
    me.DO[2] = me.GN[2].astype(BF)
    for copy in act_out:
        copy.start()

    cot_in.wait_recv()
    weight_y, weight_2 = me.imp[me.ts[y]], me.imp[me.ts[2]]
    for tile in range(3):
        grad = me.GB[tile].astype(F32) * (weight_2 if tile == 2 else weight_y)
        me.G[tile] = grad
    for part in [steps_all, times, *moves.values()]:
        part.drain()
    for copy in sends:
        copy.wait_send()
    sends.clear()

    outs = {"q": me.gq_o, "o": me.go_o, "u": me.gu_o, "d": me.gd_o}
    recvs = {
        name: [me.R1[i], me.R2[i], me.R3[i], me.R4[i]] for i, name in enumerate("qoud")
    }

    spans = {
        "d": ("d", 0, D), "u": ("u", 0, FF), "o": ("o", 0, D), "p": ("q", 0, D), "q": ("q", D, 3 * D)
    }

    plan = iter(REDUCE)

    def piece(layer, number, name, half):
        kind, begin, end = spans[name]
        width = (end - begin) // 2
        start = begin + width * half
        before = sums[number] if layer < LAYERS - 1 else None
        cols = slice(start, start + width)
        return Reduce(me, layer, grads[kind], recvs[kind], outs[kind], cols, next(plan)[0], number, before)

    def add_bias(layer, at, value):
        me.BG[layer, :, at : at + value.shape[-1]] += value

    def ln_back(layer, gain_at, shift_at, source, grad):
        hat, scale = ln_parts(source)
        me.GG[layer, :, gain_at : gain_at + D] += rows_sum(grad * hat)
        add_bias(layer, shift_at, rows_sum(grad))
        inner = grad * me.GV[layer, :, gain_at : gain_at + D]
        return scale * (inner - jnp.mean(inner, axis=-1, keepdims=True) - hat * jnp.mean(inner * hat, axis=-1, keepdims=True))

    def normed_t(layer, source, gain_at, shift_at):
        for tile in range(3):
            hat, _ = ln_parts(source[layer, tile])
            normed = (hat * me.GV[layer, :, gain_at : gain_at + D] + bias(layer, shift_at)).astype(BF)
            me.N[tile] = normed
            me.NT[:, TILE * tile : TILE * tile + TILE] = normed.T

    head_of = lax.broadcasted_iota(jnp.int32, (HEADS, D), 1) // HEAD_DIM
    selector = (head_of == lax.broadcasted_iota(jnp.int32, (HEADS, D), 0)).astype(F32)

    def backward(layer, before_out, tail):
        base = BACKWARD_AT[layer]
        normed_t(layer, me.Y, D, B_S2)
        for tile in range(3):
            me.GB[tile] = me.G[tile].astype(BF)
            add_bias(layer, B_D, rows_sum(me.G[tile]))
            me.GN[tile] = jnp.zeros((TILE, D), F32)

        def ffn(slab, carry):
            at_step(slab, fires(base, n_z))
            cols = pl.ds(pl.multiple_of(slab * D, D), D)
            b_cols = pl.ds(pl.multiple_of(B_U + slab * D, D), D)
            w_up = me.Wu[layer, :, :, :, :, :, cols].reshape(D, D)
            w_down = me.Wd[layer, slab].reshape(D, D)
            grads_h = me.GB[...].reshape(3 * TILE, D)
            up = nn(me.N[...].reshape(3 * TILE, D), w_up) + me.BV[layer, :, b_cols]
            square, tanh = gelu_parts(up)
            active = (0.5 * up * (1.0 + tanh)).astype(BF)
            slope = 0.5 * (1.0 + tanh) + (0.5 * GELU_A) * up * (1.0 - tanh * tanh) * (1.0 + 3.0 * GELU_B * square)
            grad_up = nt(grads_h, w_down) * slope
            me.BG[layer, :, b_cols] += rows_sum(grad_up)
            grad_up = grad_up.astype(BF)
            me.GN[...] += nt(grad_up, w_up).reshape(3, TILE, D)
            me.Wd[layer, slab] = tn(active, grads_h).astype(BF).reshape(2, 2, 2, 64, D)
            me.Wu[layer, :, :, :, :, :, cols] = nn(me.NT[...], grad_up).astype(BF).reshape(n_z, 2, 2, 2, 16, D)
            return carry

        lax.fori_loop(0, n_z, ffn, 0)
        fire(base + 4)
        for tile in range(3):
            mid = me.G[tile] + ln_back(layer, D, B_S2, me.Y[layer, tile], me.GN[tile])
            me.G[tile] = mid
            add_bias(layer, B_O, rows_sum(mid))
            me.GB[tile] = mid.astype(BF)
        fire(base + 5)
        before_out()
        w_out = me.Wo[layer].reshape(D, D)
        for tile in range(3):
            grad_attn = nt(me.GB[tile], w_out).astype(BF)
            me.DO[tile] = grad_attn
            delta = nt(selector, grad_attn.astype(F32) * me.AO[layer, tile].astype(F32), lax.Precision.HIGHEST)
            for pair in range(PAIRS):
                both = jnp.concatenate([delta[2 * pair : 2 * pair + 1], delta[2 * pair + 1 : 2 * pair + 2]], axis=1)
                me.DL[tile, pair] = both
        d_out = tn(me.AO[layer].reshape(3 * TILE, D), me.GB[...].reshape(3 * TILE, D))
        me.Wo[layer] = d_out.astype(BF).reshape(n_z, 2, 2, 2, 16, D)
        fire(base + 6)

        me.ACC[...] = jnp.zeros_like(me.ACC)
        third_c = send(me.PB.at[:, 1:3], me.RB1, "c")
        third_y = send(me.PB.at[:, 0], me.RB2, "y")
        from_c = me.remote(me.GL.at[0:2, :, D:], me.RB3, "c")

        def third_done():
            me.OWN[...] = me.ACC[:, 0:TILE]
            me.PB[...] = me.ACC[:, TILE : 4 * TILE].reshape(2, 3, TILE, D).astype(BF)
            me.ACC[...] = jnp.zeros_like(me.ACC)
            third_c.start()

        def third_on():
            third_c.wait_recv()
            me.OWN[...] += me.RB1[:, 0].astype(F32)
            me.PB[:, 0] = me.PB[:, 0] + me.RB1[:, 1]
            third_y.start()

        def attend_back(step, carry):
            at_step(step, [(2, third_done), (3, third_on)] + fires(base + 8, 6))
            tile = (step // 2 + 2) % 3
            slot = tile // 2 * 4
            for i in range(2):
                pair = step % 2 * 2 + i
                cols = pl.ds(pl.multiple_of(pair * 128, 128), 128)
                queries, grads_o = two_heads(me.Q[layer, tile, :, cols]), two_heads(me.DO[tile, :, cols])
                log_sum, delta = me.LSE[layer, tile, pair], me.DL[tile, pair]
                d_query = jnp.zeros((128, 2 * TILE), F32)
                for part in range(4):
                    keys, values = me.KV[layer, 0, slot + part, :, cols], me.KV[layer, 1, slot + part, :, cols]
                    rows = slice(TILE * part, TILE * part + TILE)
                    prob = jnp.exp2(nt(keys, queries) * LOG2E - log_sum)
                    grad_s = (prob * (nt(values, grads_o) - delta)).astype(BF)
                    me.ACC[1, rows, cols] += nn(prob.astype(BF), grads_o)
                    me.ACC[0, rows, cols] += nn(grad_s, queries)
                    d_query = d_query + nn(keys.T, grad_s)
                d_query = jnp.concatenate([d_query[:HEAD_DIM, :TILE], d_query[HEAD_DIM:, TILE:]], axis=0).T
                d_query = d_query * (1.0 / math.sqrt(HEAD_DIM))
                me.BG[layer, :, cols] += rows_sum(d_query)
                me.GL[tile, :, cols] = d_query.astype(BF)
            return carry

        fire(base + 7)
        lax.fori_loop(0, 6, attend_back, 0)
        for tile in range(2):
            for i in range(2):
                rows = slice(TILE * (2 + tile), TILE * (3 + tile))
                me.GL[tile, :, D * (1 + i) : D * (2 + i)] = me.ACC[i, rows].astype(BF)
        from_c.start()
        normed_t(layer, me.X, 0, B_S1)
        fire(base + 14)

        def qkv_back(first, last):
            w_qkv = me.Wq[layer, :, :, :, :, :, first:last].reshape(D, last - first)
            for tile in range(3):
                part = nt(me.GL[tile, :, first:last], w_qkv)
                me.GN[tile] = part if first == 0 else me.GN[tile] + part
            for j in range(first, last, D):
                d_qkv = nn(me.NT[...], me.GL[:, :, j : j + D].reshape(3 * TILE, D))
                me.Wq[layer, :, :, :, :, :, j : j + D] = d_qkv.astype(BF).reshape(n_z, 2, 2, 2, 16, D)

        qkv_back(0, D)
        fire(base + 15)
        from_c.wait()
        for tile in range(2):
            rows = slice(TILE * tile, TILE * tile + TILE)
            key = me.ACC[0, rows] + me.RB3[tile, :, :D].astype(F32)
            value = me.ACC[1, rows] + me.RB3[tile, :, D:].astype(F32)
            add_bias(layer, B_V, rows_sum(value))
            me.GL[tile, :, D : 2 * D] = key.astype(BF)
            me.GL[tile, :, 2 * D :] = value.astype(BF)
        third_y.wait_recv()
        third = me.OWN[...] + me.RB2[...].astype(F32)
        me.GL[2, :, D : 2 * D] = third[0].astype(BF)
        me.GL[2, :, 2 * D :] = third[1].astype(BF)
        add_bias(layer, B_V, rows_sum(third[1]))
        fire(base + 16)
        qkv_back(D, 3 * D)
        fire(base + 17)
        totals = []
        for tile in (1, 0, 2):
            grad = me.G[tile] + ln_back(layer, 0, B_S1, me.X[layer, tile], me.GN[tile])
            me.G[tile] = grad
            totals.append(rows_sum(grad))
            tail(tile, grad)
            fire(base + 17 + len(totals))
        me.TG[layer, 0:1] = totals[0] + totals[1]
        me.TG[layer, 1:2] = totals[2]
        for copy in sends:
            copy.wait_send()
        sends.clear()

    sums = []
    for layer in reversed(range(LAYERS)):
        for number, (name, half) in enumerate((name, half) for name in spans for half in range(2)):
            sums.append(piece(layer, number, name, half))
    timeline.clear()
    gin_out = me.remote(me.GB.at[1], me.gin_o.at[y], "y")
    timeline.update(by_place([*sums, Single(gin_out)], REDUCE))

    def act_done():
        for copy in act_out:
            copy.wait()

    backward(1, act_done, lambda tile, grad: None)
    finals = []

    def out_tile(tile, grad):
        me.GB[tile] = grad.astype(BF)
        if tile != 1:
            finals.append(me.local(me.GB.at[tile], me.gin_o.at[y if tile == 0 else 2]))
            finals[-1].start()

    backward(0, lambda: None, out_tile)

    for gz in range(n_z):
        lanes = slice(128 * gz, 128 * gz + 128)
        for gx in range(2):
            dp = 2 * gz + gx
            for layer in range(LAYERS):
                for r in range(5):
                    at_lane = (5 * dp + r) * 128
                    me.SR[gz, gx, 6 * layer + r : 6 * layer + r + 1] = me.BG[layer, :, at_lane : at_lane + 128]
                me.SR[gz, gx, 6 * layer + 5 : 6 * layer + 6] = me.GG[layer, :, 128 * dp : 128 * dp + 128]
                me.SR[gz, gx, 12 + 2 * layer : 14 + 2 * layer] = me.TG[layer, 0:2, lanes]
    to_dp = [
        me.remote(me.SR.at[me.far_z[hop], me.far_x[hop]], me.SX.at[me.dp], "d", hop) for hop in me.hops("d")
    ]
    for copy in to_dp:
        copy.start()
    me.SX[me.dp] = me.SR[z, x]
    fire(END_AT)
    for copy in to_dp:
        copy.wait_recv()
    fire(END_AT + 1)
    me.SY[0, 0:16] = jnp.sum(me.SX[...], axis=0)
    for dp in range(n_dp):
        for layer in range(LAYERS):
            at_row = 16 + 24 * layer + 3 * dp
            first_seq = me.SX[dp, 12 + 2 * layer : 13 + 2 * layer]
            me.SY[0, at_row : at_row + 1] = jnp.where(y == 0, first_seq, 0.0)
            me.SY[0, at_row + 1 : at_row + 2] = jnp.where(y == 1, first_seq, 0.0)
            me.SY[0, at_row + 2 : at_row + 3] = me.SX[dp, 13 + 2 * layer : 14 + 2 * layer]
    to_seq = [me.remote(me.SY.at[0], me.SY.at[hop], "s", hop) for hop in me.hops("s")]
    for copy in to_seq:
        copy.start()
    fire(END_AT + 2)
    for copy in to_seq:
        copy.wait_recv()
    fire(END_AT + 3)
    total = me.SY[0] + me.SY[1] + me.SY[2] + me.SY[3]
    hot = (me.T24[0:24, 0:1] == lax.broadcasted_iota(jnp.int32, (24, STEPS), 1)).astype(F32)
    for layer in range(LAYERS):
        bias_row = jnp.concatenate([total[6 * layer + r : 6 * layer + r + 1] for r in range(5)], axis=1)
        me.gb_o[layer : layer + 1] = nt(bias_row, own_biases, HIGH)
        me.gg_o[layer : layer + 1] = nt(total[6 * layer + 5 : 6 * layer + 6], own_gains, HIGH)
        by_seq = nt(own_lanes, total[16 + 24 * layer : 40 + 24 * layer], HIGH)
        me.gt_o[layer] = jnp.dot(by_seq, hot, precision=HIGH, preferred_element_type=F32)
    fire(END_AT + 4)

    for copy in to_dp + to_seq:
        copy.wait_send()
    for copy in [gin_out, *finals]:
        copy.wait()
    for part in sums[len(sums) // 2 :]:
        part.drain()


def fused_call(n_z, *operands):
    any_space, vmem, smem = (pl.BlockSpec(memory_space=space) for space in (pl.ANY, pltpu.VMEM, pltpu.SMEM))
    cube = (n_z, 2, 2, 2)
    tokens = (3, TILE, D)
    sizes = ((16, 3 * D), (16, D), (16, FF), (64, D))

    def many(lead):
        return [tuple(pltpu.VMEM((*lead, *size), BF) for size in sizes)]

    flat, tree = jax.tree.flatten(
        [pltpu.VMEM((LAYERS, *cube, *size), BF) for size in sizes]
        + [
            pltpu.VMEM((*cube, 16, 128), BF),
            pltpu.VMEM((*cube, 48, 128), BF),
            pltpu.VMEM((n_z, 2, 32, 128), jnp.int32),
            pltpu.VMEM((32, 128), jnp.int32),
            pltpu.VMEM((LAYERS, 8, D), F32),
            pltpu.VMEM((LAYERS, 1, 6 * D + FF), F32),
            pltpu.VMEM((LAYERS, 1, 2 * D), F32),
            pltpu.VMEM((LAYERS, 1, 6 * D + FF), F32),
            pltpu.VMEM((LAYERS, 1, 2 * D), F32),
            pltpu.VMEM((LAYERS, 8, D), F32),
            pltpu.VMEM((LAYERS, *tokens), F32),
            pltpu.VMEM(tokens, BF),
            pltpu.VMEM((D, 3 * TILE), BF),
            pltpu.VMEM((LAYERS, *tokens), BF),
            pltpu.VMEM((LAYERS, 2, 8, TILE, D), BF),
            pltpu.VMEM((LAYERS, *tokens), BF),
            pltpu.VMEM((LAYERS, 3, PAIRS, 1, 2 * TILE), F32),
            pltpu.VMEM((3, PAIRS, 1, 2 * TILE), F32),
            pltpu.VMEM((LAYERS, *tokens), F32),
            pltpu.VMEM(tokens, BF),
            pltpu.VMEM(tokens, BF),
            pltpu.VMEM(tokens, F32),
            pltpu.VMEM(tokens, F32),
            pltpu.VMEM((3, TILE, 3 * D), BF),
            pltpu.VMEM((2, 4 * TILE, D), F32),
            pltpu.VMEM((2, TILE, D), F32),
            pltpu.VMEM((2, 3, TILE, D), BF),
            pltpu.VMEM((2, 2, TILE, D), BF),
            pltpu.VMEM((2, TILE, D), BF),
            pltpu.VMEM((2, TILE, 2 * D), BF),
        ]
        + many((n_z, 2, 2))
        + many((n_z, 3))
        + many((2 * n_z - 2,))
        + many((n_z - 1,))
        + [
            pltpu.VMEM((n_z, 2, 16, 128), F32),
            pltpu.VMEM((2 * n_z, 16, 128), F32),
            pltpu.VMEM((4, 64, 128), F32),
            pltpu.SemaphoreType.DMA((N_SEMS,)),
            pltpu.SemaphoreType.DMA((N_SEMS,)),
            pltpu.SemaphoreType.DMA((32,)),
            pltpu.SemaphoreType.REGULAR((10, 4)),
        ]
    )
    outs = [
        jax.ShapeDtypeStruct(tokens, BF),
        jax.ShapeDtypeStruct(tokens, BF),
        *[jax.ShapeDtypeStruct((LAYERS, *size), F32) for size in sizes],
        jax.ShapeDtypeStruct((LAYERS, 32), F32),
        jax.ShapeDtypeStruct((LAYERS, 160), F32),
        jax.ShapeDtypeStruct((LAYERS, 16, STEPS), F32),
    ]

    def run(*refs):
        head = len(operands) + len(outs)
        fused_kernel(n_z, *refs[:head], *jax.tree.unflatten(tree, refs[head:]))

    return pl.pallas_call(
        run,
        out_shape=outs,
        in_specs=[smem, smem] + [any_space] * 6 + [vmem] * 3,
        out_specs=[any_space] * 2 + [vmem] * 7,
        scratch_shapes=flat,
        compiler_params=pltpu.CompilerParams(collective_id=0, has_side_effects=True, vmem_limit_bytes=VMEM_BYTES),
    )(*operands)


VMEM_BYTES = 127 * 512 * 1024


def fused_body(
    inputs, cotangent, w_qkv, w_out, w_up, w_down, norm_gains, biases, time_table, timesteps, importance
):
    act, grad_in, g_qkv, g_out, g_up, g_down, grad_gains, grad_biases, grad_table = fused_call(
        lax.axis_size("dp") // 2, timesteps, importance, jnp.swapaxes(inputs, 0, 1), jnp.swapaxes(cotangent, 0, 1),
        w_qkv, w_out, w_up, w_down, norm_gains, biases, jnp.swapaxes(time_table, 1, 2),
    )
    return (
        jnp.swapaxes(act, 0, 1).astype(F32), jnp.swapaxes(grad_in, 0, 1).astype(F32), g_qkv, g_out, g_up, g_down,
        grad_gains, grad_biases, jnp.swapaxes(grad_table, 1, 2),
    )


def solution(mesh):
    devices = mesh.shape["dp"] * mesh.shape["seq"]
    whole_tiles = mesh.shape["seq"] == 4 and mesh.shape["dp"] % 2 == 0 and D // devices == 16
    in_specs = (
        P("seq", "dp", None),
        P("seq", "dp", None),
        P(None, ("dp", "seq"), None),
        P(None, ("dp", "seq"), None),
        P(None, ("dp", "seq"), None),
        P(None, ("dp", "seq"), None),
        P(None, ("dp", "seq")),
        P(None, ("dp", "seq")),
        P(None, None, ("dp", "seq")),
        P("dp"),
        P(),
    )
    out_specs = (
        P("seq", "dp", None),
        P("seq", "dp", None),
        P(None, ("dp", "seq"), None),
        P(None, ("dp", "seq"), None),
        P(None, ("dp", "seq"), None),
        P(None, ("dp", "seq"), None),
        P(None, ("dp", "seq")),
        P(None, ("dp", "seq")),
        P(None, None, ("dp", "seq")),
    )
    return jax.shard_map(
        fused_body if whole_tiles else body, mesh=mesh, in_specs=in_specs, out_specs=out_specs, check_vma=False)
```

```python
import functools
import math

import jax
import jax.numpy as jnp
from jax import lax
from jax.experimental import pallas as pl
from jax.experimental.pallas import tpu as pltpu
from jax.sharding import PartitionSpec as P

D = 512
HEADS = 8
HEAD_DIM = 64
FF = 2048
STEPS = 1000
LAYERS = 2


EPS = 1e-05
HIGH = lax.Precision.HIGHEST


def layer_norm(values, gain_vec, bias_vec):
    centered = values - jnp.mean(values, axis=-1, keepdims=True)
    spread = jnp.mean(centered * centered, axis=-1, keepdims=True)
    return centered * lax.rsqrt(spread + EPS) * gain_vec + bias_vec


def attend(queries, keys_all, values_all):
    row_count, seq_count, model_width = queries.shape
    score_scale = 1.0 / math.sqrt(HEAD_DIM)

    def per_seq(seq_index, loop_state):
        outputs, log_tot = loop_state
        query_per_head = lax.dynamic_index_in_dim(queries, seq_index, 1, keepdims=False).reshape(
            row_count, HEADS, HEAD_DIM
        )
        key_per_head = lax.dynamic_index_in_dim(keys_all, seq_index, 1, keepdims=False).reshape(
            -1, HEADS, HEAD_DIM
        )
        value_per_head = lax.dynamic_index_in_dim(values_all, seq_index, 1, keepdims=False).reshape(
            -1, HEADS, HEAD_DIM
        )
        scores = (
            jnp.einsum(
                "xsv,usv->sxu", query_per_head, key_per_head, preferred_element_type=jnp.float32
            )
            * score_scale
        )
        row_max = jnp.max(scores, axis=-1, keepdims=True)
        expon = jnp.exp(scores - row_max)
        summed = jnp.sum(expon, axis=-1, keepdims=True)
        attention_probability = (expon / summed).astype(jnp.bfloat16)
        attn_out = jnp.einsum(
            "gir,rgo->igo",
            attention_probability,
            value_per_head,
            preferred_element_type=jnp.float32,
        )
        attn_out = attn_out.astype(jnp.bfloat16).reshape(row_count, 1, model_width)
        outputs = lax.dynamic_update_slice_in_dim(outputs, attn_out, seq_index, 1)
        log_tot = lax.dynamic_update_slice_in_dim(
            log_tot, (row_max + jnp.log(summed))[None, :, :, 0], seq_index, 0
        )
        return (outputs, log_tot)

    start_state = (
        jnp.zeros(queries.shape, jnp.bfloat16),
        jnp.zeros((seq_count, HEADS, row_count), jnp.float32),
    )
    return lax.fori_loop(0, seq_count, per_seq, start_state)


def attend_back(queries, keys_all, values_all, log_tot, grad_attn):
    row_count, seq_count, model_width = queries.shape
    key_count = keys_all.shape[0]
    score_scale = 1.0 / math.sqrt(HEAD_DIM)

    def per_seq(seq_index, loop_state):
        grad_query, part_key, part_value = loop_state
        query_per_head = lax.dynamic_index_in_dim(queries, seq_index, 1, keepdims=False).reshape(
            row_count, HEADS, HEAD_DIM
        )
        key_per_head = lax.dynamic_index_in_dim(keys_all, seq_index, 1, keepdims=False).reshape(
            key_count, HEADS, HEAD_DIM
        )
        value_per_head = lax.dynamic_index_in_dim(values_all, seq_index, 1, keepdims=False).reshape(
            key_count, HEADS, HEAD_DIM
        )
        hidden_state_gradient = lax.dynamic_index_in_dim(
            grad_attn, seq_index, 1, keepdims=False
        ).reshape(row_count, HEADS, HEAD_DIM)
        log_seq = lax.dynamic_index_in_dim(log_tot, seq_index, 0, keepdims=False)
        scores = (
            jnp.einsum(
                "xsv,usv->sxu", query_per_head, key_per_head, preferred_element_type=jnp.float32
            )
            * score_scale
        )
        attn_f = jnp.exp(scores - log_seq[:, :, None])
        attention_probability = attn_f.astype(jnp.bfloat16)
        value_part = jnp.einsum(
            "uxo,xuc->ouc",
            attention_probability,
            hidden_state_gradient,
            preferred_element_type=jnp.float32,
        )
        probability_gradient = jnp.einsum(
            "xsv,usv->sxu",
            hidden_state_gradient,
            value_per_head,
            preferred_element_type=jnp.float32,
        )
        row_delta = jnp.sum(probability_gradient * attn_f, axis=-1, keepdims=True)
        score_gradient = (attn_f * (probability_gradient - row_delta)).astype(jnp.bfloat16)
        query_part = (
            jnp.einsum(
                "gir,rgo->igo", score_gradient, key_per_head, preferred_element_type=jnp.float32
            )
            * score_scale
        )
        key_part = (
            jnp.einsum(
                "uxo,xuc->ouc", score_gradient, query_per_head, preferred_element_type=jnp.float32
            )
            * score_scale
        )
        grad_query = lax.dynamic_update_slice_in_dim(
            grad_query, query_part.reshape(row_count, 1, model_width), seq_index, 1
        )
        part_key = lax.dynamic_update_slice_in_dim(
            part_key, key_part.reshape(key_count, 1, model_width), seq_index, 1
        )
        part_value = lax.dynamic_update_slice_in_dim(
            part_value, value_part.reshape(key_count, 1, model_width), seq_index, 1
        )
        return (grad_query, part_key, part_value)

    start_state = (
        jnp.zeros(queries.shape, jnp.float32),
        jnp.zeros(keys_all.shape, jnp.float32),
        jnp.zeros(keys_all.shape, jnp.float32),
    )
    return lax.fori_loop(0, seq_count, per_seq, start_state)


def forward_layer(hidden, fetched, onehot):
    mat_qkv, mat_out, up_matrix, down_matrix, gain_row, bias_row, time_rows = fetched
    gain_f = gain_row.astype(jnp.float32)
    bias_f = bias_row.astype(jnp.float32)
    seq_embed = jnp.dot(onehot.astype(jnp.bfloat16), time_rows, preferred_element_type=jnp.float32)
    summed_in = hidden + seq_embed[None]
    normed_one = layer_norm(summed_in, gain_f[:D], bias_f[4 * D + FF : 5 * D + FF]).astype(
        jnp.bfloat16
    )
    linear = jnp.dot(normed_one, mat_qkv, preferred_element_type=jnp.float32)
    queries = (linear[..., :D] + bias_f[:D]).astype(jnp.bfloat16)
    keys_loc = linear[..., D : 2 * D].astype(jnp.bfloat16)
    values_loc = (linear[..., 2 * D :] + bias_f[D : 2 * D]).astype(jnp.bfloat16)
    keys_all, values_all = (
        lax.all_gather(keys_loc, "seq", axis=0, tiled=True),
        lax.all_gather(values_loc, "seq", axis=0, tiled=True),
    )
    attn_out, log_tot = attend(queries, keys_all, values_all)
    after_attn = (
        summed_in
        + jnp.dot(attn_out, mat_out, preferred_element_type=jnp.float32)
        + bias_f[2 * D : 3 * D]
    )
    second_normalized = layer_norm(after_attn, gain_f[D:], bias_f[5 * D + FF :]).astype(
        jnp.bfloat16
    )
    upward = (
        jnp.dot(second_normalized, up_matrix, preferred_element_type=jnp.float32)
        + bias_f[3 * D : 3 * D + FF]
    )
    gelu_output = jax.nn.gelu(upward).astype(jnp.bfloat16)
    result = (
        after_attn
        + jnp.dot(gelu_output, down_matrix, preferred_element_type=jnp.float32)
        + bias_f[3 * D + FF : 4 * D + FF]
    )
    record = (
        summed_in,
        normed_one,
        queries,
        keys_loc,
        values_loc,
        attn_out,
        log_tot,
        after_attn,
        second_normalized,
        upward,
        gelu_output,
        keys_all,
        values_all,
    )
    return (result, record)


def backward_layer(hidden_state_gradient, fetched, record, onehot, kv_pair):
    mat_qkv = fetched[0]
    mat_out = fetched[1]
    up_matrix = fetched[2]
    down_matrix = fetched[3]
    gain_f = fetched[4].astype(jnp.float32)
    bias_f = fetched[5].astype(jnp.float32)
    summed_in, normed_one, queries = (record[0], record[1], record[2])
    attn_out, log_tot, after_attn = (record[5], record[6], record[7])
    second_normalized, upward, gelu_output = (record[8], record[9], record[10])
    keys_all, values_all = kv_pair
    gradient_bfloat = hidden_state_gradient.astype(jnp.bfloat16)
    down_weight_gradient = jnp.einsum(
        "awt,awg->tg", gelu_output, gradient_bfloat, preferred_element_type=jnp.float32
    )
    bias_down = jnp.sum(hidden_state_gradient, axis=(0, 1))
    activation_gradient = jnp.einsum(
        "ngb,rb->ngr", gradient_bfloat, down_matrix, preferred_element_type=jnp.float32
    )
    _, gelu_back = jax.vjp(jax.nn.gelu, upward)
    grad_upward = gelu_back(activation_gradient)[0]
    bias_up = jnp.sum(grad_upward, axis=(0, 1))
    upward_bfloat = grad_upward.astype(jnp.bfloat16)
    up_weight_gradient = jnp.einsum(
        "xew,xem->wm", second_normalized, upward_bfloat, preferred_element_type=jnp.float32
    )
    second_norm_gradient = jnp.einsum(
        "iyv,tv->iyt", upward_bfloat, up_matrix, preferred_element_type=jnp.float32
    )
    _, second_back = jax.vjp(layer_norm, after_attn, gain_f[D:], bias_f[5 * D + FF :])
    from_second, gain_two, shift_two = second_back(second_norm_gradient)
    grad_mid = hidden_state_gradient + from_second
    mid_bf = grad_mid.astype(jnp.bfloat16)
    grad_out = jnp.einsum("lsc,lsd->cd", attn_out, mid_bf, preferred_element_type=jnp.float32)
    bias_out = jnp.sum(grad_mid, axis=(0, 1))
    grad_attn = jnp.einsum(
        "lsd,cd->lsc", mid_bf, mat_out, preferred_element_type=jnp.float32
    ).astype(jnp.bfloat16)
    grad_query, part_key, part_value = attend_back(
        queries, keys_all, values_all, log_tot, grad_attn
    )
    grad_key, grad_value = (
        lax.psum_scatter(
            part_key.astype(jnp.bfloat16), "seq", scatter_dimension=0, tiled=True
        ).astype(jnp.float32),
        lax.psum_scatter(
            part_value.astype(jnp.bfloat16), "seq", scatter_dimension=0, tiled=True
        ).astype(jnp.float32),
    )
    bias_query = jnp.sum(grad_query, axis=(0, 1))
    bias_value = jnp.sum(grad_value, axis=(0, 1))
    grad_linear = jnp.concatenate([grad_query, grad_key, grad_value], axis=-1).astype(jnp.bfloat16)
    grad_qkv = jnp.einsum(
        "lsc,lse->ce", normed_one, grad_linear, preferred_element_type=jnp.float32
    )
    grad_norm_one = jnp.einsum(
        "lse,ce->lsc", grad_linear, mat_qkv, preferred_element_type=jnp.float32
    )
    _, first_back = jax.vjp(layer_norm, summed_in, gain_f[:D], bias_f[4 * D + FF : 5 * D + FF])
    from_first, gain_one, shift_one = first_back(grad_norm_one)
    grad_in = grad_mid + from_first
    grad_table = jnp.dot(onehot.T, jnp.sum(grad_in, axis=0), precision=HIGH)
    grad_gain = jnp.concatenate([gain_one, gain_two])
    grad_bias = jnp.concatenate(
        [bias_query, bias_value, bias_out, bias_up, bias_down, shift_one, shift_two]
    )
    return (
        grad_in,
        (
            grad_qkv,
            grad_out,
            up_weight_gradient,
            down_weight_gradient,
            grad_gain,
            grad_bias,
            grad_table,
        ),
    )


def body(
    inputs,
    cotangent,
    w_qkv,
    w_out,
    w_up,
    w_down,
    norm_gains,
    biases,
    time_table,
    timesteps,
    importance,
):
    onehot = (timesteps[:, None] == jnp.arange(STEPS, dtype=jnp.int32)[None, :]).astype(jnp.float32)
    seq_weight = jnp.dot(onehot, importance, precision=HIGH)
    hidden = inputs.astype(jnp.float32)
    records = []
    fetched_all = []
    for layer_id in range(LAYERS):
        fetched = (
            lax.all_gather(w_qkv[layer_id], ("dp", "seq"), axis=0, tiled=True),
            lax.all_gather(w_out[layer_id], ("dp", "seq"), axis=0, tiled=True),
            lax.all_gather(w_up[layer_id], ("dp", "seq"), axis=0, tiled=True),
            lax.all_gather(w_down[layer_id], ("dp", "seq"), axis=0, tiled=True),
            lax.all_gather(norm_gains[layer_id], ("dp", "seq"), axis=0, tiled=True),
            lax.all_gather(biases[layer_id], ("dp", "seq"), axis=0, tiled=True),
            lax.all_gather(time_table[layer_id], ("dp", "seq"), axis=1, tiled=True),
        )
        hidden, record = forward_layer(hidden, fetched, onehot)
        records.append(record)
        fetched_all.append(fetched)
    hidden_state_gradient = cotangent.astype(jnp.float32) * seq_weight[None, :, None]
    shards = [None] * LAYERS
    for layer_id in reversed(range(LAYERS)):
        record = records[layer_id]
        fetched = (
            lax.all_gather(w_qkv[layer_id], ("dp", "seq"), axis=0, tiled=True),
            lax.all_gather(w_out[layer_id], ("dp", "seq"), axis=0, tiled=True),
            lax.all_gather(w_up[layer_id], ("dp", "seq"), axis=0, tiled=True),
            lax.all_gather(w_down[layer_id], ("dp", "seq"), axis=0, tiled=True),
            lax.all_gather(norm_gains[layer_id], ("dp", "seq"), axis=0, tiled=True),
            lax.all_gather(biases[layer_id], ("dp", "seq"), axis=0, tiled=True),
            lax.all_gather(time_table[layer_id], ("dp", "seq"), axis=1, tiled=True),
        )
        kv_pair = (
            lax.all_gather(record[3], "seq", axis=0, tiled=True),
            lax.all_gather(record[4], "seq", axis=0, tiled=True),
        )
        hidden_state_gradient, grads = backward_layer(
            hidden_state_gradient, fetched, record, onehot, kv_pair
        )
        shards[layer_id] = (
            lax.psum_scatter(grads[0], ("dp", "seq"), scatter_dimension=0, tiled=True),
            lax.psum_scatter(grads[1], ("dp", "seq"), scatter_dimension=0, tiled=True),
            lax.psum_scatter(grads[2], ("dp", "seq"), scatter_dimension=0, tiled=True),
            lax.psum_scatter(grads[3], ("dp", "seq"), scatter_dimension=0, tiled=True),
            lax.psum_scatter(grads[4], ("dp", "seq"), scatter_dimension=0, tiled=True),
            lax.psum_scatter(grads[5], ("dp", "seq"), scatter_dimension=0, tiled=True),
            lax.psum_scatter(grads[6], ("dp", "seq"), scatter_dimension=1, tiled=True),
        )
    stacked = [
        jnp.stack([shards[layer_id][member] for layer_id in range(LAYERS)]) for member in range(7)
    ]
    return (
        hidden,
        hidden_state_gradient,
        stacked[0],
        stacked[1],
        stacked[2],
        stacked[3],
        stacked[4],
        stacked[5],
        stacked[6],
    )


MESH_ID = pl.DeviceIdType.MESH
LOG2E = 1.4426950408889634
F32 = jnp.float32
BF = jnp.bfloat16
TILE = 256
PAIRS = HEADS // 2
N_SEMS = 256
GELU_A = math.sqrt(2.0 / math.pi)
GELU_B = 0.044715

B_Q, B_V, B_O, B_U, B_D, B_S1, B_S2 = 0, D, 2 * D, 3 * D, 3 * D + FF, 4 * D + FF, 5 * D + FF


def nn(left, right):
    return jnp.dot(left, right, preferred_element_type=F32)


def nt(left, right, precision=None):
    return lax.dot_general(left, right, (((1,), (1,)), ((), ())), preferred_element_type=F32, precision=precision)


def tn(left, right):
    return lax.dot_general(left, right, (((0,), (0,)), ((), ())), preferred_element_type=F32)


def rows_sum(value):
    return jnp.sum(value, axis=0, keepdims=True)


def ln_parts(value):
    centered = value - jnp.mean(value, axis=-1, keepdims=True)
    scale = lax.rsqrt(jnp.mean(centered * centered, axis=-1, keepdims=True) + EPS)
    return centered * scale, scale


def gelu_parts(up):
    square = up * up
    tanh = jnp.tanh(GELU_A * up * (1.0 + GELU_B * square))
    return square, tanh


class Fused:
    def __init__(self, n_z, refs):
        (self.ts, self.imp, self.xin, self.cot, self.wq_i, self.wo_i, self.wu_i, self.wd_i, self.gains_i, self.biases_i, self.tab,
         self.act_o, self.gin_o, self.gq_o, self.go_o, self.gu_o, self.gd_o, self.gg_o, self.gb_o, self.gt_o,
         self.Wq, self.Wo, self.Wu, self.Wd, self.SM, self.TS, self.TT, self.T24, self.TR, self.BV, self.GV, self.BG, self.GG,
         self.TG, self.X, self.N, self.NT, self.Q, self.KV, self.AO, self.LSE, self.DL, self.Y, self.GB, self.DO, self.G,
         self.GN, self.GL, self.ACC, self.OWN, self.PB, self.RB1, self.RB2, self.RB3,
         self.R1, self.R2, self.R3, self.R4, self.SR, self.SX, self.SY,
         self.ssem, self.rsem, self.lsem, self.credit) = refs
        dp, seq = lax.axis_index("dp"), lax.axis_index("seq")
        self.n_z = n_z
        self.dp, self.seq = dp, seq
        self.z, self.x, self.y, self.c = dp // 2, dp % 2, seq // 2, seq % 2
        self.next_sem = 0
        self.next_local = 0
        self.mine = {"z": self.z, "x": self.x, "y": self.y, "c": self.c}
        self.other = {"x": 1 - self.x, "y": 1 - self.y, "c": 1 - self.c}
        self.around = [(self.z + hop) % n_z for hop in range(n_z)]
        n_dp = 2 * n_z
        self.far_z = {hop: (dp + hop) % n_dp // 2 for hop in range(1, n_dp)}
        self.far_x = {hop: (dp + hop) % n_dp % 2 for hop in range(1, n_dp)}
        other_x, other_y = self.z * 2 + self.other["x"], self.other["y"] * 2 + self.c
        self.device = {
            **{("z", hop): (self.around[hop] * 2 + self.x, seq) for hop in range(1, n_z)},
            ("x", 1): (other_x, seq),
            ("y", 1): (dp, other_y),
            ("c", 1): (dp, self.y * 2 + self.other["c"]),
            ("p", 1): (other_x, seq),
            ("p", 2): (dp, other_y),
            ("p", 3): (other_x, other_y),
            **{("d", hop): ((dp + hop) % n_dp, seq) for hop in range(1, n_dp)},
            **{("s", hop): (dp, (seq + hop) % 4) for hop in range(1, 4)},
        }
        self.device = {key: {"dp": there[0], "seq": there[1]} for key, there in self.device.items()}

    def hops(self, dim):
        return [hop for name, hop in self.device if name == dim]

    def enter(self):
        barrier = pltpu.get_barrier_semaphore()
        who = [key for key in self.device if key[0] in "ds"] + [("p", 3)]
        for key in who:
            pl.semaphore_signal(barrier, inc=1, device_id=self.device[key], device_id_type=MESH_ID)
        pl.semaphore_wait(barrier, len(who))

    def remote(self, src, dst, dim, hop=1, number=None):
        if number is None:
            number = self.next_sem
            self.next_sem += 1
        return pltpu.make_async_remote_copy(
            src, dst, self.ssem.at[number], self.rsem.at[number], device_id=self.device[dim, hop], device_id_type=MESH_ID
        )

    def local(self, src, dst):
        number = self.next_local
        self.next_local += 1
        return pltpu.make_async_copy(src, dst, self.lsem.at[number])


class Gather:
    def __init__(self, me, view, order):
        self.copies = []
        done = ""
        for dim in order:
            block = view(*[slice(None) if other in done else me.mine[other] for other in "zxyc"])
            self.copies.append([me.remote(block, block, dim, hop) for hop in me.hops(dim)])
            done += "xy" if dim == "p" else dim

    def start(self, stage):
        if stage:
            self.arrive(stage - 1)
        for copy in self.copies[stage]:
            copy.start()

    def arrive(self, stage=-1):
        for copy in self.copies[stage]:
            copy.wait_recv()

    def drain(self):
        for copies in self.copies:
            for copy in copies:
                copy.wait_send()


class Single:
    def __init__(self, copy):
        self.copy = copy

    def start(self, stage):
        self.copy.start()


class Reduce:
    def __init__(self, me, layer, grad, recv, out, cols, order, number, before):
        self.me, self.layer, self.grad, self.recv, self.out, self.cols, self.order = me, layer, grad, recv, out, cols, order
        self.number, self.before = number, before
        self.first_sem = before.first_sem if before else me.next_sem
        self.last = len(order) - 1
        self.copies = [self.build(stage) for stage in range(len(order))]

    def block(self, fixed):
        return tuple(fixed.get(dim, slice(None)) for dim in "zxyc")

    def kept(self, stage):
        done = "".join("xy" if dim == "p" else dim for dim in self.order[:stage])
        return {dim: self.me.mine[dim] for dim in done}

    def build(self, stage):
        me, dim = self.me, self.order[stage]
        copies = []
        number = self.first_sem + sum(len(me.hops(before)) for before in self.order[:stage])
        for hop in me.hops(dim):
            fixed = self.kept(stage)
            if dim == "z":
                fixed["z"] = me.around[hop]
            elif dim == "p":
                fixed["x"] = me.mine["x"] if hop == 2 else me.other["x"]
                fixed["y"] = me.mine["y"] if hop == 1 else me.other["y"]
            else:
                fixed[dim] = me.other[dim]
            src = self.grad.at[(self.layer, *self.block(fixed), slice(None), self.cols)]
            dst = self.landed(stage, hop).at[(*self.landing(stage, hop), slice(None), self.cols)]
            copies.append(me.remote(src, dst, dim, hop, number + len(copies) if self.before else None))
        return copies

    def landed(self, stage, hop):
        return self.recv[3] if stage == self.last else self.recv[stage]

    def landing(self, stage, hop):
        dim = self.order[stage]
        if stage == self.last:
            return (hop - 1,)
        if dim == "p":
            return (slice(None), hop - 1)
        if dim == "z":
            return (slice(2 * hop - 2, 2 * hop),)
        return ((slice(0, self.me.n_z), slice(None), slice(None)), (slice(None), slice(0, 2)), (slice(0, self.me.n_z),))[stage]

    def start(self, stage):
        me = self.me
        if stage:
            self.add(stage - 1)
            dim = self.order[stage - 1]
            if self.layer == LAYERS - 1:
                for hop in me.hops(dim):
                    pl.semaphore_signal(
                        me.credit.at[self.number, stage - 1], inc=1, device_id=me.device[dim, hop], device_id_type=MESH_ID
                    )
        if stage <= self.last:
            if self.layer < LAYERS - 1:
                pl.semaphore_wait(me.credit.at[self.number, stage], len(me.hops(self.order[stage])))
                for copy in self.before.copies[stage]:
                    copy.wait_send()
            for copy in self.copies[stage]:
                copy.start()

    def add(self, stage):
        me, dim = self.me, self.order[stage]
        for copy in self.copies[stage]:
            copy.wait_recv()
        fixed = self.kept(stage + 1)
        if stage == self.last or dim in "zp":
            where = (self.layer, *self.block(fixed), slice(None), self.cols)
            total = self.grad[where].astype(F32)
            for hop in me.hops(dim):
                total = total + self.landed(stage, hop)[(*self.landing(stage, hop), slice(None), self.cols)].astype(F32)
            if stage == self.last:
                self.out[self.layer, :, self.cols] = total
            else:
                self.grad[where] = total.astype(BF)
            return

        def one(z, carry):
            where = (self.layer, *self.block({**fixed, "z": z}), slice(None), self.cols)
            came = (z, *self.landing(stage, 1)[1:], slice(None), self.cols)
            self.grad[where] = self.grad[where] + self.recv[stage][came]
            return carry

        lax.fori_loop(0, me.n_z, one, 0)

    def drain(self):
        for copies in self.copies:
            for copy in copies:
                copy.wait_send()


def at_step(index, hooks):
    for when, action in hooks:
        pl.when(index == when)(action)


BACKWARD_AT = (21, 0)
END_AT = 42
GATHER = (
    ("yzxc", 0, 2, 3, 4),
    ("zpc", 0, 2, 4),
    ("zpc", 0, 3, 6),
    ("yzxc", 0, 2, 3, 6),
    ("pzc", 2, 4, 14),
    ("zpc", 1, 5, 10),
    ("zpc", 2, 7, 14),
    ("zpc", 2, 9, 18),
    ("zpc", 0, 3, 11),
    ("pzc", 1, 3, 12),
    ("zpc", 3, 16, 21),
    ("zpc", 6, 17, 21),
    ("zpc", 2, 20, 32),
    ("zpc", 7, 22, 32),
    ("yzxc", 2, 8, 21, 32),
    ("pzc", 1, 10, 28),
    ("pzc", 17, 22, 33),
    ("zpc", 8, 23, 32),
    ("zpc", 0, 2, 5),
    ("y", 0),
    ("y", 23),
)
REDUCE = (
    ("cxzy", 9, 11, 15, 28, 43),
    ("cxyz", 9, 12, 21, 35, 41),
    ("cpz", 2, 5, 12, 15),
    ("cpz", 4, 7, 13, 32),
    ("cpz", 6, 14, 24, 37),
    ("cpz", 7, 15, 29, 34),
    ("cpz", 15, 20, 29, 40),
    ("cpz", 15, 15, 32, 40),
    ("cpz", 17, 22, 33, 40),
    ("cpz", 18, 21, 33, 36),
    ("cxzy", 28, 30, 36, 44, 44),
    ("cxyz", 29, 32, 36, 42, 44),
    ("cpz", 23, 24, 33, 44),
    ("cpz", 25, 27, 33, 43),
    ("cpz", 27, 30, 41, 45),
    ("cpz", 28, 30, 39, 42),
    ("cpz", 36, 38, 42, 46),
    ("cpz", 36, 36, 41, 42),
    ("cpz", 38, 38, 42, 44),
    ("cpz", 38, 40, 43, 46),
    ("y", 41),
)

SMALL = "small"


def pieces(name, layer):
    return 4 if name == "q" and layer == 0 else 2


def by_place(moves, plan):
    timeline = {}
    for move, (_, *places) in zip(moves, plan, strict=True):
        for stage, place in enumerate(places):
            timeline.setdefault(place, []).append((move, stage))
    return timeline


def fused_kernel(n_z, *refs):
    me = Fused(n_z, refs)
    x, y, z, c = me.x, me.y, me.z, me.c
    n_dp = 2 * n_z
    spare = slice(None)

    mats = ((me.wq_i, me.Wq), (me.wo_i, me.Wo), (me.wu_i, me.Wu), (me.wd_i, me.Wd))
    loads = [me.local(src.at[layer], dst.at[layer, z, x, y, c]) for layer in range(LAYERS) for src, dst in mats]
    for load in loads:
        load.start()
    own_tokens = [
        me.local(src.at[seq], dst.at[tile]) for src, dst in ((me.xin, me.DO), (me.cot, me.GB)) for seq, tile in ((y, 0), (2, 2))
    ]
    for load in own_tokens:
        load.start()

    row = lax.broadcasted_iota(jnp.int32, (32, 128), 0)
    steps = jnp.zeros((32, 128), jnp.int32)
    for j in range(3):
        steps = jnp.where(row == 3 * me.dp + j, me.ts[j], steps)
    me.TT[z, x] = steps

    def choose(rows, cols, first):
        here = lax.broadcasted_iota(jnp.int32, (rows, cols), 1) == first + lax.broadcasted_iota(jnp.int32, (rows, cols), 0)
        return here.astype(F32)

    own_biases, own_gains = choose(160, 640, 160 * me.seq), choose(32, 128, 32 * me.seq)
    own_lanes = choose(16, 128, 16 * (4 * x + me.seq))
    spread_b = nn(me.biases_i[...].astype(F32), own_biases)
    spread_g = nn(me.gains_i[...].astype(F32), own_gains)
    rows = []
    for layer in range(LAYERS):
        rows += [spread_b[layer : layer + 1, 128 * r : 128 * r + 128] for r in range(5)] + [spread_g[layer : layer + 1]]
    me.SM[z, x, y, c] = jnp.concatenate(rows + [jnp.zeros((16 - 6 * LAYERS, 128), F32)], axis=0).astype(BF)
    me.BG[...] = jnp.zeros_like(me.BG)
    me.GG[...] = jnp.zeros_like(me.GG)

    me.enter()
    for load in loads:
        load.wait()

    def weight(layer, ref, order, cols):
        return Gather(me, lambda *where: ref.at[(layer, *where, spare, cols)], order)

    grads = {"q": me.Wq, "o": me.Wo, "u": me.Wu, "d": me.Wd}

    steps_all = Gather(me, lambda gz, gx, gy, gc: me.TT.at[gz, gx], "d")
    times = Gather(me, lambda *where: me.TS.at[where], "zpc")
    token_in = me.remote(me.xin.at[me.other["y"]], me.DO.at[1], "y")
    cot_in = me.remote(me.cot.at[me.other["y"]], me.GB.at[1], "y")
    moves = {}
    plan = iter(GATHER)
    for layer in range(LAYERS):
        for name, ref in grads.items():
            width = ref.shape[-1] // pieces(name, layer)
            for part in range(pieces(name, layer)):
                moves[name, part, layer] = weight(layer, ref, next(plan)[0], slice(width * part, width * (part + 1)))
    moves[SMALL] = small = Gather(me, lambda *where: me.SM.at[where], next(plan)[0])
    timeline = by_place([*moves.values(), Single(token_in), Single(cot_in)], GATHER)

    def have(names, layer):
        for name in names:
            for part in range(pieces(name, layer)):
                moves[name, part, layer].arrive()

    def fire(place):
        for move, stage in timeline.get(place, ()):
            move.start(stage)

    def fires(first, count):
        return [(i, functools.partial(fire, first + i)) for i in range(count) if first + i in timeline]

    steps_all.start(0)
    fire(0)
    fire(1)
    steps_all.arrive()
    t24 = jnp.sum(me.TT[...].reshape(n_dp, 32, 128), axis=0)
    me.T24[...] = t24
    hot = (t24[:, 0:1] == lax.broadcasted_iota(jnp.int32, (32, STEPS), 1)).astype(F32).astype(BF)
    picked = jnp.concatenate([nt(hot, me.tab[layer])[:24] for layer in range(LAYERS)], axis=0).astype(BF)
    me.TS[z, x, y, c] = nn(picked, own_lanes.astype(BF)).astype(BF)
    times.start(0)
    fire(2)
    times.start(1)
    fire(3)
    times.start(2)
    fire(4)
    fire(5)

    small.arrive()
    for gz in range(n_z):
        for gx in range(2):
            block = jnp.sum(me.SM[gz, gx].reshape(4, 16, 128).astype(F32), axis=0)
            dp = 2 * gz + gx
            for layer in range(LAYERS):
                for r in range(5):
                    at = (5 * dp + r) * 128
                    me.BV[layer, :, at : at + 128] = block[6 * layer + r : 6 * layer + r + 1]
                me.GV[layer, :, 128 * dp : 128 * dp + 128] = block[6 * layer + 5 : 6 * layer + 6]
    times.arrive()
    slabs = jnp.concatenate(
        [jnp.sum(me.TS[gz].reshape(8, 48, 128).astype(F32), axis=0) for gz in range(n_z)], axis=1
    ).astype(BF)
    r8 = lax.broadcasted_iota(jnp.int32, (16, 48), 0)
    c48 = lax.broadcasted_iota(jnp.int32, (16, 48), 1)
    for layer in range(LAYERS):
        base = 24 * layer + 3 * me.dp
        pick = ((r8 == 0) & (c48 == base + y)) | ((r8 == 1) & (c48 == base + 2))
        me.TR[layer] = nn(pick.astype(F32).astype(BF), slabs)[:8]

    def time_row(layer, tile):
        return me.TR[layer, 1:2, :] if tile == 2 else me.TR[layer, 0:1, :]

    def bias(layer, at, width=D):
        return me.BV[layer, :, at : at + width]

    for load in own_tokens:
        load.wait()
    for tile in (0, 2):
        me.X[0, tile] = me.DO[tile].astype(F32) + time_row(0, tile)

    sends = [token_in, cot_in]

    def send(src, dst, dim):
        copy = me.remote(src, dst, dim)
        sends.append(copy)
        return copy

    def attention_norm(layer, tile):
        hat, _ = ln_parts(me.X[layer, tile])
        return (hat * me.GV[layer, :, :D] + bias(layer, B_S1)).astype(BF)

    def columns(layer, normed, j):
        return nn(normed, me.Wq[layer, :, :, :, :, :, D * j : D * j + D].reshape(D, D))

    def keys_values(layer, normed, slot):
        me.KV[layer, 0, slot] = columns(layer, normed, 1).astype(BF)
        me.KV[layer, 1, slot] = (columns(layer, normed, 2) + bias(layer, B_V)).astype(BF)

    low_lanes = lax.broadcasted_iota(jnp.int32, (TILE, 128), 1) < HEAD_DIM

    def two_heads(pair):
        zero = jnp.zeros_like(pair)
        return jnp.concatenate([jnp.where(low_lanes, pair, zero), jnp.where(low_lanes, zero, pair)], axis=0)

    def attend_two(layer, step):
        tile, base = step // 2, step // 4 * 4
        first = step % 2 * 2
        cols = [pl.ds(pl.multiple_of((first + i) * 128, 128), 128) for i in range(2)]
        queries = [two_heads(me.Q[layer, tile, :, cols[i]]) for i in range(2)]

        def block(which, part, i):
            return me.KV[layer, which, pl.ds(base + 2 * part, 2), :, cols[i]].reshape(2 * TILE, 128)

        def scores(part, i):
            return nt(block(0, part, i), queries[i])

        def highest(parts):
            tops = [jnp.max(part, axis=0, keepdims=True) for part in parts]
            return jnp.maximum(tops[0], tops[1]) * LOG2E

        def mix(score, top, part, i):
            values = jnp.concatenate([block(1, part, i).T, jnp.ones((16, 2 * TILE), BF)], axis=0)
            return nn(values, jnp.exp2(score * LOG2E - top).astype(BF))

        def finish(mixed, top, i):
            total = mixed[128:129]
            mixed = mixed[:128] * (1.0 / total)
            me.LSE[layer, tile, first + i] = top + jnp.log2(total)
            out = jnp.concatenate([mixed[:HEAD_DIM, :TILE], mixed[HEAD_DIM:, TILE:]], axis=0)
            me.AO[layer, tile, :, cols[i]] = out.T.astype(BF)

        now = [scores(0, 0), scores(1, 0)]
        top = highest(now)
        later, mixed = [], 0.0
        for part in range(2):
            later.append(scores(part, 1))
            mixed = mixed + mix(now[part], top, part, 0)
        finish(mixed, top, 0)
        top = highest(later)
        finish(mix(later[0], top, 0, 1) + mix(later[1], top, 1, 1), top, 1)

    kv = me.KV
    to_y = [me.remote(me.N.at[2], me.PB.at[0, layer], "y") for layer in range(LAYERS)]
    on_c = [send(kv.at[layer, :, 5], kv.at[layer, :, 7], "c") for layer in range(LAYERS)]
    to_c = [
        [send(kv.at[layer, :, a], kv.at[layer, :, b], "c") for a, b in ((0, 2), (1, 3), (4, 6))] for layer in range(LAYERS)
    ]

    def announce(layer):
        me.N[2] = attention_norm(layer, 2)
        to_y[layer].start()

    def project(layer, tile):
        normed = me.N[2] if tile == 2 else attention_norm(layer, tile)
        keys_values(layer, normed, 4 if tile == 2 else tile)
        to_c[layer][tile].start()
        queries = (columns(layer, normed, 0) + bias(layer, B_Q)).astype(BF)
        me.Q[layer, tile] = queries * jnp.asarray(1.0 / math.sqrt(HEAD_DIM), BF)

    def neighbour(layer):
        to_y[layer].wait_recv()
        keys_values(layer, me.PB[0, layer], 5)
        on_c[layer].start()

    def attention(layer, first, last, place):
        def step(index, carry):
            at_step(index - first, fires(place, last - first))
            attend_two(layer, index)
            return carry

        lax.fori_loop(first, last, step, 0)

    def rest(layer, tiles, place):
        if tiles[0] == 0:
            have("o", layer)
        fire(place)
        w_out = me.Wo[layer].reshape(D, D)
        for tile in tiles:
            after = me.X[layer, tile] + nn(me.AO[layer, tile], w_out) + bias(layer, B_O)
            me.Y[layer, tile] = after
            hat, _ = ln_parts(after)
            me.N[tile] = (hat * me.GV[layer, :, D:] + bias(layer, B_S2)).astype(BF)
            me.GN[tile] = after + bias(layer, B_D)
        if tiles[0] == 0:
            have("ud", layer)

        def ffn(half, carry):
            at_step(half, fires(place + 1, 2))
            cols = pl.ds(pl.multiple_of(half * (FF // 2), FF // 2), FF // 2)
            w_up = me.Wu[layer, :, :, :, :, :, cols].reshape(D, FF // 2)
            w_down = me.Wd[layer, pl.ds(half * (n_z // 2), n_z // 2)].reshape(FF // 2, D)
            b_up = me.BV[layer, :, pl.ds(pl.multiple_of(B_U + half * (FF // 2), D), FF // 2)]
            for tile in tiles:
                up = nn(me.N[tile], w_up) + b_up
                _, tanh = gelu_parts(up)
                me.GN[tile] += nn((0.5 * up * (1.0 + tanh)).astype(BF), w_down)
            return carry

        lax.fori_loop(0, 2, ffn, 0)

    def third_keys(layer):
        to_y[layer].wait_send()
        to_c[layer][2].wait_recv()
        on_c[layer].wait_recv()

    announce(0)
    fire(6)
    have("q", 0)
    project(0, 2)
    fire(7)
    project(0, 0)
    fire(8)
    token_in.wait_recv()
    me.X[0, 1] = me.DO[1].astype(F32) + time_row(0, 1)
    project(0, 1)
    fire(9)
    neighbour(0)
    to_c[0][0].wait_recv()
    to_c[0][1].wait_recv()
    for layer in range(LAYERS):
        at = (10, 25)[layer]
        attention(layer, 0, 4, at)
        fire(at + 4)
        if layer:
            neighbour(layer)
        fire(at + 5)
        third_keys(layer)
        attention(layer, 4, 6, at + 6)
        rest(layer, (0, 1, 2), at + 8)
        if layer == 0:
            for tile in range(3):
                me.X[1, tile] = me.GN[tile] + time_row(1, tile)
            announce(1)
            fire(21)
            have("q", 1)
            for turn, tile in enumerate((2, 0, 1)):
                project(1, tile)
                fire(22 + turn)
            to_c[1][0].wait_recv()
            to_c[1][1].wait_recv()
    act_out = [
        me.local(me.DO.at[0], me.act_o.at[y]), me.remote(me.DO.at[1], me.act_o.at[y], "y"), me.local(me.DO.at[2], me.act_o.at[2])
    ]
    for tile in range(3):
        me.DO[tile] = me.GN[tile].astype(BF)
    for copy in act_out:
        copy.start()

    cot_in.wait_recv()
    weight_y, weight_2 = me.imp[me.ts[y]], me.imp[me.ts[2]]
    for tile in range(3):
        grad = me.GB[tile].astype(F32) * (weight_2 if tile == 2 else weight_y)
        me.G[tile] = grad
    for part in [steps_all, times, *moves.values()]:
        part.drain()
    for copy in sends:
        copy.wait_send()
    sends.clear()

    outs = {"q": me.gq_o, "o": me.go_o, "u": me.gu_o, "d": me.gd_o}
    recvs = {
        name: [me.R1[i], me.R2[i], me.R3[i], me.R4[i]] for i, name in enumerate("qoud")
    }

    spans = {
        "d": ("d", 0, D), "u": ("u", 0, FF), "o": ("o", 0, D), "p": ("q", 0, D), "q": ("q", D, 3 * D)
    }

    plan = iter(REDUCE)

    def piece(layer, number, name, half):
        kind, begin, end = spans[name]
        width = (end - begin) // 2
        start = begin + width * half
        before = sums[number] if layer < LAYERS - 1 else None
        cols = slice(start, start + width)
        return Reduce(me, layer, grads[kind], recvs[kind], outs[kind], cols, next(plan)[0], number, before)

    def add_bias(layer, at, value):
        me.BG[layer, :, at : at + value.shape[-1]] += value

    def ln_back(layer, gain_at, shift_at, source, grad):
        hat, scale = ln_parts(source)
        me.GG[layer, :, gain_at : gain_at + D] += rows_sum(grad * hat)
        add_bias(layer, shift_at, rows_sum(grad))
        inner = grad * me.GV[layer, :, gain_at : gain_at + D]
        return scale * (inner - jnp.mean(inner, axis=-1, keepdims=True) - hat * jnp.mean(inner * hat, axis=-1, keepdims=True))

    def normed_t(layer, source, gain_at, shift_at):
        for tile in range(3):
            hat, _ = ln_parts(source[layer, tile])
            normed = (hat * me.GV[layer, :, gain_at : gain_at + D] + bias(layer, shift_at)).astype(BF)
            me.N[tile] = normed
            me.NT[:, TILE * tile : TILE * tile + TILE] = normed.T

    head_of = lax.broadcasted_iota(jnp.int32, (HEADS, D), 1) // HEAD_DIM
    selector = (head_of == lax.broadcasted_iota(jnp.int32, (HEADS, D), 0)).astype(F32)

    def backward(layer, before_out, tail):
        base = BACKWARD_AT[layer]
        normed_t(layer, me.Y, D, B_S2)
        for tile in range(3):
            me.GB[tile] = me.G[tile].astype(BF)
            add_bias(layer, B_D, rows_sum(me.G[tile]))
            me.GN[tile] = jnp.zeros((TILE, D), F32)

        def ffn(slab, carry):
            at_step(slab, fires(base, n_z))
            cols = pl.ds(pl.multiple_of(slab * D, D), D)
            b_cols = pl.ds(pl.multiple_of(B_U + slab * D, D), D)
            w_up = me.Wu[layer, :, :, :, :, :, cols].reshape(D, D)
            w_down = me.Wd[layer, slab].reshape(D, D)
            grads_h = me.GB[...].reshape(3 * TILE, D)
            up = nn(me.N[...].reshape(3 * TILE, D), w_up) + me.BV[layer, :, b_cols]
            square, tanh = gelu_parts(up)
            active = (0.5 * up * (1.0 + tanh)).astype(BF)
            slope = 0.5 * (1.0 + tanh) + (0.5 * GELU_A) * up * (1.0 - tanh * tanh) * (1.0 + 3.0 * GELU_B * square)
            grad_up = nt(grads_h, w_down) * slope
            me.BG[layer, :, b_cols] += rows_sum(grad_up)
            grad_up = grad_up.astype(BF)
            me.GN[...] += nt(grad_up, w_up).reshape(3, TILE, D)
            me.Wd[layer, slab] = tn(active, grads_h).astype(BF).reshape(2, 2, 2, 64, D)
            me.Wu[layer, :, :, :, :, :, cols] = nn(me.NT[...], grad_up).astype(BF).reshape(n_z, 2, 2, 2, 16, D)
            return carry

        lax.fori_loop(0, n_z, ffn, 0)
        fire(base + 4)
        for tile in range(3):
            mid = me.G[tile] + ln_back(layer, D, B_S2, me.Y[layer, tile], me.GN[tile])
            me.G[tile] = mid
            add_bias(layer, B_O, rows_sum(mid))
            me.GB[tile] = mid.astype(BF)
        fire(base + 5)
        before_out()
        w_out = me.Wo[layer].reshape(D, D)
        for tile in range(3):
            grad_attn = nt(me.GB[tile], w_out).astype(BF)
            me.DO[tile] = grad_attn
            delta = nt(selector, grad_attn.astype(F32) * me.AO[layer, tile].astype(F32), lax.Precision.HIGHEST)
            for pair in range(PAIRS):
                both = jnp.concatenate([delta[2 * pair : 2 * pair + 1], delta[2 * pair + 1 : 2 * pair + 2]], axis=1)
                me.DL[tile, pair] = both
        d_out = tn(me.AO[layer].reshape(3 * TILE, D), me.GB[...].reshape(3 * TILE, D))
        me.Wo[layer] = d_out.astype(BF).reshape(n_z, 2, 2, 2, 16, D)
        fire(base + 6)

        me.ACC[...] = jnp.zeros_like(me.ACC)
        third_c = send(me.PB, me.RB1, "c")
        third_y = me.remote(me.GL.at[2, :, D:], me.RB2, "y")
        from_c = me.remote(me.GL.at[0:2, :, D:], me.RB3, "c")

        def third_done():
            me.OWN[...] = me.ACC[:, 0:TILE]
            for i in range(2):
                me.GL[2, :, D * (1 + i) : D * (2 + i)] = me.ACC[i, TILE : 2 * TILE].astype(BF)
            me.PB[...] = me.ACC[:, 2 * TILE :].reshape(2, 2, TILE, D).astype(BF)
            me.ACC[...] = jnp.zeros_like(me.ACC)
            third_c.start()

        def third_on():
            third_c.wait_recv()
            me.OWN[...] += me.RB1[:, 0].astype(F32)
            for i in range(2):
                cols = slice(D * (1 + i), D * (2 + i))
                me.GL[2, :, cols] = me.GL[2, :, cols] + me.RB1[i, 1]
            third_y.start()

        def attend_back(step, carry):
            at_step(step, [(2, third_done), (3, third_on)] + fires(base + 8, 6))
            tile = (step // 2 + 2) % 3
            slot = tile // 2 * 4
            for i in range(2):
                pair = step % 2 * 2 + i
                cols = pl.ds(pl.multiple_of(pair * 128, 128), 128)
                queries, grads_o = two_heads(me.Q[layer, tile, :, cols]), two_heads(me.DO[tile, :, cols])
                log_sum, delta = me.LSE[layer, tile, pair], me.DL[tile, pair]
                d_query = jnp.zeros((128, 2 * TILE), F32)
                for part in range(4):
                    keys, values = me.KV[layer, 0, slot + part, :, cols], me.KV[layer, 1, slot + part, :, cols]
                    rows = slice(TILE * part, TILE * part + TILE)
                    prob = jnp.exp2(nt(keys, queries) * LOG2E - log_sum)
                    grad_s = (prob * (nt(values, grads_o) - delta)).astype(BF)
                    me.ACC[1, rows, cols] += nn(prob.astype(BF), grads_o)
                    me.ACC[0, rows, cols] += nn(grad_s, queries)
                    d_query = d_query + nn(keys.T, grad_s)
                d_query = jnp.concatenate([d_query[:HEAD_DIM, :TILE], d_query[HEAD_DIM:, TILE:]], axis=0).T
                d_query = d_query * (1.0 / math.sqrt(HEAD_DIM))
                me.BG[layer, :, cols] += rows_sum(d_query)
                me.GL[tile, :, cols] = d_query.astype(BF)
            return carry

        fire(base + 7)
        lax.fori_loop(0, 6, attend_back, 0)
        for tile in range(2):
            for i in range(2):
                rows = slice(TILE * (2 + tile), TILE * (3 + tile))
                me.GL[tile, :, D * (1 + i) : D * (2 + i)] = me.ACC[i, rows].astype(BF)
        from_c.start()
        normed_t(layer, me.X, 0, B_S1)
        fire(base + 14)

        def qkv_back(first, last):
            w_qkv = me.Wq[layer, :, :, :, :, :, first:last].reshape(D, last - first)
            part = nt(me.GL[:, :, first:last].reshape(3 * TILE, last - first), w_qkv).reshape(3, TILE, D)
            me.GN[...] = part if first == 0 else me.GN[...] + part
            for j in range(first, last, D):
                d_qkv = nn(me.NT[...], me.GL[:, :, j : j + D].reshape(3 * TILE, D))
                me.Wq[layer, :, :, :, :, :, j : j + D] = d_qkv.astype(BF).reshape(n_z, 2, 2, 2, 16, D)

        qkv_back(0, D)
        fire(base + 15)
        from_c.wait()
        for tile in range(2):
            rows = slice(TILE * tile, TILE * tile + TILE)
            key = me.ACC[0, rows] + me.RB3[tile, :, :D].astype(F32)
            value = me.ACC[1, rows] + me.RB3[tile, :, D:].astype(F32)
            add_bias(layer, B_V, rows_sum(value))
            me.GL[tile, :, D : 2 * D] = key.astype(BF)
            me.GL[tile, :, 2 * D :] = value.astype(BF)
        third_y.wait()
        third = [me.OWN[i] + me.RB2[:, D * i : D * i + D].astype(F32) for i in range(2)]
        me.GL[2, :, D : 2 * D] = third[0].astype(BF)
        me.GL[2, :, 2 * D :] = third[1].astype(BF)
        add_bias(layer, B_V, rows_sum(third[1]))
        fire(base + 16)
        qkv_back(D, 3 * D)
        fire(base + 17)
        totals = []
        for tile in (1, 0, 2):
            grad = me.G[tile] + ln_back(layer, 0, B_S1, me.X[layer, tile], me.GN[tile])
            me.G[tile] = grad
            totals.append(rows_sum(grad))
            tail(tile, grad)
            fire(base + 17 + len(totals))
        me.TG[layer, 0:1] = totals[0] + totals[1]
        me.TG[layer, 1:2] = totals[2]
        for copy in sends:
            copy.wait_send()
        sends.clear()

    sums = []
    for layer in reversed(range(LAYERS)):
        for number, (name, half) in enumerate((name, half) for name in spans for half in range(2)):
            sums.append(piece(layer, number, name, half))
    timeline.clear()
    gin_out = me.remote(me.GB.at[1], me.gin_o.at[y], "y")
    timeline.update(by_place([*sums, Single(gin_out)], REDUCE))

    def act_done():
        for copy in act_out:
            copy.wait()

    backward(1, act_done, lambda tile, grad: None)
    finals = []

    def out_tile(tile, grad):
        me.GB[tile] = grad.astype(BF)
        if tile != 1:
            finals.append(me.local(me.GB.at[tile], me.gin_o.at[y if tile == 0 else 2]))
            finals[-1].start()

    backward(0, lambda: None, out_tile)

    for gz in range(n_z):
        lanes = slice(128 * gz, 128 * gz + 128)
        for gx in range(2):
            dp = 2 * gz + gx
            for layer in range(LAYERS):
                for r in range(5):
                    at_lane = (5 * dp + r) * 128
                    me.SR[gz, gx, 6 * layer + r : 6 * layer + r + 1] = me.BG[layer, :, at_lane : at_lane + 128]
                me.SR[gz, gx, 6 * layer + 5 : 6 * layer + 6] = me.GG[layer, :, 128 * dp : 128 * dp + 128]
                me.SR[gz, gx, 12 + 2 * layer : 14 + 2 * layer] = me.TG[layer, 0:2, lanes]
    to_dp = [
        me.remote(me.SR.at[me.far_z[hop], me.far_x[hop]], me.SX.at[me.dp], "d", hop) for hop in me.hops("d")
    ]
    for copy in to_dp:
        copy.start()
    me.SX[me.dp] = me.SR[z, x]
    fire(END_AT)
    for copy in to_dp:
        copy.wait_recv()
    fire(END_AT + 1)
    me.SY[0, 0:16] = jnp.sum(me.SX[...], axis=0)
    for dp in range(n_dp):
        for layer in range(LAYERS):
            at_row = 16 + 24 * layer + 3 * dp
            first_seq = me.SX[dp, 12 + 2 * layer : 13 + 2 * layer]
            me.SY[0, at_row : at_row + 1] = jnp.where(y == 0, first_seq, 0.0)
            me.SY[0, at_row + 1 : at_row + 2] = jnp.where(y == 1, first_seq, 0.0)
            me.SY[0, at_row + 2 : at_row + 3] = me.SX[dp, 13 + 2 * layer : 14 + 2 * layer]
    to_seq = [me.remote(me.SY.at[0], me.SY.at[hop], "s", hop) for hop in me.hops("s")]
    for copy in to_seq:
        copy.start()
    fire(END_AT + 2)
    for copy in to_seq:
        copy.wait_recv()
    fire(END_AT + 3)
    total = me.SY[0] + me.SY[1] + me.SY[2] + me.SY[3]
    hot = (me.T24[0:24, 0:1] == lax.broadcasted_iota(jnp.int32, (24, STEPS), 1)).astype(F32)
    for layer in range(LAYERS):
        bias_row = jnp.concatenate([total[6 * layer + r : 6 * layer + r + 1] for r in range(5)], axis=1)
        me.gb_o[layer : layer + 1] = nt(bias_row, own_biases, HIGH)
        me.gg_o[layer : layer + 1] = nt(total[6 * layer + 5 : 6 * layer + 6], own_gains, HIGH)
        by_seq = nt(own_lanes, total[16 + 24 * layer : 40 + 24 * layer], HIGH)
        me.gt_o[layer] = jnp.dot(by_seq, hot, precision=HIGH, preferred_element_type=F32)
    fire(END_AT + 4)

    for copy in to_dp + to_seq:
        copy.wait_send()
    for copy in [gin_out, *finals]:
        copy.wait()
    for part in sums[len(sums) // 2 :]:
        part.drain()


def fused_call(n_z, *operands):
    any_space, vmem, smem = (pl.BlockSpec(memory_space=space) for space in (pl.ANY, pltpu.VMEM, pltpu.SMEM))
    cube = (n_z, 2, 2, 2)
    tokens = (3, TILE, D)
    sizes = ((16, 3 * D), (16, D), (16, FF), (64, D))

    def many(lead):
        return [tuple(pltpu.VMEM((*lead, *size), BF) for size in sizes)]

    flat, tree = jax.tree.flatten(
        [pltpu.VMEM((LAYERS, *cube, *size), BF) for size in sizes]
        + [
            pltpu.VMEM((*cube, 16, 128), BF),
            pltpu.VMEM((*cube, 48, 128), BF),
            pltpu.VMEM((n_z, 2, 32, 128), jnp.int32),
            pltpu.VMEM((32, 128), jnp.int32),
            pltpu.VMEM((LAYERS, 8, D), F32),
            pltpu.VMEM((LAYERS, 1, 6 * D + FF), F32),
            pltpu.VMEM((LAYERS, 1, 2 * D), F32),
            pltpu.VMEM((LAYERS, 1, 6 * D + FF), F32),
            pltpu.VMEM((LAYERS, 1, 2 * D), F32),
            pltpu.VMEM((LAYERS, 8, D), F32),
            pltpu.VMEM((LAYERS, *tokens), F32),
            pltpu.VMEM(tokens, BF),
            pltpu.VMEM((D, 3 * TILE), BF),
            pltpu.VMEM((LAYERS, *tokens), BF),
            pltpu.VMEM((LAYERS, 2, 8, TILE, D), BF),
            pltpu.VMEM((LAYERS, *tokens), BF),
            pltpu.VMEM((LAYERS, 3, PAIRS, 1, 2 * TILE), F32),
            pltpu.VMEM((3, PAIRS, 1, 2 * TILE), F32),
            pltpu.VMEM((LAYERS, *tokens), F32),
            pltpu.VMEM(tokens, BF),
            pltpu.VMEM(tokens, BF),
            pltpu.VMEM(tokens, F32),
            pltpu.VMEM(tokens, F32),
            pltpu.VMEM((3, TILE, 3 * D), BF),
            pltpu.VMEM((2, 4 * TILE, D), F32),
            pltpu.VMEM((2, TILE, D), F32),
            pltpu.VMEM((2, 2, TILE, D), BF),
            pltpu.VMEM((2, 2, TILE, D), BF),
            pltpu.VMEM((TILE, 2 * D), BF),
            pltpu.VMEM((2, TILE, 2 * D), BF),
        ]
        + many((n_z, 2, 2))
        + many((n_z, 3))
        + many((2 * n_z - 2,))
        + many((n_z - 1,))
        + [
            pltpu.VMEM((n_z, 2, 16, 128), F32),
            pltpu.VMEM((2 * n_z, 16, 128), F32),
            pltpu.VMEM((4, 64, 128), F32),
            pltpu.SemaphoreType.DMA((N_SEMS,)),
            pltpu.SemaphoreType.DMA((N_SEMS,)),
            pltpu.SemaphoreType.DMA((32,)),
            pltpu.SemaphoreType.REGULAR((10, 4)),
        ]
    )
    outs = [
        jax.ShapeDtypeStruct(tokens, BF),
        jax.ShapeDtypeStruct(tokens, BF),
        *[jax.ShapeDtypeStruct((LAYERS, *size), F32) for size in sizes],
        jax.ShapeDtypeStruct((LAYERS, 32), F32),
        jax.ShapeDtypeStruct((LAYERS, 160), F32),
        jax.ShapeDtypeStruct((LAYERS, 16, STEPS), F32),
    ]

    def run(*refs):
        head = len(operands) + len(outs)
        fused_kernel(n_z, *refs[:head], *jax.tree.unflatten(tree, refs[head:]))

    return pl.pallas_call(
        run,
        out_shape=outs,
        in_specs=[smem, smem] + [any_space] * 6 + [vmem] * 3,
        out_specs=[any_space] * 2 + [vmem] * 7,
        scratch_shapes=flat,
        compiler_params=pltpu.CompilerParams(collective_id=0, has_side_effects=True, vmem_limit_bytes=VMEM_BYTES),
    )(*operands)


VMEM_BYTES = 67_000_000


def fused_body(
    inputs, cotangent, w_qkv, w_out, w_up, w_down, norm_gains, biases, time_table, timesteps, importance
):
    act, grad_in, g_qkv, g_out, g_up, g_down, grad_gains, grad_biases, grad_table = fused_call(
        lax.axis_size("dp") // 2, timesteps, importance, jnp.swapaxes(inputs, 0, 1), jnp.swapaxes(cotangent, 0, 1),
        w_qkv, w_out, w_up, w_down, norm_gains, biases, jnp.swapaxes(time_table, 1, 2),
    )
    act, grad_in, *rest = finish_call((act, grad_in), (g_qkv, g_out, g_up, g_down, grad_gains, grad_biases, grad_table))
    return (jnp.swapaxes(act, 0, 1), jnp.swapaxes(grad_in, 0, 1), *rest[:-1], jnp.swapaxes(rest[-1], 1, 2))


def finish_kernel(n_wide, n_same, *refs):
    ins, outs = refs[: n_wide + n_same], refs[n_wide + n_same :]
    for source, target in zip(ins[:n_wide], outs[:n_wide]):
        target[...] = source[...].astype(F32)

    def hand_on():
        for source, target in zip(ins[n_wide:], outs[n_wide:]):
            target[...] = source[...]

    pl.when(pl.program_id(0) == 0)(hand_on)


def finish_call(wide, same):
    tile = pl.BlockSpec((1, TILE, D), lambda i: (i, 0, 0))
    whole = [pl.BlockSpec(array.shape, lambda i, rank=array.ndim: (0,) * rank) for array in same]
    return pl.pallas_call(
        functools.partial(finish_kernel, len(wide), len(same)),
        grid=(3,),
        out_shape=[jax.ShapeDtypeStruct(array.shape, F32) for array in (*wide, *same)],
        in_specs=[tile] * len(wide) + whole,
        out_specs=[tile] * len(wide) + whole,
    )(*wide, *same)


def solution(mesh):
    devices = mesh.shape["dp"] * mesh.shape["seq"]
    whole_tiles = mesh.shape["seq"] == 4 and mesh.shape["dp"] % 2 == 0 and D // devices == 16
    in_specs = (
        P("seq", "dp", None),
        P("seq", "dp", None),
        P(None, ("dp", "seq"), None),
        P(None, ("dp", "seq"), None),
        P(None, ("dp", "seq"), None),
        P(None, ("dp", "seq"), None),
        P(None, ("dp", "seq")),
        P(None, ("dp", "seq")),
        P(None, None, ("dp", "seq")),
        P("dp"),
        P(),
    )
    out_specs = (
        P("seq", "dp", None),
        P("seq", "dp", None),
        P(None, ("dp", "seq"), None),
        P(None, ("dp", "seq"), None),
        P(None, ("dp", "seq"), None),
        P(None, ("dp", "seq"), None),
        P(None, ("dp", "seq")),
        P(None, ("dp", "seq")),
        P(None, None, ("dp", "seq")),
    )
    return jax.shard_map(
        fused_body if whole_tiles else body, mesh=mesh, in_specs=in_specs, out_specs=out_specs, check_vma=False)
```

```python
import functools
import math

import jax
import jax.numpy as jnp
from jax import lax
from jax.experimental import pallas as pl
from jax.experimental.pallas import tpu as pltpu
from jax.sharding import PartitionSpec as P

D = 512
HEADS = 8
HEAD_DIM = 64
FF = 2048
STEPS = 1000
LAYERS = 2


EPS = 1e-05
HIGH = lax.Precision.HIGHEST


def layer_norm(values, gain_vec, bias_vec):
    centered = values - jnp.mean(values, axis=-1, keepdims=True)
    spread = jnp.mean(centered * centered, axis=-1, keepdims=True)
    return centered * lax.rsqrt(spread + EPS) * gain_vec + bias_vec


def attend(queries, keys_all, values_all):
    row_count, seq_count, model_width = queries.shape
    score_scale = 1.0 / math.sqrt(HEAD_DIM)

    def per_seq(seq_index, loop_state):
        outputs, log_tot = loop_state
        query_per_head = lax.dynamic_index_in_dim(queries, seq_index, 1, keepdims=False).reshape(
            row_count, HEADS, HEAD_DIM
        )
        key_per_head = lax.dynamic_index_in_dim(keys_all, seq_index, 1, keepdims=False).reshape(
            -1, HEADS, HEAD_DIM
        )
        value_per_head = lax.dynamic_index_in_dim(values_all, seq_index, 1, keepdims=False).reshape(
            -1, HEADS, HEAD_DIM
        )
        scores = (
            jnp.einsum(
                "xsv,usv->sxu", query_per_head, key_per_head, preferred_element_type=jnp.float32
            )
            * score_scale
        )
        row_max = jnp.max(scores, axis=-1, keepdims=True)
        expon = jnp.exp(scores - row_max)
        summed = jnp.sum(expon, axis=-1, keepdims=True)
        attention_probability = (expon / summed).astype(jnp.bfloat16)
        attn_out = jnp.einsum(
            "gir,rgo->igo",
            attention_probability,
            value_per_head,
            preferred_element_type=jnp.float32,
        )
        attn_out = attn_out.astype(jnp.bfloat16).reshape(row_count, 1, model_width)
        outputs = lax.dynamic_update_slice_in_dim(outputs, attn_out, seq_index, 1)
        log_tot = lax.dynamic_update_slice_in_dim(
            log_tot, (row_max + jnp.log(summed))[None, :, :, 0], seq_index, 0
        )
        return (outputs, log_tot)

    start_state = (
        jnp.zeros(queries.shape, jnp.bfloat16),
        jnp.zeros((seq_count, HEADS, row_count), jnp.float32),
    )
    return lax.fori_loop(0, seq_count, per_seq, start_state)


def attend_back(queries, keys_all, values_all, log_tot, grad_attn):
    row_count, seq_count, model_width = queries.shape
    key_count = keys_all.shape[0]
    score_scale = 1.0 / math.sqrt(HEAD_DIM)

    def per_seq(seq_index, loop_state):
        grad_query, part_key, part_value = loop_state
        query_per_head = lax.dynamic_index_in_dim(queries, seq_index, 1, keepdims=False).reshape(
            row_count, HEADS, HEAD_DIM
        )
        key_per_head = lax.dynamic_index_in_dim(keys_all, seq_index, 1, keepdims=False).reshape(
            key_count, HEADS, HEAD_DIM
        )
        value_per_head = lax.dynamic_index_in_dim(values_all, seq_index, 1, keepdims=False).reshape(
            key_count, HEADS, HEAD_DIM
        )
        hidden_state_gradient = lax.dynamic_index_in_dim(
            grad_attn, seq_index, 1, keepdims=False
        ).reshape(row_count, HEADS, HEAD_DIM)
        log_seq = lax.dynamic_index_in_dim(log_tot, seq_index, 0, keepdims=False)
        scores = (
            jnp.einsum(
                "xsv,usv->sxu", query_per_head, key_per_head, preferred_element_type=jnp.float32
            )
            * score_scale
        )
        attn_f = jnp.exp(scores - log_seq[:, :, None])
        attention_probability = attn_f.astype(jnp.bfloat16)
        value_part = jnp.einsum(
            "uxo,xuc->ouc",
            attention_probability,
            hidden_state_gradient,
            preferred_element_type=jnp.float32,
        )
        probability_gradient = jnp.einsum(
            "xsv,usv->sxu",
            hidden_state_gradient,
            value_per_head,
            preferred_element_type=jnp.float32,
        )
        row_delta = jnp.sum(probability_gradient * attn_f, axis=-1, keepdims=True)
        score_gradient = (attn_f * (probability_gradient - row_delta)).astype(jnp.bfloat16)
        query_part = (
            jnp.einsum(
                "gir,rgo->igo", score_gradient, key_per_head, preferred_element_type=jnp.float32
            )
            * score_scale
        )
        key_part = (
            jnp.einsum(
                "uxo,xuc->ouc", score_gradient, query_per_head, preferred_element_type=jnp.float32
            )
            * score_scale
        )
        grad_query = lax.dynamic_update_slice_in_dim(
            grad_query, query_part.reshape(row_count, 1, model_width), seq_index, 1
        )
        part_key = lax.dynamic_update_slice_in_dim(
            part_key, key_part.reshape(key_count, 1, model_width), seq_index, 1
        )
        part_value = lax.dynamic_update_slice_in_dim(
            part_value, value_part.reshape(key_count, 1, model_width), seq_index, 1
        )
        return (grad_query, part_key, part_value)

    start_state = (
        jnp.zeros(queries.shape, jnp.float32),
        jnp.zeros(keys_all.shape, jnp.float32),
        jnp.zeros(keys_all.shape, jnp.float32),
    )
    return lax.fori_loop(0, seq_count, per_seq, start_state)


def forward_layer(hidden, fetched, onehot):
    mat_qkv, mat_out, up_matrix, down_matrix, gain_row, bias_row, time_rows = fetched
    gain_f = gain_row.astype(jnp.float32)
    bias_f = bias_row.astype(jnp.float32)
    seq_embed = jnp.dot(onehot.astype(jnp.bfloat16), time_rows, preferred_element_type=jnp.float32)
    summed_in = hidden + seq_embed[None]
    normed_one = layer_norm(summed_in, gain_f[:D], bias_f[4 * D + FF : 5 * D + FF]).astype(
        jnp.bfloat16
    )
    linear = jnp.dot(normed_one, mat_qkv, preferred_element_type=jnp.float32)
    queries = (linear[..., :D] + bias_f[:D]).astype(jnp.bfloat16)
    keys_loc = linear[..., D : 2 * D].astype(jnp.bfloat16)
    values_loc = (linear[..., 2 * D :] + bias_f[D : 2 * D]).astype(jnp.bfloat16)
    keys_all, values_all = (
        lax.all_gather(keys_loc, "seq", axis=0, tiled=True),
        lax.all_gather(values_loc, "seq", axis=0, tiled=True),
    )
    attn_out, log_tot = attend(queries, keys_all, values_all)
    after_attn = (
        summed_in
        + jnp.dot(attn_out, mat_out, preferred_element_type=jnp.float32)
        + bias_f[2 * D : 3 * D]
    )
    second_normalized = layer_norm(after_attn, gain_f[D:], bias_f[5 * D + FF :]).astype(
        jnp.bfloat16
    )
    upward = (
        jnp.dot(second_normalized, up_matrix, preferred_element_type=jnp.float32)
        + bias_f[3 * D : 3 * D + FF]
    )
    gelu_output = jax.nn.gelu(upward).astype(jnp.bfloat16)
    result = (
        after_attn
        + jnp.dot(gelu_output, down_matrix, preferred_element_type=jnp.float32)
        + bias_f[3 * D + FF : 4 * D + FF]
    )
    record = (
        summed_in,
        normed_one,
        queries,
        keys_loc,
        values_loc,
        attn_out,
        log_tot,
        after_attn,
        second_normalized,
        upward,
        gelu_output,
        keys_all,
        values_all,
    )
    return (result, record)


def backward_layer(hidden_state_gradient, fetched, record, onehot, kv_pair):
    mat_qkv = fetched[0]
    mat_out = fetched[1]
    up_matrix = fetched[2]
    down_matrix = fetched[3]
    gain_f = fetched[4].astype(jnp.float32)
    bias_f = fetched[5].astype(jnp.float32)
    summed_in, normed_one, queries = (record[0], record[1], record[2])
    attn_out, log_tot, after_attn = (record[5], record[6], record[7])
    second_normalized, upward, gelu_output = (record[8], record[9], record[10])
    keys_all, values_all = kv_pair
    gradient_bfloat = hidden_state_gradient.astype(jnp.bfloat16)
    down_weight_gradient = jnp.einsum(
        "awt,awg->tg", gelu_output, gradient_bfloat, preferred_element_type=jnp.float32
    )
    bias_down = jnp.sum(hidden_state_gradient, axis=(0, 1))
    activation_gradient = jnp.einsum(
        "ngb,rb->ngr", gradient_bfloat, down_matrix, preferred_element_type=jnp.float32
    )
    _, gelu_back = jax.vjp(jax.nn.gelu, upward)
    grad_upward = gelu_back(activation_gradient)[0]
    bias_up = jnp.sum(grad_upward, axis=(0, 1))
    upward_bfloat = grad_upward.astype(jnp.bfloat16)
    up_weight_gradient = jnp.einsum(
        "xew,xem->wm", second_normalized, upward_bfloat, preferred_element_type=jnp.float32
    )
    second_norm_gradient = jnp.einsum(
        "iyv,tv->iyt", upward_bfloat, up_matrix, preferred_element_type=jnp.float32
    )
    _, second_back = jax.vjp(layer_norm, after_attn, gain_f[D:], bias_f[5 * D + FF :])
    from_second, gain_two, shift_two = second_back(second_norm_gradient)
    grad_mid = hidden_state_gradient + from_second
    mid_bf = grad_mid.astype(jnp.bfloat16)
    grad_out = jnp.einsum("lsc,lsd->cd", attn_out, mid_bf, preferred_element_type=jnp.float32)
    bias_out = jnp.sum(grad_mid, axis=(0, 1))
    grad_attn = jnp.einsum(
        "lsd,cd->lsc", mid_bf, mat_out, preferred_element_type=jnp.float32
    ).astype(jnp.bfloat16)
    grad_query, part_key, part_value = attend_back(
        queries, keys_all, values_all, log_tot, grad_attn
    )
    grad_key, grad_value = (
        lax.psum_scatter(
            part_key.astype(jnp.bfloat16), "seq", scatter_dimension=0, tiled=True
        ).astype(jnp.float32),
        lax.psum_scatter(
            part_value.astype(jnp.bfloat16), "seq", scatter_dimension=0, tiled=True
        ).astype(jnp.float32),
    )
    bias_query = jnp.sum(grad_query, axis=(0, 1))
    bias_value = jnp.sum(grad_value, axis=(0, 1))
    grad_linear = jnp.concatenate([grad_query, grad_key, grad_value], axis=-1).astype(jnp.bfloat16)
    grad_qkv = jnp.einsum(
        "lsc,lse->ce", normed_one, grad_linear, preferred_element_type=jnp.float32
    )
    grad_norm_one = jnp.einsum(
        "lse,ce->lsc", grad_linear, mat_qkv, preferred_element_type=jnp.float32
    )
    _, first_back = jax.vjp(layer_norm, summed_in, gain_f[:D], bias_f[4 * D + FF : 5 * D + FF])
    from_first, gain_one, shift_one = first_back(grad_norm_one)
    grad_in = grad_mid + from_first
    grad_table = jnp.dot(onehot.T, jnp.sum(grad_in, axis=0), precision=HIGH)
    grad_gain = jnp.concatenate([gain_one, gain_two])
    grad_bias = jnp.concatenate(
        [bias_query, bias_value, bias_out, bias_up, bias_down, shift_one, shift_two]
    )
    return (
        grad_in,
        (
            grad_qkv,
            grad_out,
            up_weight_gradient,
            down_weight_gradient,
            grad_gain,
            grad_bias,
            grad_table,
        ),
    )


def body(
    inputs,
    cotangent,
    w_qkv,
    w_out,
    w_up,
    w_down,
    norm_gains,
    biases,
    time_table,
    timesteps,
    importance,
):
    onehot = (timesteps[:, None] == jnp.arange(STEPS, dtype=jnp.int32)[None, :]).astype(jnp.float32)
    seq_weight = jnp.dot(onehot, importance, precision=HIGH)
    hidden = inputs.astype(jnp.float32)
    records = []
    fetched_all = []
    for layer_id in range(LAYERS):
        fetched = (
            lax.all_gather(w_qkv[layer_id], ("dp", "seq"), axis=0, tiled=True),
            lax.all_gather(w_out[layer_id], ("dp", "seq"), axis=0, tiled=True),
            lax.all_gather(w_up[layer_id], ("dp", "seq"), axis=0, tiled=True),
            lax.all_gather(w_down[layer_id], ("dp", "seq"), axis=0, tiled=True),
            lax.all_gather(norm_gains[layer_id], ("dp", "seq"), axis=0, tiled=True),
            lax.all_gather(biases[layer_id], ("dp", "seq"), axis=0, tiled=True),
            lax.all_gather(time_table[layer_id], ("dp", "seq"), axis=1, tiled=True),
        )
        hidden, record = forward_layer(hidden, fetched, onehot)
        records.append(record)
        fetched_all.append(fetched)
    hidden_state_gradient = cotangent.astype(jnp.float32) * seq_weight[None, :, None]
    shards = [None] * LAYERS
    for layer_id in reversed(range(LAYERS)):
        record = records[layer_id]
        fetched = (
            lax.all_gather(w_qkv[layer_id], ("dp", "seq"), axis=0, tiled=True),
            lax.all_gather(w_out[layer_id], ("dp", "seq"), axis=0, tiled=True),
            lax.all_gather(w_up[layer_id], ("dp", "seq"), axis=0, tiled=True),
            lax.all_gather(w_down[layer_id], ("dp", "seq"), axis=0, tiled=True),
            lax.all_gather(norm_gains[layer_id], ("dp", "seq"), axis=0, tiled=True),
            lax.all_gather(biases[layer_id], ("dp", "seq"), axis=0, tiled=True),
            lax.all_gather(time_table[layer_id], ("dp", "seq"), axis=1, tiled=True),
        )
        kv_pair = (
            lax.all_gather(record[3], "seq", axis=0, tiled=True),
            lax.all_gather(record[4], "seq", axis=0, tiled=True),
        )
        hidden_state_gradient, grads = backward_layer(
            hidden_state_gradient, fetched, record, onehot, kv_pair
        )
        shards[layer_id] = (
            lax.psum_scatter(grads[0], ("dp", "seq"), scatter_dimension=0, tiled=True),
            lax.psum_scatter(grads[1], ("dp", "seq"), scatter_dimension=0, tiled=True),
            lax.psum_scatter(grads[2], ("dp", "seq"), scatter_dimension=0, tiled=True),
            lax.psum_scatter(grads[3], ("dp", "seq"), scatter_dimension=0, tiled=True),
            lax.psum_scatter(grads[4], ("dp", "seq"), scatter_dimension=0, tiled=True),
            lax.psum_scatter(grads[5], ("dp", "seq"), scatter_dimension=0, tiled=True),
            lax.psum_scatter(grads[6], ("dp", "seq"), scatter_dimension=1, tiled=True),
        )
    stacked = [
        jnp.stack([shards[layer_id][member] for layer_id in range(LAYERS)]) for member in range(7)
    ]
    return (
        hidden,
        hidden_state_gradient,
        stacked[0],
        stacked[1],
        stacked[2],
        stacked[3],
        stacked[4],
        stacked[5],
        stacked[6],
    )


MESH_ID = pl.DeviceIdType.MESH
LOG2E = 1.4426950408889634
F32 = jnp.float32
BF = jnp.bfloat16
TILE = 256
PAIRS = HEADS // 2
N_SEMS = 256
GELU_A = math.sqrt(2.0 / math.pi)
GELU_B = 0.044715

B_Q, B_V, B_O, B_U, B_D, B_S1, B_S2 = 0, D, 2 * D, 3 * D, 3 * D + FF, 4 * D + FF, 5 * D + FF


def nn(left, right):
    return jnp.dot(left, right, preferred_element_type=F32)


def nt(left, right, precision=None):
    return lax.dot_general(left, right, (((1,), (1,)), ((), ())), preferred_element_type=F32, precision=precision)


def tn(left, right):
    return lax.dot_general(left, right, (((0,), (0,)), ((), ())), preferred_element_type=F32)


def rows_sum(value):
    return jnp.sum(value, axis=0, keepdims=True)


def ln_parts(value):
    centered = value - jnp.mean(value, axis=-1, keepdims=True)
    scale = lax.rsqrt(jnp.mean(centered * centered, axis=-1, keepdims=True) + EPS)
    return centered * scale, scale


def gelu_parts(up):
    square = up * up
    tanh = jnp.tanh(GELU_A * up * (1.0 + GELU_B * square))
    return square, tanh


class Fused:
    def __init__(self, n_z, refs):
        (self.ts, self.imp, self.xin, self.cot, self.wq_i, self.wo_i, self.wu_i, self.wd_i, self.gains_i, self.biases_i, self.tab,
         self.act_o, self.gin_o, self.gq_o, self.go_o, self.gu_o, self.gd_o, self.gg_o, self.gb_o, self.gt_o,
         self.Wq, self.Wo, self.Wu, self.Wd, self.SM, self.TS, self.TT, self.T24, self.TR, self.BV, self.GV, self.BG, self.GG,
         self.TG, self.X, self.N, self.NT, self.Q, self.KV, self.AO, self.LSE, self.DL, self.Y, self.GB, self.DO, self.G,
         self.GN, self.GL, self.ACC, self.OWN, self.PB, self.RB1, self.RB2, self.RB3,
         self.R1, self.R2, self.R3, self.R4, self.SR, self.SX, self.SY,
         self.ssem, self.rsem, self.lsem, self.credit) = refs
        dp, seq = lax.axis_index("dp"), lax.axis_index("seq")
        self.n_z = n_z
        self.dp, self.seq = dp, seq
        self.z, self.x, self.y, self.c = dp // 2, dp % 2, seq // 2, seq % 2
        self.next_sem = 0
        self.next_local = 0
        self.mine = {"z": self.z, "x": self.x, "y": self.y, "c": self.c}
        self.other = {"x": 1 - self.x, "y": 1 - self.y, "c": 1 - self.c}
        self.around = [(self.z + hop) % n_z for hop in range(n_z)]
        n_dp = 2 * n_z
        self.far_z = {hop: (dp + hop) % n_dp // 2 for hop in range(1, n_dp)}
        self.far_x = {hop: (dp + hop) % n_dp % 2 for hop in range(1, n_dp)}
        other_x, other_y = self.z * 2 + self.other["x"], self.other["y"] * 2 + self.c
        self.device = {
            **{("z", hop): (self.around[hop] * 2 + self.x, seq) for hop in range(1, n_z)},
            ("x", 1): (other_x, seq),
            ("y", 1): (dp, other_y),
            ("c", 1): (dp, self.y * 2 + self.other["c"]),
            ("p", 1): (other_x, seq),
            ("p", 2): (dp, other_y),
            ("p", 3): (other_x, other_y),
            **{("d", hop): ((dp + hop) % n_dp, seq) for hop in range(1, n_dp)},
            **{("s", hop): (dp, (seq + hop) % 4) for hop in range(1, 4)},
        }
        self.device = {key: {"dp": there[0], "seq": there[1]} for key, there in self.device.items()}

    def hops(self, dim):
        return [hop for name, hop in self.device if name == dim]

    def enter(self):
        barrier = pltpu.get_barrier_semaphore()
        who = [key for key in self.device if key[0] in "ds"] + [("p", 3)]
        for key in who:
            pl.semaphore_signal(barrier, inc=1, device_id=self.device[key], device_id_type=MESH_ID)
        pl.semaphore_wait(barrier, len(who))

    def remote(self, src, dst, dim, hop=1, number=None):
        if number is None:
            number = self.next_sem
            self.next_sem += 1
        return pltpu.make_async_remote_copy(
            src, dst, self.ssem.at[number], self.rsem.at[number], device_id=self.device[dim, hop], device_id_type=MESH_ID
        )

    def local(self, src, dst):
        number = self.next_local
        self.next_local += 1
        return pltpu.make_async_copy(src, dst, self.lsem.at[number])


class Gather:
    def __init__(self, me, view, order):
        self.copies = []
        done = ""
        for dim in order:
            block = view(*[slice(None) if other in done else me.mine[other] for other in "zxyc"])
            self.copies.append([me.remote(block, block, dim, hop) for hop in me.hops(dim)])
            done += "xy" if dim == "p" else dim

    def start(self, stage):
        if stage:
            self.arrive(stage - 1)
        for copy in self.copies[stage]:
            copy.start()

    def arrive(self, stage=-1):
        for copy in self.copies[stage]:
            copy.wait_recv()

    def drain(self):
        for copies in self.copies:
            for copy in copies:
                copy.wait_send()


class Single:
    def __init__(self, copy):
        self.copy = copy

    def start(self, stage):
        self.copy.start()


class Reduce:
    def __init__(self, me, layer, grad, recv, out, cols, order, number, before):
        self.me, self.layer, self.grad, self.recv, self.out, self.cols, self.order = me, layer, grad, recv, out, cols, order
        self.number, self.before = number, before
        self.first_sem = before.first_sem if before else me.next_sem
        self.last = len(order) - 1
        self.copies = [self.build(stage) for stage in range(len(order))]

    def block(self, fixed):
        return tuple(fixed.get(dim, slice(None)) for dim in "zxyc")

    def kept(self, stage):
        done = "".join("xy" if dim == "p" else dim for dim in self.order[:stage])
        return {dim: self.me.mine[dim] for dim in done}

    def build(self, stage):
        me, dim = self.me, self.order[stage]
        copies = []
        number = self.first_sem + sum(len(me.hops(before)) for before in self.order[:stage])
        for hop in me.hops(dim):
            fixed = self.kept(stage)
            if dim == "z":
                fixed["z"] = me.around[hop]
            elif dim == "p":
                fixed["x"] = me.mine["x"] if hop == 2 else me.other["x"]
                fixed["y"] = me.mine["y"] if hop == 1 else me.other["y"]
            else:
                fixed[dim] = me.other[dim]
            src = self.grad.at[(self.layer, *self.block(fixed), slice(None), self.cols)]
            dst = self.landed(stage, hop).at[(*self.landing(stage, hop), slice(None), self.cols)]
            copies.append(me.remote(src, dst, dim, hop, number + len(copies) if self.before else None))
        return copies

    def landed(self, stage, hop):
        return self.recv[3] if stage == self.last else self.recv[stage]

    def landing(self, stage, hop):
        dim = self.order[stage]
        if stage == self.last:
            return (hop - 1,)
        if dim == "p":
            return (slice(None), hop - 1)
        if dim == "z":
            return (slice(2 * hop - 2, 2 * hop),)
        return ((slice(0, self.me.n_z), slice(None), slice(None)), (slice(None), slice(0, 2)), (slice(0, self.me.n_z),))[stage]

    def start(self, stage):
        me = self.me
        if stage:
            self.add(stage - 1)
            dim = self.order[stage - 1]
            if self.layer == LAYERS - 1:
                for hop in me.hops(dim):
                    pl.semaphore_signal(
                        me.credit.at[self.number, stage - 1], inc=1, device_id=me.device[dim, hop], device_id_type=MESH_ID
                    )
        if stage <= self.last:
            if self.layer < LAYERS - 1:
                pl.semaphore_wait(me.credit.at[self.number, stage], len(me.hops(self.order[stage])))
                for copy in self.before.copies[stage]:
                    copy.wait_send()
            for copy in self.copies[stage]:
                copy.start()

    def add(self, stage):
        me, dim = self.me, self.order[stage]
        for copy in self.copies[stage]:
            copy.wait_recv()
        fixed = self.kept(stage + 1)
        if stage == self.last or dim in "zp":
            where = (self.layer, *self.block(fixed), slice(None), self.cols)
            total = self.grad[where].astype(F32)
            for hop in me.hops(dim):
                total = total + self.landed(stage, hop)[(*self.landing(stage, hop), slice(None), self.cols)].astype(F32)
            if stage == self.last:
                self.out[self.layer, :, self.cols] = total
            else:
                self.grad[where] = total.astype(BF)
            return

        def one(z, carry):
            where = (self.layer, *self.block({**fixed, "z": z}), slice(None), self.cols)
            came = (z, *self.landing(stage, 1)[1:], slice(None), self.cols)
            self.grad[where] = self.grad[where] + self.recv[stage][came]
            return carry

        lax.fori_loop(0, me.n_z, one, 0)

    def drain(self):
        for copies in self.copies:
            for copy in copies:
                copy.wait_send()


def at_step(index, hooks):
    for when, action in hooks:
        pl.when(index == when)(action)


BACKWARD_AT = (21, 0)
END_AT = 42
GATHER = (
    ("pzc", 5, 6, 11),
    ("pzc", 0, 5, 11),
    ("zpc", 0, 3, 11),
    ("zpc", 0, 4, 10),
    ("pzc", 0, 10, 20),
    ("zpc", 0, 5, 19),
    ("zpc", 6, 14, 20),
    ("zpc", 11, 15, 23),
    ("zyxc", 0, 5, 8, 17),
    ("zpc", 4, 7, 21),
    ("pzc", 8, 15, 25),
    ("zpc", 12, 15, 25),
    ("zpc", 1, 18, 31),
    ("zpc", 12, 18, 37),
    ("zpc", 13, 22, 33),
    ("pzc", 8, 15, 34),
    ("zpc", 12, 28, 38),
    ("pzc", 21, 28, 38),
    ("pzc", 0, 4, 6),
    ("zpc", 2, 5, 7),
    ("y", 0),
    ("y", 33),
)
REDUCE = (
    ("cpz", 10, 15, 26, 32),
    ("cxzy", 5, 12, 18, 26, 42),
    ("cpz", 2, 6, 14, 32),
    ("cxzy", 8, 11, 15, 31, 43),
    ("cpz", 6, 10, 12, 40),
    ("cpz", 11, 12, 32, 42),
    ("cpz", 15, 15, 23, 40),
    ("cpz", 15, 15, 32, 34),
    ("cpz", 21, 24, 32, 35),
    ("cpz", 17, 21, 33, 41),
    ("cpz", 26, 28, 33, 42),
    ("cxzy", 30, 33, 36, 44, 46),
    ("cpz", 23, 25, 35, 43),
    ("cxzy", 28, 31, 34, 44, 46),
    ("cpz", 32, 36, 42, 44),
    ("cpz", 29, 35, 44, 46),
    ("cpz", 36, 37, 42, 44),
    ("cpz", 36, 36, 39, 43),
    ("cpz", 38, 38, 42, 44),
    ("cpz", 38, 38, 42, 44),
    ("y", 40),
)

SMALL, TIMES = "small", "times"


def pieces(name, layer):
    return 4 if name == "q" and layer == 0 else 2


def by_place(moves, plan):
    timeline = {}
    for move, (_, *places) in zip(moves, plan, strict=True):
        for stage, place in enumerate(places):
            timeline.setdefault(place, []).append((move, stage))
    return timeline


def fused_kernel(n_z, *refs):
    me = Fused(n_z, refs)
    x, y, z, c = me.x, me.y, me.z, me.c
    n_dp = 2 * n_z
    spare = slice(None)

    mats = ((me.wq_i, me.Wq), (me.wo_i, me.Wo), (me.wu_i, me.Wu), (me.wd_i, me.Wd))
    loads = [me.local(src.at[layer], dst.at[layer, z, x, y, c]) for layer in range(LAYERS) for src, dst in mats]
    for load in loads:
        load.start()
    own_tokens = [
        me.local(src.at[seq], dst.at[tile]) for src, dst in ((me.xin, me.DO), (me.cot, me.GB)) for seq, tile in ((y, 0), (2, 2))
    ]
    for load in own_tokens:
        load.start()

    row = lax.broadcasted_iota(jnp.int32, (32, 128), 0)
    steps = jnp.zeros((32, 128), jnp.int32)
    for j in range(3):
        steps = jnp.where(row == 3 * me.dp + j, me.ts[j], steps)
    me.TT[z, x] = steps

    def choose(rows, cols, first):
        here = lax.broadcasted_iota(jnp.int32, (rows, cols), 1) == first + lax.broadcasted_iota(jnp.int32, (rows, cols), 0)
        return here.astype(F32)

    own_biases, own_gains = choose(160, 640, 160 * me.seq), choose(32, 128, 32 * me.seq)
    own_lanes = choose(16, 128, 16 * (4 * x + me.seq))
    spread_b = nn(me.biases_i[...].astype(F32), own_biases)
    spread_g = nn(me.gains_i[...].astype(F32), own_gains)
    rows = []
    for layer in range(LAYERS):
        rows += [spread_b[layer : layer + 1, 128 * r : 128 * r + 128] for r in range(5)] + [spread_g[layer : layer + 1]]
    me.SM[z, x, y, c] = jnp.concatenate(rows + [jnp.zeros((16 - 6 * LAYERS, 128), F32)], axis=0).astype(BF)
    me.BG[...] = jnp.zeros_like(me.BG)
    me.GG[...] = jnp.zeros_like(me.GG)

    me.enter()
    for load in loads:
        load.wait()

    def weight(layer, ref, order, cols):
        return Gather(me, lambda *where: ref.at[(layer, *where, spare, cols)], order)

    grads = {"q": me.Wq, "o": me.Wo, "u": me.Wu, "d": me.Wd}

    steps_all = Gather(me, lambda gz, gx, gy, gc: me.TT.at[gz, gx], "d")
    token_in = me.remote(me.xin.at[me.other["y"]], me.DO.at[1], "y")
    cot_in = me.remote(me.cot.at[me.other["y"]], me.GB.at[1], "y")
    moves = {}
    plan = iter(GATHER)
    for layer in range(LAYERS):
        for name, ref in grads.items():
            width = ref.shape[-1] // pieces(name, layer)
            for part in range(pieces(name, layer)):
                moves[name, part, layer] = weight(layer, ref, next(plan)[0], slice(width * part, width * (part + 1)))
    moves[SMALL] = small = Gather(me, lambda *where: me.SM.at[where], next(plan)[0])
    moves[TIMES] = times = Gather(me, lambda *where: me.TS.at[where], next(plan)[0])
    timeline = by_place([*moves.values(), Single(token_in), Single(cot_in)], GATHER)

    def have(names, layer):
        for name in names:
            for part in range(pieces(name, layer)):
                moves[name, part, layer].arrive()

    def fire(place):
        for move, stage in timeline.get(place, ()):
            move.start(stage)

    def fires(first, count):
        return [(i, functools.partial(fire, first + i)) for i in range(count) if first + i in timeline]

    steps_all.start(0)
    fire(0)
    fire(1)
    steps_all.arrive()
    t24 = jnp.sum(me.TT[...].reshape(n_dp, 32, 128), axis=0)
    me.T24[...] = t24
    hot = (t24[:, 0:1] == lax.broadcasted_iota(jnp.int32, (32, STEPS), 1)).astype(F32).astype(BF)
    picked = jnp.concatenate([nt(hot, me.tab[layer])[:24] for layer in range(LAYERS)], axis=0).astype(BF)
    me.TS[z, x, y, c] = nn(picked, own_lanes.astype(BF)).astype(BF)
    for place in range(2, 11):
        fire(place)

    small.arrive()
    for gz in range(n_z):
        for gx in range(2):
            block = jnp.sum(me.SM[gz, gx].reshape(4, 16, 128).astype(F32), axis=0)
            dp = 2 * gz + gx
            for layer in range(LAYERS):
                for r in range(5):
                    at = (5 * dp + r) * 128
                    me.BV[layer, :, at : at + 128] = block[6 * layer + r : 6 * layer + r + 1]
                me.GV[layer, :, 128 * dp : 128 * dp + 128] = block[6 * layer + 5 : 6 * layer + 6]
    times.arrive()
    slabs = jnp.concatenate(
        [jnp.sum(me.TS[gz].reshape(8, 48, 128).astype(F32), axis=0) for gz in range(n_z)], axis=1
    ).astype(BF)
    r8 = lax.broadcasted_iota(jnp.int32, (16, 48), 0)
    c48 = lax.broadcasted_iota(jnp.int32, (16, 48), 1)
    for layer in range(LAYERS):
        base = 24 * layer + 3 * me.dp
        pick = ((r8 == 0) & (c48 == base + y)) | ((r8 == 1) & (c48 == base + 2))
        me.TR[layer] = nn(pick.astype(F32).astype(BF), slabs)[:8]

    def time_row(layer, tile):
        return me.TR[layer, 1:2, :] if tile == 2 else me.TR[layer, 0:1, :]

    def bias(layer, at, width=D):
        return me.BV[layer, :, at : at + width]

    for load in own_tokens:
        load.wait()
    for tile in (0, 2):
        me.X[0, tile] = me.DO[tile].astype(F32) + time_row(0, tile)

    sends = [token_in, cot_in]

    def send(src, dst, dim):
        copy = me.remote(src, dst, dim)
        sends.append(copy)
        return copy

    def attention_norm(layer, tile):
        hat, _ = ln_parts(me.X[layer, tile])
        return (hat * me.GV[layer, :, :D] + bias(layer, B_S1)).astype(BF)

    def columns(layer, normed, j):
        return nn(normed, me.Wq[layer, :, :, :, :, :, D * j : D * j + D].reshape(D, D))

    def keys_values(layer, normed, slot):
        me.KV[layer, 0, slot] = columns(layer, normed, 1).astype(BF)
        me.KV[layer, 1, slot] = (columns(layer, normed, 2) + bias(layer, B_V)).astype(BF)

    low_lanes = lax.broadcasted_iota(jnp.int32, (TILE, 128), 1) < HEAD_DIM

    def two_heads(pair):
        zero = jnp.zeros_like(pair)
        return jnp.concatenate([jnp.where(low_lanes, pair, zero), jnp.where(low_lanes, zero, pair)], axis=0)

    def attend_two(layer, step):
        tile, base = step // 2, step // 4 * 4
        first = step % 2 * 2
        cols = [pl.ds(pl.multiple_of((first + i) * 128, 128), 128) for i in range(2)]
        queries = [two_heads(me.Q[layer, tile, :, cols[i]]) for i in range(2)]

        def block(which, part, i):
            return me.KV[layer, which, pl.ds(base + 2 * part, 2), :, cols[i]].reshape(2 * TILE, 128)

        def scores(part, i):
            return nt(block(0, part, i), queries[i])

        def highest(parts):
            tops = [jnp.max(part, axis=0, keepdims=True) for part in parts]
            return jnp.maximum(tops[0], tops[1]) * LOG2E

        def mix(score, top, part, i):
            values = jnp.concatenate([block(1, part, i).T, jnp.ones((16, 2 * TILE), BF)], axis=0)
            return nn(values, jnp.exp2(score * LOG2E - top).astype(BF))

        def finish(mixed, top, i):
            total = mixed[128:129]
            mixed = mixed[:128] * (1.0 / total)
            me.LSE[layer, tile, first + i] = top + jnp.log2(total)
            out = jnp.concatenate([mixed[:HEAD_DIM, :TILE], mixed[HEAD_DIM:, TILE:]], axis=0)
            me.AO[layer, tile, :, cols[i]] = out.T.astype(BF)

        now = [scores(0, 0), scores(1, 0)]
        top = highest(now)
        later, mixed = [], 0.0
        for part in range(2):
            later.append(scores(part, 1))
            mixed = mixed + mix(now[part], top, part, 0)
        finish(mixed, top, 0)
        top = highest(later)
        finish(mix(later[0], top, 0, 1) + mix(later[1], top, 1, 1), top, 1)

    kv = me.KV
    to_y = [me.remote(me.N.at[2], me.PB.at[0, layer], "y") for layer in range(LAYERS)]
    on_c = [send(kv.at[layer, :, 5], kv.at[layer, :, 7], "c") for layer in range(LAYERS)]
    to_c = [
        [send(kv.at[layer, :, a], kv.at[layer, :, b], "c") for a, b in ((0, 2), (1, 3), (4, 6))] for layer in range(LAYERS)
    ]

    def announce(layer):
        me.N[2] = attention_norm(layer, 2)
        to_y[layer].start()

    def project(layer, tile):
        normed = me.N[2] if tile == 2 else attention_norm(layer, tile)
        keys_values(layer, normed, 4 if tile == 2 else tile)
        to_c[layer][tile].start()
        queries = (columns(layer, normed, 0) + bias(layer, B_Q)).astype(BF)
        me.Q[layer, tile] = queries * jnp.asarray(1.0 / math.sqrt(HEAD_DIM), BF)

    def neighbour(layer):
        to_y[layer].wait_recv()
        keys_values(layer, me.PB[0, layer], 5)
        on_c[layer].start()

    def attention(layer, first, last, place):
        def step(index, carry):
            at_step(index - first, fires(place, last - first))
            attend_two(layer, index)
            return carry

        lax.fori_loop(first, last, step, 0)

    def rest(layer, tiles, place):
        if tiles[0] == 0:
            have("o", layer)
        fire(place)
        w_out = me.Wo[layer].reshape(D, D)
        for tile in tiles:
            after = me.X[layer, tile] + nn(me.AO[layer, tile], w_out) + bias(layer, B_O)
            me.Y[layer, tile] = after
            hat, _ = ln_parts(after)
            me.N[tile] = (hat * me.GV[layer, :, D:] + bias(layer, B_S2)).astype(BF)
            me.GN[tile] = after + bias(layer, B_D)
        if tiles[0] == 0:
            have("ud", layer)

        def ffn(half, carry):
            at_step(half, fires(place + 1, 2))
            cols = pl.ds(pl.multiple_of(half * (FF // 2), FF // 2), FF // 2)
            w_up = me.Wu[layer, :, :, :, :, :, cols].reshape(D, FF // 2)
            w_down = me.Wd[layer, pl.ds(half * (n_z // 2), n_z // 2)].reshape(FF // 2, D)
            b_up = me.BV[layer, :, pl.ds(pl.multiple_of(B_U + half * (FF // 2), D), FF // 2)]
            for tile in tiles:
                up = nn(me.N[tile], w_up) + b_up
                _, tanh = gelu_parts(up)
                me.GN[tile] += nn((0.5 * up * (1.0 + tanh)).astype(BF), w_down)
            return carry

        lax.fori_loop(0, 2, ffn, 0)

    def third_keys(layer):
        to_y[layer].wait_send()
        to_c[layer][2].wait_recv()
        on_c[layer].wait_recv()

    announce(0)
    fire(11)
    have("q", 0)
    project(0, 2)
    fire(12)
    project(0, 0)
    fire(13)
    token_in.wait_recv()
    me.X[0, 1] = me.DO[1].astype(F32) + time_row(0, 1)
    project(0, 1)
    fire(14)
    neighbour(0)
    to_c[0][0].wait_recv()
    to_c[0][1].wait_recv()
    for layer in range(LAYERS):
        at = (15, 30)[layer]
        attention(layer, 0, 4, at)
        fire(at + 4)
        if layer:
            neighbour(layer)
        fire(at + 5)
        third_keys(layer)
        attention(layer, 4, 6, at + 6)
        rest(layer, (0, 1, 2), at + 8)
        if layer == 0:
            for tile in range(3):
                me.X[1, tile] = me.GN[tile] + time_row(1, tile)
            announce(1)
            fire(26)
            have("q", 1)
            for turn, tile in enumerate((2, 0, 1)):
                project(1, tile)
                fire(27 + turn)
            to_c[1][0].wait_recv()
            to_c[1][1].wait_recv()
    act_out = [
        me.local(me.DO.at[0], me.act_o.at[y]), me.remote(me.DO.at[1], me.act_o.at[y], "y"), me.local(me.DO.at[2], me.act_o.at[2])
    ]
    for tile in range(3):
        me.DO[tile] = me.GN[tile].astype(BF)
    for copy in act_out:
        copy.start()

    cot_in.wait_recv()
    weight_y, weight_2 = me.imp[me.ts[y]], me.imp[me.ts[2]]
    for tile in range(3):
        grad = me.GB[tile].astype(F32) * (weight_2 if tile == 2 else weight_y)
        me.G[tile] = grad
    for part in [steps_all, *moves.values()]:
        part.drain()
    for copy in sends:
        copy.wait_send()
    sends.clear()

    outs = {"q": me.gq_o, "o": me.go_o, "u": me.gu_o, "d": me.gd_o}
    recvs = {
        name: [me.R1[i], me.R2[i], me.R3[i], me.R4[i]] for i, name in enumerate("qoud")
    }

    spans = {
        "d": ("d", 0, D), "u": ("u", 0, FF), "o": ("o", 0, D), "p": ("q", 0, D), "q": ("q", D, 3 * D)
    }

    plan = iter(REDUCE)

    def piece(layer, number, name, half):
        kind, begin, end = spans[name]
        width = (end - begin) // 2
        start = begin + width * half
        before = sums[number] if layer < LAYERS - 1 else None
        cols = slice(start, start + width)
        return Reduce(me, layer, grads[kind], recvs[kind], outs[kind], cols, next(plan)[0], number, before)

    def add_bias(layer, at, value):
        me.BG[layer, :, at : at + value.shape[-1]] += value

    def ln_back(layer, gain_at, shift_at, source, grad):
        hat, scale = ln_parts(source)
        me.GG[layer, :, gain_at : gain_at + D] += rows_sum(grad * hat)
        add_bias(layer, shift_at, rows_sum(grad))
        inner = grad * me.GV[layer, :, gain_at : gain_at + D]
        return scale * (inner - jnp.mean(inner, axis=-1, keepdims=True) - hat * jnp.mean(inner * hat, axis=-1, keepdims=True))

    def normed_t(layer, source, gain_at, shift_at):
        for tile in range(3):
            hat, _ = ln_parts(source[layer, tile])
            normed = (hat * me.GV[layer, :, gain_at : gain_at + D] + bias(layer, shift_at)).astype(BF)
            me.N[tile] = normed
            me.NT[:, TILE * tile : TILE * tile + TILE] = normed.T

    head_of = lax.broadcasted_iota(jnp.int32, (HEADS, D), 1) // HEAD_DIM
    selector = (head_of == lax.broadcasted_iota(jnp.int32, (HEADS, D), 0)).astype(F32)

    def backward(layer, before_out, tail):
        base = BACKWARD_AT[layer]
        normed_t(layer, me.Y, D, B_S2)
        for tile in range(3):
            me.GB[tile] = me.G[tile].astype(BF)
            add_bias(layer, B_D, rows_sum(me.G[tile]))
            me.GN[tile] = jnp.zeros((TILE, D), F32)

        def ffn(slab, carry):
            at_step(slab, fires(base, n_z))
            cols = pl.ds(pl.multiple_of(slab * D, D), D)
            b_cols = pl.ds(pl.multiple_of(B_U + slab * D, D), D)
            w_up = me.Wu[layer, :, :, :, :, :, cols].reshape(D, D)
            w_down = me.Wd[layer, slab].reshape(D, D)
            grads_h = me.GB[...].reshape(3 * TILE, D)
            up = nn(me.N[...].reshape(3 * TILE, D), w_up) + me.BV[layer, :, b_cols]
            square, tanh = gelu_parts(up)
            active = (0.5 * up * (1.0 + tanh)).astype(BF)
            slope = 0.5 * (1.0 + tanh) + (0.5 * GELU_A) * up * (1.0 - tanh * tanh) * (1.0 + 3.0 * GELU_B * square)
            grad_up = nt(grads_h, w_down) * slope
            me.BG[layer, :, b_cols] += rows_sum(grad_up)
            grad_up = grad_up.astype(BF)
            me.GN[...] += nt(grad_up, w_up).reshape(3, TILE, D)
            me.Wd[layer, slab] = tn(active, grads_h).astype(BF).reshape(2, 2, 2, 64, D)
            me.Wu[layer, :, :, :, :, :, cols] = nn(me.NT[...], grad_up).astype(BF).reshape(n_z, 2, 2, 2, 16, D)
            return carry

        lax.fori_loop(0, n_z, ffn, 0)
        fire(base + 4)
        for tile in range(3):
            mid = me.G[tile] + ln_back(layer, D, B_S2, me.Y[layer, tile], me.GN[tile])
            me.G[tile] = mid
            add_bias(layer, B_O, rows_sum(mid))
            me.GB[tile] = mid.astype(BF)
        fire(base + 5)
        before_out()
        w_out = me.Wo[layer].reshape(D, D)
        me.DO[...] = nt(me.GB[...].reshape(3 * TILE, D), w_out).astype(BF).reshape(3, TILE, D)
        for tile in range(3):
            delta = nt(selector, me.DO[tile].astype(F32) * me.AO[layer, tile].astype(F32), lax.Precision.HIGHEST)
            for pair in range(PAIRS):
                both = jnp.concatenate([delta[2 * pair : 2 * pair + 1], delta[2 * pair + 1 : 2 * pair + 2]], axis=1)
                me.DL[tile, pair] = both
        d_out = tn(me.AO[layer].reshape(3 * TILE, D), me.GB[...].reshape(3 * TILE, D))
        me.Wo[layer] = d_out.astype(BF).reshape(n_z, 2, 2, 2, 16, D)
        fire(base + 6)

        me.ACC[...] = jnp.zeros_like(me.ACC)
        third_c = send(me.PB, me.RB1, "c")
        third_y = me.remote(me.GL.at[2, :, D:], me.RB2, "y")
        from_c = me.remote(me.GL.at[0:2, :, D:], me.RB3, "c")

        def third_done():
            me.OWN[...] = me.ACC[:, 0:TILE]
            for i in range(2):
                me.GL[2, :, D * (1 + i) : D * (2 + i)] = me.ACC[i, TILE : 2 * TILE].astype(BF)
            me.PB[...] = me.ACC[:, 2 * TILE :].reshape(2, 2, TILE, D).astype(BF)
            me.ACC[...] = jnp.zeros_like(me.ACC)
            third_c.start()

        def third_on():
            third_c.wait_recv()
            me.OWN[...] += me.RB1[:, 0].astype(F32)
            for i in range(2):
                cols = slice(D * (1 + i), D * (2 + i))
                me.GL[2, :, cols] = me.GL[2, :, cols] + me.RB1[i, 1]
            third_y.start()

        def attend_back(step, carry):
            at_step(step, [(2, third_done), (3, third_on)] + fires(base + 8, 6))
            tile = (step // 2 + 2) % 3
            slot = tile // 2 * 4
            for i in range(2):
                pair = step % 2 * 2 + i
                cols = pl.ds(pl.multiple_of(pair * 128, 128), 128)
                queries, grads_o = two_heads(me.Q[layer, tile, :, cols]), two_heads(me.DO[tile, :, cols])
                log_sum, delta = me.LSE[layer, tile, pair], me.DL[tile, pair]
                d_query = jnp.zeros((128, 2 * TILE), F32)
                for part in range(4):
                    keys, values = me.KV[layer, 0, slot + part, :, cols], me.KV[layer, 1, slot + part, :, cols]
                    rows = slice(TILE * part, TILE * part + TILE)
                    prob = jnp.exp2(nt(keys, queries) * LOG2E - log_sum)
                    grad_s = (prob * (nt(values, grads_o) - delta)).astype(BF)
                    me.ACC[1, rows, cols] += nn(prob.astype(BF), grads_o)
                    me.ACC[0, rows, cols] += nn(grad_s, queries)
                    d_query = d_query + nn(keys.T, grad_s)
                d_query = jnp.concatenate([d_query[:HEAD_DIM, :TILE], d_query[HEAD_DIM:, TILE:]], axis=0).T
                d_query = d_query * (1.0 / math.sqrt(HEAD_DIM))
                me.BG[layer, :, cols] += rows_sum(d_query)
                me.GL[tile, :, cols] = d_query.astype(BF)
            return carry

        fire(base + 7)
        lax.fori_loop(0, 6, attend_back, 0)
        for tile in range(2):
            for i in range(2):
                rows = slice(TILE * (2 + tile), TILE * (3 + tile))
                me.GL[tile, :, D * (1 + i) : D * (2 + i)] = me.ACC[i, rows].astype(BF)
        from_c.start()
        normed_t(layer, me.X, 0, B_S1)
        fire(base + 14)

        def qkv_back(first, last):
            w_qkv = me.Wq[layer, :, :, :, :, :, first:last].reshape(D, last - first)
            part = nt(me.GL[:, :, first:last].reshape(3 * TILE, last - first), w_qkv).reshape(3, TILE, D)
            me.GN[...] = part if first == 0 else me.GN[...] + part
            for j in range(first, last, D):
                d_qkv = nn(me.NT[...], me.GL[:, :, j : j + D].reshape(3 * TILE, D))
                me.Wq[layer, :, :, :, :, :, j : j + D] = d_qkv.astype(BF).reshape(n_z, 2, 2, 2, 16, D)

        qkv_back(0, D)
        fire(base + 15)
        from_c.wait()
        for tile in range(2):
            rows = slice(TILE * tile, TILE * tile + TILE)
            key = me.ACC[0, rows] + me.RB3[tile, :, :D].astype(F32)
            value = me.ACC[1, rows] + me.RB3[tile, :, D:].astype(F32)
            add_bias(layer, B_V, rows_sum(value))
            me.GL[tile, :, D : 2 * D] = key.astype(BF)
            me.GL[tile, :, 2 * D :] = value.astype(BF)
        third_y.wait()
        third = [me.OWN[i] + me.RB2[:, D * i : D * i + D].astype(F32) for i in range(2)]
        me.GL[2, :, D : 2 * D] = third[0].astype(BF)
        me.GL[2, :, 2 * D :] = third[1].astype(BF)
        add_bias(layer, B_V, rows_sum(third[1]))
        fire(base + 16)
        qkv_back(D, 3 * D)
        fire(base + 17)
        totals = []
        for tile in (1, 0, 2):
            grad = me.G[tile] + ln_back(layer, 0, B_S1, me.X[layer, tile], me.GN[tile])
            me.G[tile] = grad
            totals.append(rows_sum(grad))
            tail(tile, grad)
            fire(base + 17 + len(totals))
        me.TG[layer, 0:1] = totals[0] + totals[1]
        me.TG[layer, 1:2] = totals[2]
        for copy in sends:
            copy.wait_send()
        sends.clear()

    sums = []
    for layer in reversed(range(LAYERS)):
        for number, (name, half) in enumerate((name, half) for name in spans for half in range(2)):
            sums.append(piece(layer, number, name, half))
    timeline.clear()
    gin_out = me.remote(me.GB.at[1], me.gin_o.at[y], "y")
    timeline.update(by_place([*sums, Single(gin_out)], REDUCE))

    def act_done():
        for copy in act_out:
            copy.wait()

    backward(1, act_done, lambda tile, grad: None)
    finals = []

    def out_tile(tile, grad):
        me.GB[tile] = grad.astype(BF)
        if tile != 1:
            finals.append(me.local(me.GB.at[tile], me.gin_o.at[y if tile == 0 else 2]))
            finals[-1].start()

    backward(0, lambda: None, out_tile)

    for gz in range(n_z):
        lanes = slice(128 * gz, 128 * gz + 128)
        for gx in range(2):
            dp = 2 * gz + gx
            for layer in range(LAYERS):
                for r in range(5):
                    at_lane = (5 * dp + r) * 128
                    me.SR[gz, gx, 6 * layer + r : 6 * layer + r + 1] = me.BG[layer, :, at_lane : at_lane + 128]
                me.SR[gz, gx, 6 * layer + 5 : 6 * layer + 6] = me.GG[layer, :, 128 * dp : 128 * dp + 128]
                me.SR[gz, gx, 12 + 2 * layer : 14 + 2 * layer] = me.TG[layer, 0:2, lanes]
    to_dp = [
        me.remote(me.SR.at[me.far_z[hop], me.far_x[hop]], me.SX.at[me.dp], "d", hop) for hop in me.hops("d")
    ]
    for copy in to_dp:
        copy.start()
    me.SX[me.dp] = me.SR[z, x]
    fire(END_AT)
    for copy in to_dp:
        copy.wait_recv()
    fire(END_AT + 1)
    me.SY[0, 0:16] = jnp.sum(me.SX[...], axis=0)
    for dp in range(n_dp):
        for layer in range(LAYERS):
            at_row = 16 + 24 * layer + 3 * dp
            first_seq = me.SX[dp, 12 + 2 * layer : 13 + 2 * layer]
            me.SY[0, at_row : at_row + 1] = jnp.where(y == 0, first_seq, 0.0)
            me.SY[0, at_row + 1 : at_row + 2] = jnp.where(y == 1, first_seq, 0.0)
            me.SY[0, at_row + 2 : at_row + 3] = me.SX[dp, 13 + 2 * layer : 14 + 2 * layer]
    to_seq = [me.remote(me.SY.at[0], me.SY.at[hop], "s", hop) for hop in me.hops("s")]
    for copy in to_seq:
        copy.start()
    fire(END_AT + 2)
    for copy in to_seq:
        copy.wait_recv()
    fire(END_AT + 3)
    total = me.SY[0] + me.SY[1] + me.SY[2] + me.SY[3]
    hot = (me.T24[0:24, 0:1] == lax.broadcasted_iota(jnp.int32, (24, STEPS), 1)).astype(F32)
    for layer in range(LAYERS):
        bias_row = jnp.concatenate([total[6 * layer + r : 6 * layer + r + 1] for r in range(5)], axis=1)
        me.gb_o[layer : layer + 1] = nt(bias_row, own_biases, HIGH)
        me.gg_o[layer : layer + 1] = nt(total[6 * layer + 5 : 6 * layer + 6], own_gains, HIGH)
        by_seq = nt(own_lanes, total[16 + 24 * layer : 40 + 24 * layer], HIGH)
        me.gt_o[layer] = jnp.dot(by_seq, hot, precision=HIGH, preferred_element_type=F32)
    fire(END_AT + 4)

    for copy in to_dp + to_seq:
        copy.wait_send()
    for copy in [gin_out, *finals]:
        copy.wait()
    for part in sums[len(sums) // 2 :]:
        part.drain()


def fused_call(n_z, *operands):
    any_space, vmem, smem = (pl.BlockSpec(memory_space=space) for space in (pl.ANY, pltpu.VMEM, pltpu.SMEM))
    cube = (n_z, 2, 2, 2)
    tokens = (3, TILE, D)
    sizes = ((16, 3 * D), (16, D), (16, FF), (64, D))

    def many(lead):
        return [tuple(pltpu.VMEM((*lead, *size), BF) for size in sizes)]

    flat, tree = jax.tree.flatten(
        [pltpu.VMEM((LAYERS, *cube, *size), BF) for size in sizes]
        + [
            pltpu.VMEM((*cube, 16, 128), BF),
            pltpu.VMEM((*cube, 48, 128), BF),
            pltpu.VMEM((n_z, 2, 32, 128), jnp.int32),
            pltpu.VMEM((32, 128), jnp.int32),
            pltpu.VMEM((LAYERS, 8, D), F32),
            pltpu.VMEM((LAYERS, 1, 6 * D + FF), F32),
            pltpu.VMEM((LAYERS, 1, 2 * D), F32),
            pltpu.VMEM((LAYERS, 1, 6 * D + FF), F32),
            pltpu.VMEM((LAYERS, 1, 2 * D), F32),
            pltpu.VMEM((LAYERS, 8, D), F32),
            pltpu.VMEM((LAYERS, *tokens), F32),
            pltpu.VMEM(tokens, BF),
            pltpu.VMEM((D, 3 * TILE), BF),
            pltpu.VMEM((LAYERS, *tokens), BF),
            pltpu.VMEM((LAYERS, 2, 8, TILE, D), BF),
            pltpu.VMEM((LAYERS, *tokens), BF),
            pltpu.VMEM((LAYERS, 3, PAIRS, 1, 2 * TILE), F32),
            pltpu.VMEM((3, PAIRS, 1, 2 * TILE), F32),
            pltpu.VMEM((LAYERS, *tokens), F32),
            pltpu.VMEM(tokens, BF),
            pltpu.VMEM(tokens, BF),
            pltpu.VMEM(tokens, F32),
            pltpu.VMEM(tokens, F32),
            pltpu.VMEM((3, TILE, 3 * D), BF),
            pltpu.VMEM((2, 4 * TILE, D), F32),
            pltpu.VMEM((2, TILE, D), F32),
            pltpu.VMEM((2, 2, TILE, D), BF),
            pltpu.VMEM((2, 2, TILE, D), BF),
            pltpu.VMEM((TILE, 2 * D), BF),
            pltpu.VMEM((2, TILE, 2 * D), BF),
        ]
        + many((n_z, 2, 2))
        + many((n_z, 3))
        + many((2 * n_z - 2,))
        + many((n_z - 1,))
        + [
            pltpu.VMEM((n_z, 2, 16, 128), F32),
            pltpu.VMEM((2 * n_z, 16, 128), F32),
            pltpu.VMEM((4, 64, 128), F32),
            pltpu.SemaphoreType.DMA((N_SEMS,)),
            pltpu.SemaphoreType.DMA((N_SEMS,)),
            pltpu.SemaphoreType.DMA((32,)),
            pltpu.SemaphoreType.REGULAR((10, 4)),
        ]
    )
    outs = [
        jax.ShapeDtypeStruct(tokens, BF),
        jax.ShapeDtypeStruct(tokens, BF),
        *[jax.ShapeDtypeStruct((LAYERS, *size), F32) for size in sizes],
        jax.ShapeDtypeStruct((LAYERS, 32), F32),
        jax.ShapeDtypeStruct((LAYERS, 160), F32),
        jax.ShapeDtypeStruct((LAYERS, 16, STEPS), F32),
    ]

    def run(*refs):
        head = len(operands) + len(outs)
        fused_kernel(n_z, *refs[:head], *jax.tree.unflatten(tree, refs[head:]))

    return pl.pallas_call(
        run,
        out_shape=outs,
        in_specs=[smem, smem] + [any_space] * 6 + [vmem] * 3,
        out_specs=[any_space] * 2 + [vmem] * 7,
        scratch_shapes=flat,
        compiler_params=pltpu.CompilerParams(collective_id=0, has_side_effects=True, vmem_limit_bytes=VMEM_BYTES),
    )(*operands)


VMEM_BYTES = 67_000_000


def fused_body(
    inputs, cotangent, w_qkv, w_out, w_up, w_down, norm_gains, biases, time_table, timesteps, importance
):
    act, grad_in, g_qkv, g_out, g_up, g_down, grad_gains, grad_biases, grad_table = fused_call(
        lax.axis_size("dp") // 2, timesteps, importance, jnp.swapaxes(inputs, 0, 1), jnp.swapaxes(cotangent, 0, 1),
        w_qkv, w_out, w_up, w_down, norm_gains, biases, jnp.swapaxes(time_table, 1, 2),
    )
    act, grad_in, *rest = finish_call((act, grad_in), (g_qkv, g_out, g_up, g_down, grad_gains, grad_biases, grad_table))
    return (jnp.swapaxes(act, 0, 1), jnp.swapaxes(grad_in, 0, 1), *rest[:-1], jnp.swapaxes(rest[-1], 1, 2))


def finish_kernel(n_wide, n_same, *refs):
    ins, outs = refs[: n_wide + n_same], refs[n_wide + n_same :]
    for source, target in zip(ins[:n_wide], outs[:n_wide]):
        target[...] = source[...].astype(F32)

    def hand_on():
        for source, target in zip(ins[n_wide:], outs[n_wide:]):
            target[...] = source[...]

    pl.when(pl.program_id(0) == 0)(hand_on)


def finish_call(wide, same):
    tile = pl.BlockSpec((1, TILE, D), lambda i: (i, 0, 0))
    whole = [pl.BlockSpec(array.shape, lambda i, rank=array.ndim: (0,) * rank) for array in same]
    return pl.pallas_call(
        functools.partial(finish_kernel, len(wide), len(same)),
        grid=(3,),
        out_shape=[jax.ShapeDtypeStruct(array.shape, F32) for array in (*wide, *same)],
        in_specs=[tile] * len(wide) + whole,
        out_specs=[tile] * len(wide) + whole,
    )(*wide, *same)


def solution(mesh):
    devices = mesh.shape["dp"] * mesh.shape["seq"]
    whole_tiles = mesh.shape["seq"] == 4 and mesh.shape["dp"] % 2 == 0 and D // devices == 16
    in_specs = (
        P("seq", "dp", None),
        P("seq", "dp", None),
        P(None, ("dp", "seq"), None),
        P(None, ("dp", "seq"), None),
        P(None, ("dp", "seq"), None),
        P(None, ("dp", "seq"), None),
        P(None, ("dp", "seq")),
        P(None, ("dp", "seq")),
        P(None, None, ("dp", "seq")),
        P("dp"),
        P(),
    )
    out_specs = (
        P("seq", "dp", None),
        P("seq", "dp", None),
        P(None, ("dp", "seq"), None),
        P(None, ("dp", "seq"), None),
        P(None, ("dp", "seq"), None),
        P(None, ("dp", "seq"), None),
        P(None, ("dp", "seq")),
        P(None, ("dp", "seq")),
        P(None, None, ("dp", "seq")),
    )
    return jax.shard_map(
        fused_body if whole_tiles else body, mesh=mesh, in_specs=in_specs, out_specs=out_specs, check_vma=False)
```

```python
import functools
import math

import jax
import jax.numpy as jnp
from jax import lax
from jax.experimental import pallas as pl
from jax.experimental.pallas import tpu as pltpu
from jax.sharding import PartitionSpec as P

D = 512
HEADS = 8
HEAD_DIM = 64
FF = 2048
STEPS = 1000
LAYERS = 2


EPS = 1e-05
HIGH = lax.Precision.HIGHEST


def layer_norm(values, gain_vec, bias_vec):
    centered = values - jnp.mean(values, axis=-1, keepdims=True)
    spread = jnp.mean(centered * centered, axis=-1, keepdims=True)
    return centered * lax.rsqrt(spread + EPS) * gain_vec + bias_vec


def attend(queries, keys_all, values_all):
    row_count, seq_count, model_width = queries.shape
    score_scale = 1.0 / math.sqrt(HEAD_DIM)

    def per_seq(seq_index, loop_state):
        outputs, log_tot = loop_state
        query_per_head = lax.dynamic_index_in_dim(queries, seq_index, 1, keepdims=False).reshape(
            row_count, HEADS, HEAD_DIM
        )
        key_per_head = lax.dynamic_index_in_dim(keys_all, seq_index, 1, keepdims=False).reshape(
            -1, HEADS, HEAD_DIM
        )
        value_per_head = lax.dynamic_index_in_dim(values_all, seq_index, 1, keepdims=False).reshape(
            -1, HEADS, HEAD_DIM
        )
        scores = (
            jnp.einsum(
                "xsv,usv->sxu", query_per_head, key_per_head, preferred_element_type=jnp.float32
            )
            * score_scale
        )
        row_max = jnp.max(scores, axis=-1, keepdims=True)
        expon = jnp.exp(scores - row_max)
        summed = jnp.sum(expon, axis=-1, keepdims=True)
        attention_probability = (expon / summed).astype(jnp.bfloat16)
        attn_out = jnp.einsum(
            "gir,rgo->igo",
            attention_probability,
            value_per_head,
            preferred_element_type=jnp.float32,
        )
        attn_out = attn_out.astype(jnp.bfloat16).reshape(row_count, 1, model_width)
        outputs = lax.dynamic_update_slice_in_dim(outputs, attn_out, seq_index, 1)
        log_tot = lax.dynamic_update_slice_in_dim(
            log_tot, (row_max + jnp.log(summed))[None, :, :, 0], seq_index, 0
        )
        return (outputs, log_tot)

    start_state = (
        jnp.zeros(queries.shape, jnp.bfloat16),
        jnp.zeros((seq_count, HEADS, row_count), jnp.float32),
    )
    return lax.fori_loop(0, seq_count, per_seq, start_state)


def attend_back(queries, keys_all, values_all, log_tot, grad_attn):
    row_count, seq_count, model_width = queries.shape
    key_count = keys_all.shape[0]
    score_scale = 1.0 / math.sqrt(HEAD_DIM)

    def per_seq(seq_index, loop_state):
        grad_query, part_key, part_value = loop_state
        query_per_head = lax.dynamic_index_in_dim(queries, seq_index, 1, keepdims=False).reshape(
            row_count, HEADS, HEAD_DIM
        )
        key_per_head = lax.dynamic_index_in_dim(keys_all, seq_index, 1, keepdims=False).reshape(
            key_count, HEADS, HEAD_DIM
        )
        value_per_head = lax.dynamic_index_in_dim(values_all, seq_index, 1, keepdims=False).reshape(
            key_count, HEADS, HEAD_DIM
        )
        hidden_state_gradient = lax.dynamic_index_in_dim(
            grad_attn, seq_index, 1, keepdims=False
        ).reshape(row_count, HEADS, HEAD_DIM)
        log_seq = lax.dynamic_index_in_dim(log_tot, seq_index, 0, keepdims=False)
        scores = (
            jnp.einsum(
                "xsv,usv->sxu", query_per_head, key_per_head, preferred_element_type=jnp.float32
            )
            * score_scale
        )
        attn_f = jnp.exp(scores - log_seq[:, :, None])
        attention_probability = attn_f.astype(jnp.bfloat16)
        value_part = jnp.einsum(
            "uxo,xuc->ouc",
            attention_probability,
            hidden_state_gradient,
            preferred_element_type=jnp.float32,
        )
        probability_gradient = jnp.einsum(
            "xsv,usv->sxu",
            hidden_state_gradient,
            value_per_head,
            preferred_element_type=jnp.float32,
        )
        row_delta = jnp.sum(probability_gradient * attn_f, axis=-1, keepdims=True)
        score_gradient = (attn_f * (probability_gradient - row_delta)).astype(jnp.bfloat16)
        query_part = (
            jnp.einsum(
                "gir,rgo->igo", score_gradient, key_per_head, preferred_element_type=jnp.float32
            )
            * score_scale
        )
        key_part = (
            jnp.einsum(
                "uxo,xuc->ouc", score_gradient, query_per_head, preferred_element_type=jnp.float32
            )
            * score_scale
        )
        grad_query = lax.dynamic_update_slice_in_dim(
            grad_query, query_part.reshape(row_count, 1, model_width), seq_index, 1
        )
        part_key = lax.dynamic_update_slice_in_dim(
            part_key, key_part.reshape(key_count, 1, model_width), seq_index, 1
        )
        part_value = lax.dynamic_update_slice_in_dim(
            part_value, value_part.reshape(key_count, 1, model_width), seq_index, 1
        )
        return (grad_query, part_key, part_value)

    start_state = (
        jnp.zeros(queries.shape, jnp.float32),
        jnp.zeros(keys_all.shape, jnp.float32),
        jnp.zeros(keys_all.shape, jnp.float32),
    )
    return lax.fori_loop(0, seq_count, per_seq, start_state)


def forward_layer(hidden, fetched, onehot):
    mat_qkv, mat_out, up_matrix, down_matrix, gain_row, bias_row, time_rows = fetched
    gain_f = gain_row.astype(jnp.float32)
    bias_f = bias_row.astype(jnp.float32)
    seq_embed = jnp.dot(onehot.astype(jnp.bfloat16), time_rows, preferred_element_type=jnp.float32)
    summed_in = hidden + seq_embed[None]
    normed_one = layer_norm(summed_in, gain_f[:D], bias_f[4 * D + FF : 5 * D + FF]).astype(
        jnp.bfloat16
    )
    linear = jnp.dot(normed_one, mat_qkv, preferred_element_type=jnp.float32)
    queries = (linear[..., :D] + bias_f[:D]).astype(jnp.bfloat16)
    keys_loc = linear[..., D : 2 * D].astype(jnp.bfloat16)
    values_loc = (linear[..., 2 * D :] + bias_f[D : 2 * D]).astype(jnp.bfloat16)
    keys_all, values_all = (
        lax.all_gather(keys_loc, "seq", axis=0, tiled=True),
        lax.all_gather(values_loc, "seq", axis=0, tiled=True),
    )
    attn_out, log_tot = attend(queries, keys_all, values_all)
    after_attn = (
        summed_in
        + jnp.dot(attn_out, mat_out, preferred_element_type=jnp.float32)
        + bias_f[2 * D : 3 * D]
    )
    second_normalized = layer_norm(after_attn, gain_f[D:], bias_f[5 * D + FF :]).astype(
        jnp.bfloat16
    )
    upward = (
        jnp.dot(second_normalized, up_matrix, preferred_element_type=jnp.float32)
        + bias_f[3 * D : 3 * D + FF]
    )
    gelu_output = jax.nn.gelu(upward).astype(jnp.bfloat16)
    result = (
        after_attn
        + jnp.dot(gelu_output, down_matrix, preferred_element_type=jnp.float32)
        + bias_f[3 * D + FF : 4 * D + FF]
    )
    record = (
        summed_in,
        normed_one,
        queries,
        keys_loc,
        values_loc,
        attn_out,
        log_tot,
        after_attn,
        second_normalized,
        upward,
        gelu_output,
        keys_all,
        values_all,
    )
    return (result, record)


def backward_layer(hidden_state_gradient, fetched, record, onehot, kv_pair):
    mat_qkv = fetched[0]
    mat_out = fetched[1]
    up_matrix = fetched[2]
    down_matrix = fetched[3]
    gain_f = fetched[4].astype(jnp.float32)
    bias_f = fetched[5].astype(jnp.float32)
    summed_in, normed_one, queries = (record[0], record[1], record[2])
    attn_out, log_tot, after_attn = (record[5], record[6], record[7])
    second_normalized, upward, gelu_output = (record[8], record[9], record[10])
    keys_all, values_all = kv_pair
    gradient_bfloat = hidden_state_gradient.astype(jnp.bfloat16)
    down_weight_gradient = jnp.einsum(
        "awt,awg->tg", gelu_output, gradient_bfloat, preferred_element_type=jnp.float32
    )
    bias_down = jnp.sum(hidden_state_gradient, axis=(0, 1))
    activation_gradient = jnp.einsum(
        "ngb,rb->ngr", gradient_bfloat, down_matrix, preferred_element_type=jnp.float32
    )
    _, gelu_back = jax.vjp(jax.nn.gelu, upward)
    grad_upward = gelu_back(activation_gradient)[0]
    bias_up = jnp.sum(grad_upward, axis=(0, 1))
    upward_bfloat = grad_upward.astype(jnp.bfloat16)
    up_weight_gradient = jnp.einsum(
        "xew,xem->wm", second_normalized, upward_bfloat, preferred_element_type=jnp.float32
    )
    second_norm_gradient = jnp.einsum(
        "iyv,tv->iyt", upward_bfloat, up_matrix, preferred_element_type=jnp.float32
    )
    _, second_back = jax.vjp(layer_norm, after_attn, gain_f[D:], bias_f[5 * D + FF :])
    from_second, gain_two, shift_two = second_back(second_norm_gradient)
    grad_mid = hidden_state_gradient + from_second
    mid_bf = grad_mid.astype(jnp.bfloat16)
    grad_out = jnp.einsum("lsc,lsd->cd", attn_out, mid_bf, preferred_element_type=jnp.float32)
    bias_out = jnp.sum(grad_mid, axis=(0, 1))
    grad_attn = jnp.einsum(
        "lsd,cd->lsc", mid_bf, mat_out, preferred_element_type=jnp.float32
    ).astype(jnp.bfloat16)
    grad_query, part_key, part_value = attend_back(
        queries, keys_all, values_all, log_tot, grad_attn
    )
    grad_key, grad_value = (
        lax.psum_scatter(
            part_key.astype(jnp.bfloat16), "seq", scatter_dimension=0, tiled=True
        ).astype(jnp.float32),
        lax.psum_scatter(
            part_value.astype(jnp.bfloat16), "seq", scatter_dimension=0, tiled=True
        ).astype(jnp.float32),
    )
    bias_query = jnp.sum(grad_query, axis=(0, 1))
    bias_value = jnp.sum(grad_value, axis=(0, 1))
    grad_linear = jnp.concatenate([grad_query, grad_key, grad_value], axis=-1).astype(jnp.bfloat16)
    grad_qkv = jnp.einsum(
        "lsc,lse->ce", normed_one, grad_linear, preferred_element_type=jnp.float32
    )
    grad_norm_one = jnp.einsum(
        "lse,ce->lsc", grad_linear, mat_qkv, preferred_element_type=jnp.float32
    )
    _, first_back = jax.vjp(layer_norm, summed_in, gain_f[:D], bias_f[4 * D + FF : 5 * D + FF])
    from_first, gain_one, shift_one = first_back(grad_norm_one)
    grad_in = grad_mid + from_first
    grad_table = jnp.dot(onehot.T, jnp.sum(grad_in, axis=0), precision=HIGH)
    grad_gain = jnp.concatenate([gain_one, gain_two])
    grad_bias = jnp.concatenate(
        [bias_query, bias_value, bias_out, bias_up, bias_down, shift_one, shift_two]
    )
    return (
        grad_in,
        (
            grad_qkv,
            grad_out,
            up_weight_gradient,
            down_weight_gradient,
            grad_gain,
            grad_bias,
            grad_table,
        ),
    )


def body(
    inputs,
    cotangent,
    w_qkv,
    w_out,
    w_up,
    w_down,
    norm_gains,
    biases,
    time_table,
    timesteps,
    importance,
):
    onehot = (timesteps[:, None] == jnp.arange(STEPS, dtype=jnp.int32)[None, :]).astype(jnp.float32)
    seq_weight = jnp.dot(onehot, importance, precision=HIGH)
    hidden = inputs.astype(jnp.float32)
    records = []
    fetched_all = []
    for layer_id in range(LAYERS):
        fetched = (
            lax.all_gather(w_qkv[layer_id], ("dp", "seq"), axis=0, tiled=True),
            lax.all_gather(w_out[layer_id], ("dp", "seq"), axis=0, tiled=True),
            lax.all_gather(w_up[layer_id], ("dp", "seq"), axis=0, tiled=True),
            lax.all_gather(w_down[layer_id], ("dp", "seq"), axis=0, tiled=True),
            lax.all_gather(norm_gains[layer_id], ("dp", "seq"), axis=0, tiled=True),
            lax.all_gather(biases[layer_id], ("dp", "seq"), axis=0, tiled=True),
            lax.all_gather(time_table[layer_id], ("dp", "seq"), axis=1, tiled=True),
        )
        hidden, record = forward_layer(hidden, fetched, onehot)
        records.append(record)
        fetched_all.append(fetched)
    hidden_state_gradient = cotangent.astype(jnp.float32) * seq_weight[None, :, None]
    shards = [None] * LAYERS
    for layer_id in reversed(range(LAYERS)):
        record = records[layer_id]
        fetched = (
            lax.all_gather(w_qkv[layer_id], ("dp", "seq"), axis=0, tiled=True),
            lax.all_gather(w_out[layer_id], ("dp", "seq"), axis=0, tiled=True),
            lax.all_gather(w_up[layer_id], ("dp", "seq"), axis=0, tiled=True),
            lax.all_gather(w_down[layer_id], ("dp", "seq"), axis=0, tiled=True),
            lax.all_gather(norm_gains[layer_id], ("dp", "seq"), axis=0, tiled=True),
            lax.all_gather(biases[layer_id], ("dp", "seq"), axis=0, tiled=True),
            lax.all_gather(time_table[layer_id], ("dp", "seq"), axis=1, tiled=True),
        )
        kv_pair = (
            lax.all_gather(record[3], "seq", axis=0, tiled=True),
            lax.all_gather(record[4], "seq", axis=0, tiled=True),
        )
        hidden_state_gradient, grads = backward_layer(
            hidden_state_gradient, fetched, record, onehot, kv_pair
        )
        shards[layer_id] = (
            lax.psum_scatter(grads[0], ("dp", "seq"), scatter_dimension=0, tiled=True),
            lax.psum_scatter(grads[1], ("dp", "seq"), scatter_dimension=0, tiled=True),
            lax.psum_scatter(grads[2], ("dp", "seq"), scatter_dimension=0, tiled=True),
            lax.psum_scatter(grads[3], ("dp", "seq"), scatter_dimension=0, tiled=True),
            lax.psum_scatter(grads[4], ("dp", "seq"), scatter_dimension=0, tiled=True),
            lax.psum_scatter(grads[5], ("dp", "seq"), scatter_dimension=0, tiled=True),
            lax.psum_scatter(grads[6], ("dp", "seq"), scatter_dimension=1, tiled=True),
        )
    stacked = [
        jnp.stack([shards[layer_id][member] for layer_id in range(LAYERS)]) for member in range(7)
    ]
    return (
        hidden,
        hidden_state_gradient,
        stacked[0],
        stacked[1],
        stacked[2],
        stacked[3],
        stacked[4],
        stacked[5],
        stacked[6],
    )


MESH_ID = pl.DeviceIdType.MESH
LOG2E = 1.4426950408889634
F32 = jnp.float32
BF = jnp.bfloat16
TILE = 256
PAIRS = HEADS // 2
N_SEMS = 256
GELU_A = math.sqrt(2.0 / math.pi)
GELU_B = 0.044715

B_Q, B_V, B_O, B_U, B_D, B_S1, B_S2 = 0, D, 2 * D, 3 * D, 3 * D + FF, 4 * D + FF, 5 * D + FF


def nn(left, right):
    return jnp.dot(left, right, preferred_element_type=F32)


def nt(left, right, precision=None):
    return lax.dot_general(left, right, (((1,), (1,)), ((), ())), preferred_element_type=F32, precision=precision)


def tn(left, right):
    return lax.dot_general(left, right, (((0,), (0,)), ((), ())), preferred_element_type=F32)


def rows_sum(value):
    return jnp.sum(value, axis=0, keepdims=True)


def ln_parts(value):
    centered = value - jnp.mean(value, axis=-1, keepdims=True)
    scale = lax.rsqrt(jnp.mean(centered * centered, axis=-1, keepdims=True) + EPS)
    return centered * scale, scale


def gelu_parts(up):
    square = up * up
    tanh = jnp.tanh(GELU_A * up * (1.0 + GELU_B * square))
    return square, tanh


class Fused:
    def __init__(self, n_z, refs):
        (self.ts, self.imp, self.xin, self.cot, self.wq_i, self.wo_i, self.wu_i, self.wd_i, self.gains_i, self.biases_i, self.tab,
         self.act_o, self.gin_o, self.gq_o, self.go_o, self.gu_o, self.gd_o, self.gg_o, self.gb_o, self.gt_o,
         self.Wq, self.Wo, self.Wu, self.Wd, self.SM, self.TS, self.TT, self.T24, self.TR, self.BV, self.GV, self.BG, self.GG,
         self.TG, self.X, self.N, self.NT, self.Q, self.KV, self.AO, self.LSE, self.DL, self.Y, self.GB, self.DO, self.G,
         self.GN, self.GL, self.ACC, self.OWN, self.PB, self.RB1, self.RB2, self.RB3,
         self.R1, self.R2, self.R3, self.R4, self.SR, self.SX, self.SY,
         self.ssem, self.rsem, self.lsem, self.credit) = refs
        dp, seq = lax.axis_index("dp"), lax.axis_index("seq")
        self.n_z = n_z
        self.dp, self.seq = dp, seq
        self.z, self.x, self.y, self.c = dp // 2, dp % 2, seq // 2, seq % 2
        self.next_sem = 0
        self.next_local = 0
        self.mine = {"z": self.z, "x": self.x, "y": self.y, "c": self.c}
        self.other = {"x": 1 - self.x, "y": 1 - self.y, "c": 1 - self.c}
        self.around = [(self.z + hop) % n_z for hop in range(n_z)]
        n_dp = 2 * n_z
        self.far_z = {hop: (dp + hop) % n_dp // 2 for hop in range(1, n_dp)}
        self.far_x = {hop: (dp + hop) % n_dp % 2 for hop in range(1, n_dp)}
        other_x, other_y = self.z * 2 + self.other["x"], self.other["y"] * 2 + self.c
        self.device = {
            **{("z", hop): (self.around[hop] * 2 + self.x, seq) for hop in range(1, n_z)},
            ("x", 1): (other_x, seq),
            ("y", 1): (dp, other_y),
            ("c", 1): (dp, self.y * 2 + self.other["c"]),
            ("p", 1): (other_x, seq),
            ("p", 2): (dp, other_y),
            ("p", 3): (other_x, other_y),
            **{("d", hop): ((dp + hop) % n_dp, seq) for hop in range(1, n_dp)},
            **{("s", hop): (dp, (seq + hop) % 4) for hop in range(1, 4)},
        }
        self.device = {key: {"dp": there[0], "seq": there[1]} for key, there in self.device.items()}

    def hops(self, dim):
        return [hop for name, hop in self.device if name == dim]

    def enter(self):
        barrier = pltpu.get_barrier_semaphore()
        who = [key for key in self.device if key[0] in "ds"] + [("p", 3)]
        for key in who:
            pl.semaphore_signal(barrier, inc=1, device_id=self.device[key], device_id_type=MESH_ID)
        pl.semaphore_wait(barrier, len(who))

    def remote(self, src, dst, dim, hop=1, number=None):
        if number is None:
            number = self.next_sem
            self.next_sem += 1
        return pltpu.make_async_remote_copy(
            src, dst, self.ssem.at[number], self.rsem.at[number], device_id=self.device[dim, hop], device_id_type=MESH_ID
        )

    def local(self, src, dst):
        number = self.next_local
        self.next_local += 1
        return pltpu.make_async_copy(src, dst, self.lsem.at[number])


class Gather:
    def __init__(self, me, view, order):
        self.copies = []
        done = ""
        for dim in order:
            block = view(*[slice(None) if other in done else me.mine[other] for other in "zxyc"])
            self.copies.append([me.remote(block, block, dim, hop) for hop in me.hops(dim)])
            done += "xy" if dim == "p" else dim

    def start(self, stage):
        if stage:
            self.arrive(stage - 1)
        for copy in self.copies[stage]:
            copy.start()

    def arrive(self, stage=-1):
        for copy in self.copies[stage]:
            copy.wait_recv()

    def drain(self):
        for copies in self.copies:
            for copy in copies:
                copy.wait_send()


class Single:
    def __init__(self, copy):
        self.copy = copy

    def start(self, stage):
        self.copy.start()


class Reduce:
    def __init__(self, me, layer, grad, recv, out, cols, order, number, before):
        self.me, self.layer, self.grad, self.recv, self.out, self.cols, self.order = me, layer, grad, recv, out, cols, order
        self.number, self.before = number, before
        self.first_sem = before.first_sem if before else me.next_sem
        self.last = len(order) - 1
        self.copies = [self.build(stage) for stage in range(len(order))]

    def block(self, fixed):
        return tuple(fixed.get(dim, slice(None)) for dim in "zxyc")

    def kept(self, stage):
        done = "".join("xy" if dim == "p" else dim for dim in self.order[:stage])
        return {dim: self.me.mine[dim] for dim in done}

    def build(self, stage):
        me, dim = self.me, self.order[stage]
        copies = []
        number = self.first_sem + sum(len(me.hops(before)) for before in self.order[:stage])
        for hop in me.hops(dim):
            fixed = self.kept(stage)
            if dim == "z":
                fixed["z"] = me.around[hop]
            elif dim == "p":
                fixed["x"] = me.mine["x"] if hop == 2 else me.other["x"]
                fixed["y"] = me.mine["y"] if hop == 1 else me.other["y"]
            else:
                fixed[dim] = me.other[dim]
            src = self.grad.at[(self.layer, *self.block(fixed), slice(None), self.cols)]
            dst = self.landed(stage, hop).at[(*self.landing(stage, hop), slice(None), self.cols)]
            copies.append(me.remote(src, dst, dim, hop, number + len(copies) if self.before else None))
        return copies

    def landed(self, stage, hop):
        return self.recv[3] if stage == self.last else self.recv[stage]

    def landing(self, stage, hop):
        dim = self.order[stage]
        if stage == self.last:
            return (hop - 1,)
        if dim == "p":
            return (slice(None), hop - 1)
        if dim == "z":
            return (slice(2 * hop - 2, 2 * hop),)
        return ((slice(0, self.me.n_z), slice(None), slice(None)), (slice(None), slice(0, 2)), (slice(0, self.me.n_z),))[stage]

    def start(self, stage):
        me = self.me
        if stage:
            self.add(stage - 1)
            dim = self.order[stage - 1]
            if self.layer == LAYERS - 1:
                for hop in me.hops(dim):
                    pl.semaphore_signal(
                        me.credit.at[self.number, stage - 1], inc=1, device_id=me.device[dim, hop], device_id_type=MESH_ID
                    )
        if stage <= self.last:
            if self.layer < LAYERS - 1:
                pl.semaphore_wait(me.credit.at[self.number, stage], len(me.hops(self.order[stage])))
                for copy in self.before.copies[stage]:
                    copy.wait_send()
            for copy in self.copies[stage]:
                copy.start()

    def add(self, stage):
        me, dim = self.me, self.order[stage]
        for copy in self.copies[stage]:
            copy.wait_recv()
        fixed = self.kept(stage + 1)
        if stage == self.last or dim in "zp":
            where = (self.layer, *self.block(fixed), slice(None), self.cols)
            total = self.grad[where].astype(F32)
            for hop in me.hops(dim):
                total = total + self.landed(stage, hop)[(*self.landing(stage, hop), slice(None), self.cols)].astype(F32)
            if stage == self.last:
                self.out[self.layer, :, self.cols] = total
            else:
                self.grad[where] = total.astype(BF)
            return

        def one(z, carry):
            where = (self.layer, *self.block({**fixed, "z": z}), slice(None), self.cols)
            came = (z, *self.landing(stage, 1)[1:], slice(None), self.cols)
            self.grad[where] = self.grad[where] + self.recv[stage][came]
            return carry

        lax.fori_loop(0, me.n_z, one, 0)

    def drain(self):
        for copies in self.copies:
            for copy in copies:
                copy.wait_send()


def at_step(index, hooks):
    for when, action in hooks:
        pl.when(index == when)(action)


BACKWARD_AT = (21, 0)
END_AT = 42
GATHER = (
    ("pzc", 5, 6, 11),
    ("pzc", 0, 5, 11),
    ("zpc", 0, 3, 11),
    ("zpc", 0, 4, 10),
    ("pzc", 0, 10, 20),
    ("zpc", 0, 5, 19),
    ("zpc", 6, 14, 20),
    ("zpc", 11, 15, 23),
    ("zyxc", 0, 5, 8, 17),
    ("zpc", 4, 7, 21),
    ("pzc", 8, 15, 25),
    ("zpc", 12, 15, 25),
    ("zpc", 1, 18, 31),
    ("zpc", 12, 18, 37),
    ("zpc", 13, 22, 33),
    ("pzc", 8, 15, 34),
    ("zpc", 12, 28, 38),
    ("pzc", 21, 28, 38),
    ("pzc", 0, 4, 6),
    ("zpc", 2, 5, 7),
    ("y", 0),
    ("y", 33),
)
REDUCE = (
    ("cpz", 10, 15, 26, 32),
    ("cxzy", 5, 12, 18, 26, 42),
    ("cpz", 2, 6, 14, 32),
    ("cxzy", 8, 11, 15, 31, 43),
    ("cpz", 6, 10, 12, 40),
    ("cpz", 11, 12, 32, 42),
    ("cpz", 15, 15, 23, 40),
    ("cpz", 15, 15, 32, 34),
    ("cpz", 21, 24, 32, 35),
    ("cpz", 17, 21, 33, 41),
    ("cpz", 26, 28, 33, 42),
    ("cxzy", 30, 33, 36, 44, 46),
    ("cpz", 23, 25, 35, 43),
    ("cxzy", 28, 31, 34, 44, 46),
    ("cpz", 32, 36, 42, 44),
    ("cpz", 29, 35, 44, 46),
    ("cpz", 36, 37, 42, 44),
    ("cpz", 36, 36, 39, 43),
    ("cpz", 37.25, 38, 42, 44),
    ("cpz", 37.5, 38, 42, 44),
    ("y", 40),
)

SMALL, TIMES = "small", "times"


def pieces(name, layer):
    return 4 if name == "q" and layer == 0 else 2


def by_place(moves, plan):
    timeline = {}
    for move, (_, *places) in zip(moves, plan, strict=True):
        for stage, place in enumerate(places):
            timeline.setdefault(place, []).append((move, stage))
    return timeline


def fused_kernel(n_z, *refs):
    me = Fused(n_z, refs)
    x, y, z, c = me.x, me.y, me.z, me.c
    n_dp = 2 * n_z
    spare = slice(None)

    mats = ((me.wq_i, me.Wq), (me.wo_i, me.Wo), (me.wu_i, me.Wu), (me.wd_i, me.Wd))
    loads = [me.local(src.at[layer], dst.at[layer, z, x, y, c]) for layer in range(LAYERS) for src, dst in mats]
    for load in loads:
        load.start()
    own_tokens = [
        me.local(src.at[seq], dst.at[tile]) for src, dst in ((me.xin, me.DO), (me.cot, me.GB)) for seq, tile in ((y, 0), (2, 2))
    ]
    for load in own_tokens:
        load.start()

    row = lax.broadcasted_iota(jnp.int32, (32, 128), 0)
    steps = jnp.zeros((32, 128), jnp.int32)
    for j in range(3):
        steps = jnp.where(row == 3 * me.dp + j, me.ts[j], steps)
    me.TT[z, x] = steps

    def choose(rows, cols, first):
        here = lax.broadcasted_iota(jnp.int32, (rows, cols), 1) == first + lax.broadcasted_iota(jnp.int32, (rows, cols), 0)
        return here.astype(F32)

    own_biases, own_gains = choose(160, 640, 160 * me.seq), choose(32, 128, 32 * me.seq)
    own_lanes = choose(16, 128, 16 * (4 * x + me.seq))
    spread_b = nn(me.biases_i[...].astype(F32), own_biases)
    spread_g = nn(me.gains_i[...].astype(F32), own_gains)
    rows = []
    for layer in range(LAYERS):
        rows += [spread_b[layer : layer + 1, 128 * r : 128 * r + 128] for r in range(5)] + [spread_g[layer : layer + 1]]
    me.SM[z, x, y, c] = jnp.concatenate(rows + [jnp.zeros((16 - 6 * LAYERS, 128), F32)], axis=0).astype(BF)
    me.BG[...] = jnp.zeros_like(me.BG)
    me.GG[...] = jnp.zeros_like(me.GG)

    me.enter()
    for load in loads:
        load.wait()

    def weight(layer, ref, order, cols):
        return Gather(me, lambda *where: ref.at[(layer, *where, spare, cols)], order)

    grads = {"q": me.Wq, "o": me.Wo, "u": me.Wu, "d": me.Wd}

    steps_all = Gather(me, lambda gz, gx, gy, gc: me.TT.at[gz, gx], "d")
    token_in = me.remote(me.xin.at[me.other["y"]], me.DO.at[1], "y")
    cot_in = me.remote(me.cot.at[me.other["y"]], me.GB.at[1], "y")
    moves = {}
    plan = iter(GATHER)
    for layer in range(LAYERS):
        for name, ref in grads.items():
            width = ref.shape[-1] // pieces(name, layer)
            for part in range(pieces(name, layer)):
                moves[name, part, layer] = weight(layer, ref, next(plan)[0], slice(width * part, width * (part + 1)))
    moves[SMALL] = small = Gather(me, lambda *where: me.SM.at[where], next(plan)[0])
    moves[TIMES] = times = Gather(me, lambda *where: me.TS.at[where], next(plan)[0])
    timeline = by_place([*moves.values(), Single(token_in), Single(cot_in)], GATHER)

    def have(names, layer):
        for name in names:
            for part in range(pieces(name, layer)):
                moves[name, part, layer].arrive()

    def fire(place):
        for move, stage in timeline.get(place, ()):
            move.start(stage)

    def fires(first, count):
        return [(i, functools.partial(fire, first + i)) for i in range(count) if first + i in timeline]

    steps_all.start(0)
    fire(0)
    fire(1)
    steps_all.arrive()
    t24 = jnp.sum(me.TT[...].reshape(n_dp, 32, 128), axis=0)
    me.T24[...] = t24
    hot = (t24[:, 0:1] == lax.broadcasted_iota(jnp.int32, (32, STEPS), 1)).astype(F32).astype(BF)
    picked = jnp.concatenate([nt(hot, me.tab[layer])[:24] for layer in range(LAYERS)], axis=0).astype(BF)
    me.TS[z, x, y, c] = nn(picked, own_lanes.astype(BF)).astype(BF)
    for place in range(2, 11):
        fire(place)

    small.arrive()
    for gz in range(n_z):
        for gx in range(2):
            block = jnp.sum(me.SM[gz, gx].reshape(4, 16, 128).astype(F32), axis=0)
            dp = 2 * gz + gx
            for layer in range(LAYERS):
                for r in range(5):
                    at = (5 * dp + r) * 128
                    me.BV[layer, :, at : at + 128] = block[6 * layer + r : 6 * layer + r + 1]
                me.GV[layer, :, 128 * dp : 128 * dp + 128] = block[6 * layer + 5 : 6 * layer + 6]
    times.arrive()
    slabs = jnp.concatenate(
        [jnp.sum(me.TS[gz].reshape(8, 48, 128).astype(F32), axis=0) for gz in range(n_z)], axis=1
    ).astype(BF)
    r8 = lax.broadcasted_iota(jnp.int32, (16, 48), 0)
    c48 = lax.broadcasted_iota(jnp.int32, (16, 48), 1)
    for layer in range(LAYERS):
        base = 24 * layer + 3 * me.dp
        pick = ((r8 == 0) & (c48 == base + y)) | ((r8 == 1) & (c48 == base + 2))
        me.TR[layer] = nn(pick.astype(F32).astype(BF), slabs)[:8]

    def time_row(layer, tile):
        return me.TR[layer, 1:2, :] if tile == 2 else me.TR[layer, 0:1, :]

    def bias(layer, at, width=D):
        return me.BV[layer, :, at : at + width]

    for load in own_tokens:
        load.wait()
    for tile in (0, 2):
        me.X[0, tile] = me.DO[tile].astype(F32) + time_row(0, tile)

    sends = [token_in, cot_in]

    def send(src, dst, dim):
        copy = me.remote(src, dst, dim)
        sends.append(copy)
        return copy

    def attention_norm(layer, tile):
        hat, _ = ln_parts(me.X[layer, tile])
        return (hat * me.GV[layer, :, :D] + bias(layer, B_S1)).astype(BF)

    def columns(layer, normed, j):
        return nn(normed, me.Wq[layer, :, :, :, :, :, D * j : D * j + D].reshape(D, D))

    def keys_values(layer, normed, slot):
        me.KV[layer, 0, slot] = columns(layer, normed, 1).astype(BF)
        me.KV[layer, 1, slot] = (columns(layer, normed, 2) + bias(layer, B_V)).astype(BF)

    low_lanes = lax.broadcasted_iota(jnp.int32, (TILE, 128), 1) < HEAD_DIM

    def two_heads(pair):
        zero = jnp.zeros_like(pair)
        return jnp.concatenate([jnp.where(low_lanes, pair, zero), jnp.where(low_lanes, zero, pair)], axis=0)

    def attend_two(layer, step):
        tile, base = step // 2, step // 4 * 4
        first = step % 2 * 2
        cols = [pl.ds(pl.multiple_of((first + i) * 128, 128), 128) for i in range(2)]
        queries = [two_heads(me.Q[layer, tile, :, cols[i]]) for i in range(2)]

        def block(which, part, i):
            return me.KV[layer, which, pl.ds(base + 2 * part, 2), :, cols[i]].reshape(2 * TILE, 128)

        def scores(part, i):
            return nt(block(0, part, i), queries[i])

        def highest(parts):
            tops = [jnp.max(part, axis=0, keepdims=True) for part in parts]
            return jnp.maximum(tops[0], tops[1]) * LOG2E

        def mix(score, top, part, i):
            values = jnp.concatenate([block(1, part, i).T, jnp.ones((16, 2 * TILE), BF)], axis=0)
            return nn(values, jnp.exp2(score * LOG2E - top).astype(BF))

        def finish(mixed, top, i):
            total = mixed[128:129]
            mixed = mixed[:128] * (1.0 / total)
            me.LSE[layer, tile, first + i] = top + jnp.log2(total)
            out = jnp.concatenate([mixed[:HEAD_DIM, :TILE], mixed[HEAD_DIM:, TILE:]], axis=0)
            me.AO[layer, tile, :, cols[i]] = out.T.astype(BF)

        now = [scores(0, 0), scores(1, 0)]
        top = highest(now)
        later, mixed = [], 0.0
        for part in range(2):
            later.append(scores(part, 1))
            mixed = mixed + mix(now[part], top, part, 0)
        finish(mixed, top, 0)
        top = highest(later)
        finish(mix(later[0], top, 0, 1) + mix(later[1], top, 1, 1), top, 1)

    kv = me.KV
    to_y = [me.remote(me.N.at[2], me.PB.at[0, layer], "y") for layer in range(LAYERS)]
    on_c = [send(kv.at[layer, :, 5], kv.at[layer, :, 7], "c") for layer in range(LAYERS)]
    to_c = [
        [send(kv.at[layer, :, a], kv.at[layer, :, b], "c") for a, b in ((0, 2), (1, 3), (4, 6))] for layer in range(LAYERS)
    ]

    def announce(layer):
        me.N[2] = attention_norm(layer, 2)
        to_y[layer].start()

    def project(layer, tile):
        normed = me.N[2] if tile == 2 else attention_norm(layer, tile)
        keys_values(layer, normed, 4 if tile == 2 else tile)
        to_c[layer][tile].start()
        queries = (columns(layer, normed, 0) + bias(layer, B_Q)).astype(BF)
        me.Q[layer, tile] = queries * jnp.asarray(1.0 / math.sqrt(HEAD_DIM), BF)

    def neighbour(layer):
        to_y[layer].wait_recv()
        keys_values(layer, me.PB[0, layer], 5)
        on_c[layer].start()

    def attention(layer, first, last, place):
        def step(index, carry):
            at_step(index - first, fires(place, last - first))
            attend_two(layer, index)
            return carry

        lax.fori_loop(first, last, step, 0)

    def rest(layer, tiles, place):
        if tiles[0] == 0:
            have("o", layer)
        fire(place)
        w_out = me.Wo[layer].reshape(D, D)
        for tile in tiles:
            after = me.X[layer, tile] + nn(me.AO[layer, tile], w_out) + bias(layer, B_O)
            me.Y[layer, tile] = after
            hat, _ = ln_parts(after)
            me.N[tile] = (hat * me.GV[layer, :, D:] + bias(layer, B_S2)).astype(BF)
            me.GN[tile] = after + bias(layer, B_D)
        if tiles[0] == 0:
            have("ud", layer)

        def ffn(half, carry):
            at_step(half, fires(place + 1, 2))
            cols = pl.ds(pl.multiple_of(half * (FF // 2), FF // 2), FF // 2)
            w_up = me.Wu[layer, :, :, :, :, :, cols].reshape(D, FF // 2)
            w_down = me.Wd[layer, pl.ds(half * (n_z // 2), n_z // 2)].reshape(FF // 2, D)
            b_up = me.BV[layer, :, pl.ds(pl.multiple_of(B_U + half * (FF // 2), D), FF // 2)]
            for tile in tiles:
                up = nn(me.N[tile], w_up) + b_up
                _, tanh = gelu_parts(up)
                me.GN[tile] += nn((0.5 * up * (1.0 + tanh)).astype(BF), w_down)
            return carry

        lax.fori_loop(0, 2, ffn, 0)

    def third_keys(layer):
        to_y[layer].wait_send()
        to_c[layer][2].wait_recv()
        on_c[layer].wait_recv()

    announce(0)
    fire(11)
    have("q", 0)
    project(0, 2)
    fire(12)
    project(0, 0)
    fire(13)
    token_in.wait_recv()
    me.X[0, 1] = me.DO[1].astype(F32) + time_row(0, 1)
    project(0, 1)
    fire(14)
    neighbour(0)
    to_c[0][0].wait_recv()
    to_c[0][1].wait_recv()
    for layer in range(LAYERS):
        at = (15, 30)[layer]
        attention(layer, 0, 4, at)
        fire(at + 4)
        if layer:
            neighbour(layer)
        fire(at + 5)
        third_keys(layer)
        attention(layer, 4, 6, at + 6)
        rest(layer, (0, 1, 2), at + 8)
        if layer == 0:
            for tile in range(3):
                me.X[1, tile] = me.GN[tile] + time_row(1, tile)
            announce(1)
            fire(26)
            have("q", 1)
            for turn, tile in enumerate((2, 0, 1)):
                project(1, tile)
                fire(27 + turn)
            to_c[1][0].wait_recv()
            to_c[1][1].wait_recv()
    act_out = [
        me.local(me.DO.at[0], me.act_o.at[y]), me.remote(me.DO.at[1], me.act_o.at[y], "y"), me.local(me.DO.at[2], me.act_o.at[2])
    ]
    for tile in range(3):
        me.DO[tile] = me.GN[tile].astype(BF)
    for copy in act_out:
        copy.start()

    cot_in.wait_recv()
    weight_y, weight_2 = me.imp[me.ts[y]], me.imp[me.ts[2]]
    for tile in range(3):
        grad = me.GB[tile].astype(F32) * (weight_2 if tile == 2 else weight_y)
        me.G[tile] = grad
    for part in [steps_all, *moves.values()]:
        part.drain()
    for copy in sends:
        copy.wait_send()
    sends.clear()

    outs = {"q": me.gq_o, "o": me.go_o, "u": me.gu_o, "d": me.gd_o}
    recvs = {
        name: [me.R1[i], me.R2[i], me.R3[i], me.R4[i]] for i, name in enumerate("qoud")
    }

    spans = {
        "d": ("d", 0, D), "u": ("u", 0, FF), "o": ("o", 0, D), "p": ("q", 0, D), "q": ("q", D, 3 * D)
    }

    plan = iter(REDUCE)

    def piece(layer, number, name, half):
        kind, begin, end = spans[name]
        width = (end - begin) // 2
        start = begin + width * half
        before = sums[number] if layer < LAYERS - 1 else None
        cols = slice(start, start + width)
        return Reduce(me, layer, grads[kind], recvs[kind], outs[kind], cols, next(plan)[0], number, before)

    def add_bias(layer, at, value):
        me.BG[layer, :, at : at + value.shape[-1]] += value

    def ln_back(layer, gain_at, shift_at, source, grad):
        hat, scale = ln_parts(source)
        me.GG[layer, :, gain_at : gain_at + D] += rows_sum(grad * hat)
        add_bias(layer, shift_at, rows_sum(grad))
        inner = grad * me.GV[layer, :, gain_at : gain_at + D]
        return scale * (inner - jnp.mean(inner, axis=-1, keepdims=True) - hat * jnp.mean(inner * hat, axis=-1, keepdims=True))

    def normed_t(layer, source, gain_at, shift_at):
        for tile in range(3):
            hat, _ = ln_parts(source[layer, tile])
            normed = (hat * me.GV[layer, :, gain_at : gain_at + D] + bias(layer, shift_at)).astype(BF)
            me.N[tile] = normed
            me.NT[:, TILE * tile : TILE * tile + TILE] = normed.T

    head_of = lax.broadcasted_iota(jnp.int32, (HEADS, D), 1) // HEAD_DIM
    selector = (head_of == lax.broadcasted_iota(jnp.int32, (HEADS, D), 0)).astype(F32)

    def backward(layer, before_out, tail):
        base = BACKWARD_AT[layer]
        normed_t(layer, me.Y, D, B_S2)
        for tile in range(3):
            me.GB[tile] = me.G[tile].astype(BF)
            add_bias(layer, B_D, rows_sum(me.G[tile]))
            me.GN[tile] = jnp.zeros((TILE, D), F32)

        def ffn(slab, carry):
            at_step(slab, fires(base, n_z))
            cols = pl.ds(pl.multiple_of(slab * D, D), D)
            b_cols = pl.ds(pl.multiple_of(B_U + slab * D, D), D)
            w_up = me.Wu[layer, :, :, :, :, :, cols].reshape(D, D)
            w_down = me.Wd[layer, slab].reshape(D, D)
            grads_h = me.GB[...].reshape(3 * TILE, D)
            up = nn(me.N[...].reshape(3 * TILE, D), w_up) + me.BV[layer, :, b_cols]
            square, tanh = gelu_parts(up)
            active = (0.5 * up * (1.0 + tanh)).astype(BF)
            slope = 0.5 * (1.0 + tanh) + (0.5 * GELU_A) * up * (1.0 - tanh * tanh) * (1.0 + 3.0 * GELU_B * square)
            grad_up = nt(grads_h, w_down) * slope
            me.BG[layer, :, b_cols] += rows_sum(grad_up)
            grad_up = grad_up.astype(BF)
            me.GN[...] += nt(grad_up, w_up).reshape(3, TILE, D)
            me.Wd[layer, slab] = tn(active, grads_h).astype(BF).reshape(2, 2, 2, 64, D)
            me.Wu[layer, :, :, :, :, :, cols] = nn(me.NT[...], grad_up).astype(BF).reshape(n_z, 2, 2, 2, 16, D)
            return carry

        lax.fori_loop(0, n_z, ffn, 0)
        fire(base + 4)
        for tile in range(3):
            mid = me.G[tile] + ln_back(layer, D, B_S2, me.Y[layer, tile], me.GN[tile])
            me.G[tile] = mid
            add_bias(layer, B_O, rows_sum(mid))
            me.GB[tile] = mid.astype(BF)
        fire(base + 5)
        before_out()
        w_out = me.Wo[layer].reshape(D, D)
        me.DO[...] = nt(me.GB[...].reshape(3 * TILE, D), w_out).astype(BF).reshape(3, TILE, D)
        for tile in range(3):
            delta = nt(selector, me.DO[tile].astype(F32) * me.AO[layer, tile].astype(F32), lax.Precision.HIGHEST)
            for pair in range(PAIRS):
                both = jnp.concatenate([delta[2 * pair : 2 * pair + 1], delta[2 * pair + 1 : 2 * pair + 2]], axis=1)
                me.DL[tile, pair] = both
        d_out = tn(me.AO[layer].reshape(3 * TILE, D), me.GB[...].reshape(3 * TILE, D))
        me.Wo[layer] = d_out.astype(BF).reshape(n_z, 2, 2, 2, 16, D)
        fire(base + 6)

        me.ACC[...] = jnp.zeros_like(me.ACC)
        third_c = send(me.PB, me.RB1, "c")
        third_y = me.remote(me.GL.at[2, :, D:], me.RB2, "y")
        from_c = me.remote(me.GL.at[0:2, :, D:], me.RB3, "c")

        def third_done():
            me.OWN[...] = me.ACC[:, 0:TILE]
            for i in range(2):
                me.GL[2, :, D * (1 + i) : D * (2 + i)] = me.ACC[i, TILE : 2 * TILE].astype(BF)
            me.PB[...] = me.ACC[:, 2 * TILE :].reshape(2, 2, TILE, D).astype(BF)
            me.ACC[...] = jnp.zeros_like(me.ACC)
            third_c.start()

        def third_on():
            third_c.wait_recv()
            me.OWN[...] += me.RB1[:, 0].astype(F32)
            for i in range(2):
                cols = slice(D * (1 + i), D * (2 + i))
                me.GL[2, :, cols] = me.GL[2, :, cols] + me.RB1[i, 1]
            third_y.start()

        def attend_back(step, carry):
            at_step(step, [(2, third_done), (3, third_on)] + fires(base + 8, 6))
            tile = (step // 2 + 2) % 3
            slot = tile // 2 * 4
            for i in range(2):
                pair = step % 2 * 2 + i
                cols = pl.ds(pl.multiple_of(pair * 128, 128), 128)
                queries, grads_o = two_heads(me.Q[layer, tile, :, cols]), two_heads(me.DO[tile, :, cols])
                log_sum, delta = me.LSE[layer, tile, pair], me.DL[tile, pair]
                d_query = jnp.zeros((128, 2 * TILE), F32)
                for part in range(4):
                    keys, values = me.KV[layer, 0, slot + part, :, cols], me.KV[layer, 1, slot + part, :, cols]
                    rows = slice(TILE * part, TILE * part + TILE)
                    prob = jnp.exp2(nt(keys, queries) * LOG2E - log_sum)
                    grad_s = (prob * (nt(values, grads_o) - delta)).astype(BF)
                    me.ACC[1, rows, cols] += nn(prob.astype(BF), grads_o)
                    me.ACC[0, rows, cols] += nn(grad_s, queries)
                    d_query = d_query + nn(keys.T, grad_s)
                d_query = jnp.concatenate([d_query[:HEAD_DIM, :TILE], d_query[HEAD_DIM:, TILE:]], axis=0).T
                d_query = d_query * (1.0 / math.sqrt(HEAD_DIM))
                me.BG[layer, :, cols] += rows_sum(d_query)
                me.GL[tile, :, cols] = d_query.astype(BF)
            return carry

        fire(base + 7)
        lax.fori_loop(0, 6, attend_back, 0)
        for tile in range(2):
            for i in range(2):
                rows = slice(TILE * (2 + tile), TILE * (3 + tile))
                me.GL[tile, :, D * (1 + i) : D * (2 + i)] = me.ACC[i, rows].astype(BF)
        from_c.start()
        normed_t(layer, me.X, 0, B_S1)
        fire(base + 14)

        def qkv_back(first, last):
            w_qkv = me.Wq[layer, :, :, :, :, :, first:last].reshape(D, last - first)
            part = nt(me.GL[:, :, first:last].reshape(3 * TILE, last - first), w_qkv).reshape(3, TILE, D)
            me.GN[...] = part if first == 0 else me.GN[...] + part
            for j in range(first, last, D):
                d_qkv = nn(me.NT[...], me.GL[:, :, j : j + D].reshape(3 * TILE, D))
                me.Wq[layer, :, :, :, :, :, j : j + D] = d_qkv.astype(BF).reshape(n_z, 2, 2, 2, 16, D)

        qkv_back(0, D)
        fire(base + 15)
        from_c.wait()
        for tile in range(2):
            rows = slice(TILE * tile, TILE * tile + TILE)
            key = me.ACC[0, rows] + me.RB3[tile, :, :D].astype(F32)
            value = me.ACC[1, rows] + me.RB3[tile, :, D:].astype(F32)
            add_bias(layer, B_V, rows_sum(value))
            me.GL[tile, :, D : 2 * D] = key.astype(BF)
            me.GL[tile, :, 2 * D :] = value.astype(BF)
        third_y.wait()
        third = [me.OWN[i] + me.RB2[:, D * i : D * i + D].astype(F32) for i in range(2)]
        me.GL[2, :, D : 2 * D] = third[0].astype(BF)
        me.GL[2, :, 2 * D :] = third[1].astype(BF)
        add_bias(layer, B_V, rows_sum(third[1]))
        fire(base + 16)
        qkv_back(D, 2 * D)
        fire(base + 16.25)
        qkv_back(2 * D, 3 * D)
        fire(base + 16.5)
        fire(base + 17)
        totals = []
        for tile in (1, 0, 2):
            grad = me.G[tile] + ln_back(layer, 0, B_S1, me.X[layer, tile], me.GN[tile])
            me.G[tile] = grad
            totals.append(rows_sum(grad))
            tail(tile, grad)
            fire(base + 17 + len(totals))
        me.TG[layer, 0:1] = totals[0] + totals[1]
        me.TG[layer, 1:2] = totals[2]
        for copy in sends:
            copy.wait_send()
        sends.clear()

    sums = []
    for layer in reversed(range(LAYERS)):
        for number, (name, half) in enumerate((name, half) for name in spans for half in range(2)):
            sums.append(piece(layer, number, name, half))
    timeline.clear()
    gin_out = me.remote(me.GB.at[1], me.gin_o.at[y], "y")
    timeline.update(by_place([*sums, Single(gin_out)], REDUCE))

    def act_done():
        for copy in act_out:
            copy.wait()

    backward(1, act_done, lambda tile, grad: None)
    finals = []

    def out_tile(tile, grad):
        me.GB[tile] = grad.astype(BF)
        if tile != 1:
            finals.append(me.local(me.GB.at[tile], me.gin_o.at[y if tile == 0 else 2]))
            finals[-1].start()

    backward(0, lambda: None, out_tile)

    for gz in range(n_z):
        lanes = slice(128 * gz, 128 * gz + 128)
        for gx in range(2):
            dp = 2 * gz + gx
            for layer in range(LAYERS):
                for r in range(5):
                    at_lane = (5 * dp + r) * 128
                    me.SR[gz, gx, 6 * layer + r : 6 * layer + r + 1] = me.BG[layer, :, at_lane : at_lane + 128]
                me.SR[gz, gx, 6 * layer + 5 : 6 * layer + 6] = me.GG[layer, :, 128 * dp : 128 * dp + 128]
                me.SR[gz, gx, 12 + 2 * layer : 14 + 2 * layer] = me.TG[layer, 0:2, lanes]
    to_dp = [
        me.remote(me.SR.at[me.far_z[hop], me.far_x[hop]], me.SX.at[me.dp], "d", hop) for hop in me.hops("d")
    ]
    for copy in to_dp:
        copy.start()
    me.SX[me.dp] = me.SR[z, x]
    fire(END_AT)
    for copy in to_dp:
        copy.wait_recv()
    fire(END_AT + 1)
    me.SY[0, 0:16] = jnp.sum(me.SX[...], axis=0)
    for dp in range(n_dp):
        for layer in range(LAYERS):
            at_row = 16 + 24 * layer + 3 * dp
            first_seq = me.SX[dp, 12 + 2 * layer : 13 + 2 * layer]
            me.SY[0, at_row : at_row + 1] = jnp.where(y == 0, first_seq, 0.0)
            me.SY[0, at_row + 1 : at_row + 2] = jnp.where(y == 1, first_seq, 0.0)
            me.SY[0, at_row + 2 : at_row + 3] = me.SX[dp, 13 + 2 * layer : 14 + 2 * layer]
    to_seq = [me.remote(me.SY.at[0], me.SY.at[hop], "s", hop) for hop in me.hops("s")]
    for copy in to_seq:
        copy.start()
    fire(END_AT + 2)
    for copy in to_seq:
        copy.wait_recv()
    fire(END_AT + 3)
    total = me.SY[0] + me.SY[1] + me.SY[2] + me.SY[3]
    hot = (me.T24[0:24, 0:1] == lax.broadcasted_iota(jnp.int32, (24, STEPS), 1)).astype(F32)
    for layer in range(LAYERS):
        bias_row = jnp.concatenate([total[6 * layer + r : 6 * layer + r + 1] for r in range(5)], axis=1)
        me.gb_o[layer : layer + 1] = nt(bias_row, own_biases, HIGH)
        me.gg_o[layer : layer + 1] = nt(total[6 * layer + 5 : 6 * layer + 6], own_gains, HIGH)
        by_seq = nt(own_lanes, total[16 + 24 * layer : 40 + 24 * layer], HIGH)
        me.gt_o[layer] = jnp.dot(by_seq, hot, precision=HIGH, preferred_element_type=F32)
    fire(END_AT + 4)

    for copy in to_dp + to_seq:
        copy.wait_send()
    for copy in [gin_out, *finals]:
        copy.wait()
    for part in sums[len(sums) // 2 :]:
        part.drain()


def fused_call(n_z, *operands):
    any_space, vmem, smem = (pl.BlockSpec(memory_space=space) for space in (pl.ANY, pltpu.VMEM, pltpu.SMEM))
    cube = (n_z, 2, 2, 2)
    tokens = (3, TILE, D)
    sizes = ((16, 3 * D), (16, D), (16, FF), (64, D))

    def many(lead):
        return [tuple(pltpu.VMEM((*lead, *size), BF) for size in sizes)]

    flat, tree = jax.tree.flatten(
        [pltpu.VMEM((LAYERS, *cube, *size), BF) for size in sizes]
        + [
            pltpu.VMEM((*cube, 16, 128), BF),
            pltpu.VMEM((*cube, 48, 128), BF),
            pltpu.VMEM((n_z, 2, 32, 128), jnp.int32),
            pltpu.VMEM((32, 128), jnp.int32),
            pltpu.VMEM((LAYERS, 8, D), F32),
            pltpu.VMEM((LAYERS, 1, 6 * D + FF), F32),
            pltpu.VMEM((LAYERS, 1, 2 * D), F32),
            pltpu.VMEM((LAYERS, 1, 6 * D + FF), F32),
            pltpu.VMEM((LAYERS, 1, 2 * D), F32),
            pltpu.VMEM((LAYERS, 8, D), F32),
            pltpu.VMEM((LAYERS, *tokens), F32),
            pltpu.VMEM(tokens, BF),
            pltpu.VMEM((D, 3 * TILE), BF),
            pltpu.VMEM((LAYERS, *tokens), BF),
            pltpu.VMEM((LAYERS, 2, 8, TILE, D), BF),
            pltpu.VMEM((LAYERS, *tokens), BF),
            pltpu.VMEM((LAYERS, 3, PAIRS, 1, 2 * TILE), F32),
            pltpu.VMEM((3, PAIRS, 1, 2 * TILE), F32),
            pltpu.VMEM((LAYERS, *tokens), F32),
            pltpu.VMEM(tokens, BF),
            pltpu.VMEM(tokens, BF),
            pltpu.VMEM(tokens, F32),
            pltpu.VMEM(tokens, F32),
            pltpu.VMEM((3, TILE, 3 * D), BF),
            pltpu.VMEM((2, 4 * TILE, D), F32),
            pltpu.VMEM((2, TILE, D), F32),
            pltpu.VMEM((2, 2, TILE, D), BF),
            pltpu.VMEM((2, 2, TILE, D), BF),
            pltpu.VMEM((TILE, 2 * D), BF),
            pltpu.VMEM((2, TILE, 2 * D), BF),
        ]
        + many((n_z, 2, 2))
        + many((n_z, 3))
        + many((2 * n_z - 2,))
        + many((n_z - 1,))
        + [
            pltpu.VMEM((n_z, 2, 16, 128), F32),
            pltpu.VMEM((2 * n_z, 16, 128), F32),
            pltpu.VMEM((4, 64, 128), F32),
            pltpu.SemaphoreType.DMA((N_SEMS,)),
            pltpu.SemaphoreType.DMA((N_SEMS,)),
            pltpu.SemaphoreType.DMA((32,)),
            pltpu.SemaphoreType.REGULAR((10, 4)),
        ]
    )
    outs = [
        jax.ShapeDtypeStruct(tokens, BF),
        jax.ShapeDtypeStruct(tokens, BF),
        *[jax.ShapeDtypeStruct((LAYERS, *size), F32) for size in sizes],
        jax.ShapeDtypeStruct((LAYERS, 32), F32),
        jax.ShapeDtypeStruct((LAYERS, 160), F32),
        jax.ShapeDtypeStruct((LAYERS, 16, STEPS), F32),
    ]

    def run(*refs):
        head = len(operands) + len(outs)
        fused_kernel(n_z, *refs[:head], *jax.tree.unflatten(tree, refs[head:]))

    return pl.pallas_call(
        run,
        out_shape=outs,
        in_specs=[smem, smem] + [any_space] * 6 + [vmem] * 3,
        out_specs=[any_space] * 2 + [vmem] * 7,
        scratch_shapes=flat,
        compiler_params=pltpu.CompilerParams(collective_id=0, has_side_effects=True, vmem_limit_bytes=VMEM_BYTES),
    )(*operands)


VMEM_BYTES = 67_000_000


def fused_body(
    inputs, cotangent, w_qkv, w_out, w_up, w_down, norm_gains, biases, time_table, timesteps, importance
):
    act, grad_in, g_qkv, g_out, g_up, g_down, grad_gains, grad_biases, grad_table = fused_call(
        lax.axis_size("dp") // 2, timesteps, importance, jnp.swapaxes(inputs, 0, 1), jnp.swapaxes(cotangent, 0, 1),
        w_qkv, w_out, w_up, w_down, norm_gains, biases, jnp.swapaxes(time_table, 1, 2),
    )
    act, grad_in, *rest = finish_call((act, grad_in), (g_qkv, g_out, g_up, g_down, grad_gains, grad_biases, grad_table))
    return (jnp.swapaxes(act, 0, 1), jnp.swapaxes(grad_in, 0, 1), *rest[:-1], jnp.swapaxes(rest[-1], 1, 2))


def finish_kernel(n_wide, n_same, *refs):
    ins, outs = refs[: n_wide + n_same], refs[n_wide + n_same :]
    for source, target in zip(ins[:n_wide], outs[:n_wide]):
        target[...] = source[...].astype(F32)

    def hand_on():
        for source, target in zip(ins[n_wide:], outs[n_wide:]):
            target[...] = source[...]

    pl.when(pl.program_id(0) == 0)(hand_on)


def finish_call(wide, same):
    tile = pl.BlockSpec((1, TILE, D), lambda i: (i, 0, 0))
    whole = [pl.BlockSpec(array.shape, lambda i, rank=array.ndim: (0,) * rank) for array in same]
    return pl.pallas_call(
        functools.partial(finish_kernel, len(wide), len(same)),
        grid=(3,),
        out_shape=[jax.ShapeDtypeStruct(array.shape, F32) for array in (*wide, *same)],
        in_specs=[tile] * len(wide) + whole,
        out_specs=[tile] * len(wide) + whole,
    )(*wide, *same)


def solution(mesh):
    devices = mesh.shape["dp"] * mesh.shape["seq"]
    whole_tiles = mesh.shape["seq"] == 4 and mesh.shape["dp"] % 2 == 0 and D // devices == 16
    in_specs = (
        P("seq", "dp", None),
        P("seq", "dp", None),
        P(None, ("dp", "seq"), None),
        P(None, ("dp", "seq"), None),
        P(None, ("dp", "seq"), None),
        P(None, ("dp", "seq"), None),
        P(None, ("dp", "seq")),
        P(None, ("dp", "seq")),
        P(None, None, ("dp", "seq")),
        P("dp"),
        P(),
    )
    out_specs = (
        P("seq", "dp", None),
        P("seq", "dp", None),
        P(None, ("dp", "seq"), None),
        P(None, ("dp", "seq"), None),
        P(None, ("dp", "seq"), None),
        P(None, ("dp", "seq"), None),
        P(None, ("dp", "seq")),
        P(None, ("dp", "seq")),
        P(None, None, ("dp", "seq")),
    )
    return jax.shard_map(
        fused_body if whole_tiles else body, mesh=mesh, in_specs=in_specs, out_specs=out_specs, check_vma=False)
```
